128 devices in a mesh: dp: 16 (over y, x), dim: 8 (over z, core).
Axes of the slice: x: 4, y: 4, z: 4, core: 2. Of those that a mesh axis runs over, the one named last changes fastest.
Arguments:
- noise: bfloat16 [256, 324480], P(('dp', 'dim')), may hold values from -5 to 5
- data: bfloat16 [256, 324480], P(('dp', 'dim')), may hold values from -10 to 10
Outputs:
- targets: bfloat16 [256, 324480], P(('dp', 'dim'))
- row_potential: float32 [256], P(('dp', 'dim'))
- col_potential: float32 [256], P(('dp', 'dim'))
The draws below stay inside these ranges and needn't reach their ends.
All inputs are finite; a program needn't handle non-finite values.
Results may differ from the reference program's by a relative error of at most 0.014.
Values may be sent and summed in bfloat16 or wider, within the bound.
No kernel may reach another device: no remote copies, remote signals or barrier semaphores. Data moves between devices by JAX's collectives and lax.ppermute only.
A program may use at most 128 MiB of HBM per device.

```python
import math
import jax
import jax.numpy as jnp
from jax import lax

SWEEPS = 20
LATENT = 324480
BATCH = 256


def draw_noise(key, part):
    key = jax.random.fold_in(key, 11)
    key_vals = jax.random.fold_in(key, 1)
    values = jnp.clip(jax.random.normal(key_vals, (BATCH, LATENT), jnp.float32), -5.0, 5.0)
    return values.astype(jnp.bfloat16)


def draw_data(key, part):
    key = jax.random.fold_in(key, 23)
    key_vals = jax.random.fold_in(key, 1)
    key_rows = jax.random.fold_in(key, 2)
    scales = jnp.exp(jax.random.uniform(key_rows, (BATCH, 1), jnp.float32, -0.69, 0.69))
    values = jnp.clip(jax.random.normal(key_vals, (BATCH, LATENT), jnp.float32), -5.0, 5.0)
    return jnp.clip(values * scales, -10.0, 10.0).astype(jnp.bfloat16)


def setup_inputs(seed: int = 0) -> dict:
    keys = jax.random.split(jax.random.key(seed), 3)
    noise = draw_noise(jax.random.fold_in(keys[2], 71), 0)
    data = draw_data(jax.random.fold_in(keys[2], 71), 0)
    return {"noise": noise, "data": data}


def lse_rows(values):
    top = lax.optimization_barrier(jnp.max(values, axis=1, keepdims=True))
    return top[:, 0] + jnp.log(lax.optimization_barrier(jnp.sum(jnp.exp(values - top), axis=1)))

def lse_cols(values):
    top = lax.optimization_barrier(jnp.max(values, axis=0, keepdims=True))
    return top[0] + jnp.log(lax.optimization_barrier(jnp.sum(jnp.exp(values - top), axis=0)))

def reference(noise, data):
    gram = lax.dot_general(noise, data, (((1,), (1,)), ((), ())), preferred_element_type=jnp.float32)
    noise_sq = lax.optimization_barrier(jnp.sum(jnp.square(noise.astype(jnp.float32)), axis=1))
    data_sq = lax.optimization_barrier(jnp.sum(jnp.square(data.astype(jnp.float32)), axis=1))
    cost = (noise_sq[:, None] + data_sq[None, :] - 2.0 * gram) / LATENT
    temper = 0.25 / math.sqrt(LATENT)

    def sweep(step, carry):
        row_pot, col_pot = carry
        row_pot = -temper * lse_rows((col_pot[None, :] - cost) / temper)
        col_pot = -temper * lse_cols((row_pot[:, None] - cost) / temper)
        return (row_pot, col_pot)
    start = (jnp.zeros((BATCH,), jnp.float32), jnp.zeros((BATCH,), jnp.float32))
    row_pot, col_pot = lax.fori_loop(0, SWEEPS, sweep, start)
    weights = jax.nn.softmax((col_pot[None, :] - cost) / temper, axis=1).astype(jnp.bfloat16)
    targets = jnp.dot(weights, data, preferred_element_type=jnp.float32).astype(jnp.bfloat16)
    return (targets, row_pot, col_pot)
```

```python
import math

import jax
import jax.numpy as jnp
from jax import lax
from jax.experimental import pallas as pl
from jax.experimental.pallas import tpu as pltpu
from jax.sharding import PartitionSpec as P

SWEEPS = 20
LATENT = 324480
BATCH = 256
AXES = ("dp", "dim")
LANES = 128
TEMPER = 0.25 / math.sqrt(LATENT)
UNIT = TEMPER * math.log(2.0)
DRIFT = 2.0**40
VMEM = 48 * 1024 * 1024


def pieces_of(value, pieces_ref):
    for piece in range(BATCH * 2 // 4):
        row, half = 4 * (piece // 2), LANES * (piece % 2)
        pieces_ref[piece] = value[row : row + 4, half : half + LANES]


def whole_of(pieces_ref):
    rows = []
    for row in range(BATCH // 4):
        rows.append(jnp.concatenate([pieces_ref[2 * row], pieces_ref[2 * row + 1]], axis=1))
    return jnp.concatenate(rows, axis=0)


def gram_kernel(noise_ref, data_ref, out_ref):
    data = data_ref[...]
    gram = lax.dot_general(
        data, noise_ref[...], (((1,), (1,)), ((), ())), preferred_element_type=jnp.float32
    )
    wide = data.astype(jnp.float32)
    data_sq = jnp.sum(wide * wide, axis=1, keepdims=True)
    pieces_of(data_sq - 2.0 * gram, out_ref)


def sum_kernel(parts_ref, out_ref):
    total = jnp.sum(parts_ref[...], axis=0)
    out_ref[...] = jnp.broadcast_to(total[None], out_ref.shape)


def sweep_kernel(cost_ref, data_ref, out_ref, pots_ref, bias, kern, row_base, col_base, row_fac, col_fac):
    bias[...] = whole_of(cost_ref) * (-1.0 / (LATENT * UNIT))

    def log_sweep():
        col = col_base[...] + jnp.log2(col_fac[...])
        scaled = bias[...] + col
        top = jnp.max(scaled, axis=0, keepdims=True)
        row = -(top + jnp.log2(jnp.sum(jnp.exp2(scaled - top), axis=0, keepdims=True)))
        scaled = bias[...] + row
        top = jnp.max(scaled, axis=1, keepdims=True)
        col = -(top + jnp.log2(jnp.sum(jnp.exp2(scaled - top), axis=1, keepdims=True)))
        row_base[...] = row
        col_base[...] = col
        row_fac[...] = jnp.ones_like(row)
        col_fac[...] = jnp.ones_like(col)
        kern[...] = jnp.exp2(scaled + col)

    col_base[...] = jnp.zeros_like(col_base)
    col_fac[...] = jnp.ones_like(col_fac)
    log_sweep()

    def sweep(step, carry):
        row = 1.0 / jnp.sum(kern[...] * col_fac[...], axis=0, keepdims=True)
        col = 1.0 / jnp.sum(kern[...] * row, axis=1, keepdims=True)
        near = (
            (jnp.max(row) <= DRIFT)
            & (jnp.min(row) >= 1.0 / DRIFT)
            & (jnp.max(col) <= DRIFT)
            & (jnp.min(col) >= 1.0 / DRIFT)
        )

        @pl.when(near)
        def _():
            row_fac[...] = row
            col_fac[...] = col

        @pl.when(jnp.logical_not(near))
        def _():
            log_sweep()

        return carry

    lax.fori_loop(1, SWEEPS, sweep, 0)
    near = jnp.min(jnp.sum(kern[...] * col_fac[...], axis=0)) >= 1.0 / DRIFT

    @pl.when(near)
    def _():
        kern[...] = kern[...] * col_fac[...]

    @pl.when(jnp.logical_not(near))
    def _():
        scaled = bias[...] + (col_base[...] + jnp.log2(col_fac[...]))
        kern[...] = jnp.exp2(scaled - jnp.max(scaled, axis=0, keepdims=True))

    scaled = kern[...]
    weights = (scaled / jnp.sum(scaled, axis=0, keepdims=True)).astype(jnp.bfloat16)
    out_ref[...] = lax.dot_general(
        weights, data_ref[...], (((0,), (0,)), ((), ())), preferred_element_type=jnp.float32
    ).astype(jnp.bfloat16)
    pots_ref[0:1, :] = (row_base[...] + jnp.log2(row_fac[...])) * UNIT
    pots_ref[1:2, :] = jnp.transpose((col_base[...] + jnp.log2(col_fac[...])) * UNIT)


def on_device(noise, data):
    devices = lax.axis_size(AXES)
    own = noise.shape[0]
    ent = -(-LATENT // (LANES * devices)) * LANES
    params = pltpu.CompilerParams(vmem_limit_bytes=VMEM)

    both = jnp.concatenate([noise, data], axis=0)
    both = jnp.pad(both, ((0, 0), (0, ent * devices - LATENT))).reshape(2 * own, devices, ent)
    both = lax.all_to_all(both, AXES, split_axis=1, concat_axis=1)
    noise_ent = both[:own].transpose(1, 0, 2).reshape(BATCH, ent)
    data_ent = both[own:].transpose(1, 0, 2).reshape(BATCH, ent)

    pieces = jax.ShapeDtypeStruct((devices, 4, LANES), jnp.float32)
    parts = pl.pallas_call(gram_kernel, out_shape=pieces, compiler_params=params)(noise_ent, data_ent)
    parts = lax.all_to_all(parts, AXES, split_axis=0, concat_axis=0)
    total = pl.pallas_call(sum_kernel, out_shape=pieces, compiler_params=params)(parts)
    total = lax.all_to_all(total, AXES, split_axis=0, concat_axis=0)

    moved, pots = pl.pallas_call(
        sweep_kernel,
        out_shape=(
            jax.ShapeDtypeStruct((BATCH, ent), jnp.bfloat16),
            jax.ShapeDtypeStruct((2, BATCH), jnp.float32),
        ),
        scratch_shapes=[
            pltpu.VMEM((BATCH, BATCH), jnp.float32),
            pltpu.VMEM((BATCH, BATCH), jnp.float32),
            pltpu.VMEM((1, BATCH), jnp.float32),
            pltpu.VMEM((BATCH, 1), jnp.float32),
            pltpu.VMEM((1, BATCH), jnp.float32),
            pltpu.VMEM((BATCH, 1), jnp.float32),
        ],
        compiler_params=params,
    )(total, data_ent)
    targets = lax.all_to_all(moved.reshape(devices, own, ent), AXES, split_axis=0, concat_axis=0)
    targets = targets.transpose(1, 0, 2).reshape(own, devices * ent)[:, :LATENT]

    offset = lax.axis_index(AXES) * own
    mine = lax.dynamic_slice_in_dim(pots, offset, own, 1)
    wide = noise.astype(jnp.float32)
    noise_sq = jnp.sum(wide * wide, axis=1)
    return (targets, mine[0] + noise_sq / LATENT, mine[1])


def solution(mesh):
    return jax.shard_map(
        on_device,
        mesh=mesh,
        in_specs=(P(AXES, None), P(AXES, None)),
        out_specs=(P(AXES, None), P(AXES), P(AXES)),
        check_vma=False,
    )
```

```python
import math

import jax
import jax.numpy as jnp
from jax import lax
from jax.experimental import pallas as pl
from jax.experimental.pallas import tpu as pltpu
from jax.sharding import PartitionSpec as P

SWEEPS = 20
LATENT = 324480
BATCH = 256
AXES = ("dp", "dim")
LANES = 128
TEMPER = 0.25 / math.sqrt(LATENT)
UNIT = TEMPER * math.log(2.0)
DRIFT = 2.0**40
VMEM = 16 * 1024 * 1024
UNITS = 4
UNIT_TILES = 5


def pack_kernel(noise_ref, data_ref, out_ref, zeros, sems):
    devices, units = out_ref.shape[0], noise_ref.shape[0]
    zeros[...] = jnp.zeros_like(zeros)
    copies = []
    for kind, ref in enumerate((noise_ref, data_ref)):
        for q in range(UNITS):
            slot = kind * UNITS + q
            start = q * devices
            count = min(devices, units - start)
            copies.append((ref.at[pl.ds(start, count)], out_ref.at[pl.ds(0, count), slot]))
            if count < devices:
                copies.append((zeros, out_ref.at[pl.ds(count, devices - count), slot]))
    copies = [pltpu.make_async_copy(src, dst, sems.at[n]) for n, (src, dst) in enumerate(copies)]
    for copy in copies:
        copy.start()
    for copy in copies:
        copy.wait()


def unpack_kernel(moved_ref, out_ref, sems):
    devices, units = moved_ref.shape[0], out_ref.shape[0]
    copies = []
    for q in range(UNITS):
        start = q * devices
        count = min(devices, units - start)
        copies.append(
            pltpu.make_async_copy(
                moved_ref.at[pl.ds(0, count), q], out_ref.at[pl.ds(start, count)], sems.at[q]
            )
        )
    for copy in copies:
        copy.start()
    for copy in copies:
        copy.wait()


def pieces_of(value, pieces_ref):
    for piece in range(BATCH * 2 // 4):
        row, half = 4 * (piece // 2), LANES * (piece % 2)
        pieces_ref[piece] = value[row : row + 4, half : half + LANES]


def whole_of(pieces_ref):
    rows = []
    for row in range(BATCH // 4):
        rows.append(jnp.concatenate([pieces_ref[2 * row], pieces_ref[2 * row + 1]], axis=1))
    return jnp.concatenate(rows, axis=0)


def gram_kernel(both_ref, out_ref):
    ent = both_ref.shape[1] // 2
    data = both_ref[:, ent:]
    gram = lax.dot_general(
        data, both_ref[:, :ent], (((1,), (1,)), ((), ())), preferred_element_type=jnp.float32
    )
    wide = data.astype(jnp.float32)
    data_sq = jnp.sum(wide * wide, axis=1, keepdims=True)
    pieces_of(data_sq - 2.0 * gram, out_ref)


def sum_kernel(parts_ref, out_ref):
    total = jnp.sum(parts_ref[...], axis=0)
    out_ref[...] = jnp.broadcast_to(total[None], out_ref.shape)


def sweep_kernel(cost_ref, both_ref, out_ref, pots_ref, bias, kern, row_base, col_base, row_fac, col_fac):
    bias[...] = whole_of(cost_ref) * (-1.0 / (LATENT * UNIT))

    def log_sweep():
        col = col_base[...] + jnp.log2(col_fac[...])
        scaled = bias[...] + col
        top = jnp.max(scaled, axis=0, keepdims=True)
        row = -(top + jnp.log2(jnp.sum(jnp.exp2(scaled - top), axis=0, keepdims=True)))
        scaled = bias[...] + row
        top = jnp.max(scaled, axis=1, keepdims=True)
        col = -(top + jnp.log2(jnp.sum(jnp.exp2(scaled - top), axis=1, keepdims=True)))
        row_base[...] = row
        col_base[...] = col
        row_fac[...] = jnp.ones_like(row)
        col_fac[...] = jnp.ones_like(col)
        kern[...] = jnp.exp2(scaled + col)

    col_base[...] = jnp.zeros_like(col_base)
    col_fac[...] = jnp.ones_like(col_fac)
    log_sweep()

    def sweep(step, carry):
        row = 1.0 / jnp.sum(kern[...] * col_fac[...], axis=0, keepdims=True)
        col = 1.0 / jnp.sum(kern[...] * row, axis=1, keepdims=True)
        near = (
            (jnp.max(row) <= DRIFT)
            & (jnp.min(row) >= 1.0 / DRIFT)
            & (jnp.max(col) <= DRIFT)
            & (jnp.min(col) >= 1.0 / DRIFT)
        )

        @pl.when(near)
        def _():
            row_fac[...] = row
            col_fac[...] = col

        @pl.when(jnp.logical_not(near))
        def _():
            log_sweep()

        return carry

    lax.fori_loop(1, SWEEPS, sweep, 0)
    near = jnp.min(jnp.sum(kern[...] * col_fac[...], axis=0)) >= 1.0 / DRIFT

    @pl.when(near)
    def _():
        kern[...] = kern[...] * col_fac[...]

    @pl.when(jnp.logical_not(near))
    def _():
        scaled = bias[...] + (col_base[...] + jnp.log2(col_fac[...]))
        kern[...] = jnp.exp2(scaled - jnp.max(scaled, axis=0, keepdims=True))

    scaled = kern[...]
    weights = (scaled / jnp.sum(scaled, axis=0, keepdims=True)).astype(jnp.bfloat16)
    out_ref[...] = lax.dot_general(
        weights, both_ref[:, both_ref.shape[1] // 2 :], (((0,), (0,)), ((), ())), preferred_element_type=jnp.float32
    ).astype(jnp.bfloat16)
    pots_ref[0:1, :] = (row_base[...] + jnp.log2(row_fac[...])) * UNIT
    pots_ref[1:2, :] = jnp.transpose((col_base[...] + jnp.log2(col_fac[...])) * UNIT)


def on_device(noise, data):
    devices = lax.axis_size(AXES)
    own = noise.shape[0]
    ent = UNITS * UNIT_TILES * LANES
    params = pltpu.CompilerParams(vmem_limit_bytes=VMEM)
    anywhere = pl.BlockSpec(memory_space=pl.ANY)

    def units_of(rows):
        units = rows.shape[1] // (UNIT_TILES * LANES)
        return rows.reshape(own, units, UNIT_TILES, LANES).transpose(1, 2, 0, 3)

    both = pl.pallas_call(
        pack_kernel,
        out_shape=jax.ShapeDtypeStruct((devices, 2 * UNITS, UNIT_TILES, own, LANES), noise.dtype),
        in_specs=[anywhere, anywhere],
        out_specs=anywhere,
        scratch_shapes=[
            pltpu.VMEM((UNITS * devices - LATENT // (UNIT_TILES * LANES), UNIT_TILES, own, LANES), noise.dtype),
            pltpu.SemaphoreType.DMA((4 * UNITS,)),
        ],
    )(units_of(noise), units_of(data))
    both = both.reshape(devices, -1, own, LANES).transpose(0, 2, 1, 3).reshape(devices, own, 2 * ent)
    both = lax.all_to_all(both, AXES, split_axis=0, concat_axis=0).reshape(BATCH, 2 * ent)

    pieces = jax.ShapeDtypeStruct((devices, 4, LANES), jnp.float32)
    parts = pl.pallas_call(gram_kernel, out_shape=pieces, compiler_params=params)(both)
    parts = lax.all_to_all(parts, AXES, split_axis=0, concat_axis=0)
    total = pl.pallas_call(sum_kernel, out_shape=pieces, compiler_params=params)(parts)
    total = lax.all_to_all(total, AXES, split_axis=0, concat_axis=0)

    moved, pots = pl.pallas_call(
        sweep_kernel,
        out_shape=(
            jax.ShapeDtypeStruct((BATCH, ent), jnp.bfloat16),
            jax.ShapeDtypeStruct((2, BATCH), jnp.float32),
        ),
        scratch_shapes=[
            pltpu.VMEM((BATCH, BATCH), jnp.float32),
            pltpu.VMEM((BATCH, BATCH), jnp.float32),
            pltpu.VMEM((1, BATCH), jnp.float32),
            pltpu.VMEM((BATCH, 1), jnp.float32),
            pltpu.VMEM((1, BATCH), jnp.float32),
            pltpu.VMEM((BATCH, 1), jnp.float32),
        ],
        compiler_params=params,
    )(total, both)
    moved = lax.all_to_all(moved.reshape(devices, own, ent), AXES, split_axis=0, concat_axis=0)
    moved = moved.reshape(devices, own, UNITS, UNIT_TILES, LANES).transpose(0, 2, 3, 1, 4)
    targets = pl.pallas_call(
        unpack_kernel,
        out_shape=jax.ShapeDtypeStruct((LATENT // (UNIT_TILES * LANES), UNIT_TILES, own, LANES), moved.dtype),
        in_specs=[anywhere],
        out_specs=anywhere,
        scratch_shapes=[pltpu.SemaphoreType.DMA((UNITS,))],
    )(moved)
    targets = targets.transpose(2, 0, 1, 3).reshape(own, LATENT)

    offset = lax.axis_index(AXES) * own
    mine = lax.dynamic_slice_in_dim(pots, offset, own, 1)
    wide = noise.astype(jnp.float32)
    noise_sq = jnp.sum(wide * wide, axis=1)
    return (targets, mine[0] + noise_sq / LATENT, mine[1])


def solution(mesh):
    return jax.shard_map(
        on_device,
        mesh=mesh,
        in_specs=(P(AXES, None), P(AXES, None)),
        out_specs=(P(AXES, None), P(AXES), P(AXES)),
        check_vma=False,
    )
```

```python
import math

import jax
import jax.numpy as jnp
from jax import lax
from jax.experimental import pallas as pl
from jax.experimental.pallas import tpu as pltpu
from jax.sharding import PartitionSpec as P

SWEEPS = 20
LATENT = 324480
BATCH = 256
AXES = ("dp", "dim")
LANES = 128
TEMPER = 0.25 / math.sqrt(LATENT)
BIT = TEMPER * math.log(2.0)
DRIFT = 2.0**40
VMEM = 12 * 1024 * 1024
UNITS = 4
UNIT = 640


def pack_kernel(noise_ref, data_ref, out_ref, zeros, sems):
    devices, units = out_ref.shape[0], noise_ref.shape[0]
    zeros[...] = jnp.zeros_like(zeros)
    copies = []
    for kind, ref in enumerate((noise_ref, data_ref)):
        for q in range(UNITS):
            slot = kind * UNITS + q
            start = q * devices
            count = min(devices, units - start)
            copies.append((ref.at[pl.ds(start, count)], out_ref.at[pl.ds(0, count), slot]))
            if count < devices:
                copies.append((zeros, out_ref.at[pl.ds(count, devices - count), slot]))
    copies = [pltpu.make_async_copy(src, dst, sems.at[n]) for n, (src, dst) in enumerate(copies)]
    for copy in copies:
        copy.start()
    for copy in copies:
        copy.wait()


def unpack_kernel(moved_ref, out_ref, sems):
    devices, units = moved_ref.shape[0], out_ref.shape[0]
    copies = []
    for q in range(UNITS):
        start = q * devices
        count = min(devices, units - start)
        copies.append(
            pltpu.make_async_copy(
                moved_ref.at[pl.ds(0, count), q], out_ref.at[pl.ds(start, count)], sems.at[q]
            )
        )
    for copy in copies:
        copy.start()
    for copy in copies:
        copy.wait()


def pieces_of(value, pieces_ref):
    for piece in range(BATCH * 2 // 4):
        row, half = 4 * (piece // 2), LANES * (piece % 2)
        pieces_ref[piece] = value[row : row + 4, half : half + LANES]


def whole_of(pieces_ref):
    rows = []
    for row in range(BATCH // 4):
        rows.append(jnp.concatenate([pieces_ref[2 * row], pieces_ref[2 * row + 1]], axis=1))
    return jnp.concatenate(rows, axis=0)


def gram_kernel(both_ref, out_ref):
    ent = both_ref.shape[1] // 2
    data = both_ref[:, ent:]
    gram = lax.dot_general(
        data, both_ref[:, :ent], (((1,), (1,)), ((), ())), preferred_element_type=jnp.float32
    )
    wide = data.astype(jnp.float32)
    data_sq = jnp.sum(wide * wide, axis=1, keepdims=True)
    pieces_of(data_sq - 2.0 * gram, out_ref)


def sum_kernel(parts_ref, out_ref):
    total = jnp.sum(parts_ref[...], axis=0)
    out_ref[...] = jnp.broadcast_to(total[None], out_ref.shape)


def sweep_kernel(cost_ref, both_ref, out_ref, pots_ref, bias, kern, row_base, col_base, row_fac, col_fac):
    bias[...] = whole_of(cost_ref) * (-1.0 / (LATENT * BIT))

    def log_sweep():
        col = col_base[...] + jnp.log2(col_fac[...])
        scaled = bias[...] + col
        top = jnp.max(scaled, axis=0, keepdims=True)
        row = -(top + jnp.log2(jnp.sum(jnp.exp2(scaled - top), axis=0, keepdims=True)))
        scaled = bias[...] + row
        top = jnp.max(scaled, axis=1, keepdims=True)
        col = -(top + jnp.log2(jnp.sum(jnp.exp2(scaled - top), axis=1, keepdims=True)))
        row_base[...] = row
        col_base[...] = col
        row_fac[...] = jnp.ones_like(row)
        col_fac[...] = jnp.ones_like(col)
        kern[...] = jnp.exp2(scaled + col)

    col_base[...] = jnp.zeros_like(col_base)
    col_fac[...] = jnp.ones_like(col_fac)
    log_sweep()

    def sweep(step, carry):
        row = 1.0 / jnp.sum(kern[...] * col_fac[...], axis=0, keepdims=True)
        col = 1.0 / jnp.sum(kern[...] * row, axis=1, keepdims=True)
        near = (
            (jnp.max(row) <= DRIFT)
            & (jnp.min(row) >= 1.0 / DRIFT)
            & (jnp.max(col) <= DRIFT)
            & (jnp.min(col) >= 1.0 / DRIFT)
        )

        @pl.when(near)
        def _():
            row_fac[...] = row
            col_fac[...] = col

        @pl.when(jnp.logical_not(near))
        def _():
            log_sweep()

        return carry

    lax.fori_loop(1, SWEEPS, sweep, 0)
    near = jnp.min(jnp.sum(kern[...] * col_fac[...], axis=0)) >= 1.0 / DRIFT

    @pl.when(near)
    def _():
        kern[...] = kern[...] * col_fac[...]

    @pl.when(jnp.logical_not(near))
    def _():
        scaled = bias[...] + (col_base[...] + jnp.log2(col_fac[...]))
        kern[...] = jnp.exp2(scaled - jnp.max(scaled, axis=0, keepdims=True))

    scaled = kern[...]
    weights = (scaled / jnp.sum(scaled, axis=0, keepdims=True)).astype(jnp.bfloat16)
    out_ref[...] = lax.dot_general(
        weights, both_ref[:, both_ref.shape[1] // 2 :], (((0,), (0,)), ((), ())), preferred_element_type=jnp.float32
    ).astype(jnp.bfloat16)
    pots_ref[0:1, :] = (row_base[...] + jnp.log2(row_fac[...])) * BIT
    pots_ref[1:2, :] = jnp.transpose((col_base[...] + jnp.log2(col_fac[...])) * BIT)


def on_device(noise, data):
    devices = lax.axis_size(AXES)
    own = noise.shape[0]
    ent = UNITS * UNIT
    units = LATENT // UNIT
    params = pltpu.CompilerParams(vmem_limit_bytes=VMEM)
    anywhere = pl.BlockSpec(memory_space=pl.ANY)

    def units_of(rows):
        return rows.reshape(own, units, UNIT).transpose(1, 0, 2)

    both = pl.pallas_call(
        pack_kernel,
        out_shape=jax.ShapeDtypeStruct((devices, 2 * UNITS, own, UNIT), noise.dtype),
        in_specs=[anywhere, anywhere],
        out_specs=anywhere,
        scratch_shapes=[
            pltpu.VMEM((UNITS * devices - units, own, UNIT), noise.dtype),
            pltpu.SemaphoreType.DMA((4 * UNITS,)),
        ],
        compiler_params=params,
    )(units_of(noise), units_of(data))
    both = both.transpose(0, 2, 1, 3).reshape(devices, own, 2 * ent)
    both = lax.all_to_all(both, AXES, split_axis=0, concat_axis=0).reshape(BATCH, 2 * ent)

    pieces = jax.ShapeDtypeStruct((devices, 4, LANES), jnp.float32)
    parts = pl.pallas_call(gram_kernel, out_shape=pieces, compiler_params=params)(both)
    parts = lax.all_to_all(parts, AXES, split_axis=0, concat_axis=0)
    total = pl.pallas_call(sum_kernel, out_shape=pieces, compiler_params=params)(parts)
    total = lax.all_to_all(total, AXES, split_axis=0, concat_axis=0)

    moved, pots = pl.pallas_call(
        sweep_kernel,
        out_shape=(
            jax.ShapeDtypeStruct((BATCH, ent), jnp.bfloat16),
            jax.ShapeDtypeStruct((2, BATCH), jnp.float32),
        ),
        scratch_shapes=[
            pltpu.VMEM((BATCH, BATCH), jnp.float32),
            pltpu.VMEM((BATCH, BATCH), jnp.float32),
            pltpu.VMEM((1, BATCH), jnp.float32),
            pltpu.VMEM((BATCH, 1), jnp.float32),
            pltpu.VMEM((1, BATCH), jnp.float32),
            pltpu.VMEM((BATCH, 1), jnp.float32),
        ],
        compiler_params=params,
    )(total, both)
    moved = lax.all_to_all(moved.reshape(devices, own, ent), AXES, split_axis=0, concat_axis=0)
    moved = moved.reshape(devices, own, UNITS, UNIT).transpose(0, 2, 1, 3)
    targets = pl.pallas_call(
        unpack_kernel,
        out_shape=jax.ShapeDtypeStruct((units, own, UNIT), moved.dtype),
        in_specs=[anywhere],
        out_specs=anywhere,
        scratch_shapes=[pltpu.SemaphoreType.DMA((UNITS,))],
        compiler_params=params,
    )(moved)
    targets = targets.transpose(1, 0, 2).reshape(own, LATENT)

    offset = lax.axis_index(AXES) * own
    mine = lax.dynamic_slice_in_dim(pots, offset, own, 1)
    wide = noise.astype(jnp.float32)
    noise_sq = jnp.sum(wide * wide, axis=1)
    return (targets, mine[0] + noise_sq / LATENT, mine[1])


def solution(mesh):
    return jax.shard_map(
        on_device,
        mesh=mesh,
        in_specs=(P(AXES, None), P(AXES, None)),
        out_specs=(P(AXES, None), P(AXES), P(AXES)),
        check_vma=False,
    )
```

```python
import math

import jax
import jax.numpy as jnp
from jax import lax
from jax.experimental import pallas as pl
from jax.experimental.pallas import tpu as pltpu
from jax.sharding import PartitionSpec as P

SWEEPS = 20
LATENT = 324480
BATCH = 256
AXES = ("dp", "dim")
LANES = 128
TEMPER = 0.25 / math.sqrt(LATENT)
BIT = TEMPER * math.log(2.0)
DRIFT = 2.0**40
VMEM = 24 * 1024 * 1024
UNITS = 4
UNIT = 640


def pack_kernel(noise_ref, data_ref, out_ref, zeros, sems):
    devices, units = out_ref.shape[0], noise_ref.shape[0]
    zeros[...] = jnp.zeros_like(zeros)
    copies = []
    for kind, ref in enumerate((noise_ref, data_ref)):
        for q in range(UNITS):
            slot = kind * UNITS + q
            start = q * devices
            count = min(devices, units - start)
            copies.append((ref.at[pl.ds(start, count)], out_ref.at[pl.ds(0, count), slot]))
            if count < devices:
                copies.append((zeros, out_ref.at[pl.ds(count, devices - count), slot]))
    copies = [pltpu.make_async_copy(src, dst, sems.at[n]) for n, (src, dst) in enumerate(copies)]
    for copy in copies:
        copy.start()
    for copy in copies:
        copy.wait()


def unpack_kernel(moved_ref, out_ref, sems):
    devices, units = moved_ref.shape[0], out_ref.shape[0]
    copies = []
    for q in range(UNITS):
        start = q * devices
        count = min(devices, units - start)
        copies.append(
            pltpu.make_async_copy(
                moved_ref.at[pl.ds(0, count), q], out_ref.at[pl.ds(start, count)], sems.at[q]
            )
        )
    for copy in copies:
        copy.start()
    for copy in copies:
        copy.wait()


def pieces_of(value, pieces_ref):
    for piece in range(BATCH * 2 // 4):
        row, half = 4 * (piece // 2), LANES * (piece % 2)
        pieces_ref[piece] = value[row : row + 4, half : half + LANES]


def whole_of(pieces_ref):
    rows = []
    for row in range(BATCH // 4):
        rows.append(jnp.concatenate([pieces_ref[2 * row], pieces_ref[2 * row + 1]], axis=1))
    return jnp.concatenate(rows, axis=0)


def gram_kernel(both_ref, out_ref, data_ref):
    ent = data_ref.shape[1]
    noise = both_ref[:, :, :ent].reshape(data_ref.shape)
    data = both_ref[:, :, ent:].reshape(data_ref.shape)
    data_ref[...] = data
    gram = lax.dot_general(
        data, noise, (((1,), (1,)), ((), ())), preferred_element_type=jnp.float32
    )
    wide = data.astype(jnp.float32)
    data_sq = jnp.sum(wide * wide, axis=1, keepdims=True)
    pieces_of(data_sq - 2.0 * gram, out_ref)


def sum_kernel(parts_ref, out_ref):
    total = jnp.sum(parts_ref[...], axis=0)
    out_ref[...] = jnp.broadcast_to(total[None], out_ref.shape)


def sweep_kernel(cost_ref, data_ref, out_ref, pots_ref, bias, kern, row_base, col_base, row_fac, col_fac):
    bias[...] = whole_of(cost_ref) * (-1.0 / (LATENT * BIT))

    def log_sweep():
        col = col_base[...] + jnp.log2(col_fac[...])
        scaled = bias[...] + col
        top = jnp.max(scaled, axis=0, keepdims=True)
        row = -(top + jnp.log2(jnp.sum(jnp.exp2(scaled - top), axis=0, keepdims=True)))
        scaled = bias[...] + row
        top = jnp.max(scaled, axis=1, keepdims=True)
        col = -(top + jnp.log2(jnp.sum(jnp.exp2(scaled - top), axis=1, keepdims=True)))
        row_base[...] = row
        col_base[...] = col
        row_fac[...] = jnp.ones_like(row)
        col_fac[...] = jnp.ones_like(col)
        kern[...] = jnp.exp2(scaled + col)

    col_base[...] = jnp.zeros_like(col_base)
    col_fac[...] = jnp.ones_like(col_fac)
    log_sweep()

    def sweep(step, carry):
        row = 1.0 / jnp.sum(kern[...] * col_fac[...], axis=0, keepdims=True)
        col = 1.0 / jnp.sum(kern[...] * row, axis=1, keepdims=True)
        near = (
            (jnp.max(row) <= DRIFT)
            & (jnp.min(row) >= 1.0 / DRIFT)
            & (jnp.max(col) <= DRIFT)
            & (jnp.min(col) >= 1.0 / DRIFT)
        )

        @pl.when(near)
        def _():
            row_fac[...] = row
            col_fac[...] = col

        @pl.when(jnp.logical_not(near))
        def _():
            log_sweep()

        return carry

    lax.fori_loop(1, SWEEPS, sweep, 0)
    near = jnp.min(jnp.sum(kern[...] * col_fac[...], axis=0)) >= 1.0 / DRIFT

    @pl.when(near)
    def _():
        kern[...] = kern[...] * col_fac[...]

    @pl.when(jnp.logical_not(near))
    def _():
        scaled = bias[...] + (col_base[...] + jnp.log2(col_fac[...]))
        kern[...] = jnp.exp2(scaled - jnp.max(scaled, axis=0, keepdims=True))

    scaled = kern[...]
    weights = (scaled / jnp.sum(scaled, axis=0, keepdims=True)).astype(jnp.bfloat16)
    moved = lax.dot_general(
        weights, data_ref[...], (((0,), (0,)), ((), ())), preferred_element_type=jnp.float32
    )
    out_ref[...] = moved.astype(jnp.bfloat16).reshape(out_ref.shape)
    pots_ref[0:1, :] = (row_base[...] + jnp.log2(row_fac[...])) * BIT
    pots_ref[1:2, :] = jnp.transpose((col_base[...] + jnp.log2(col_fac[...])) * BIT)


def on_device(noise, data):
    devices = lax.axis_size(AXES)
    own = noise.shape[0]
    ent = UNITS * UNIT
    units = LATENT // UNIT
    params = pltpu.CompilerParams(vmem_limit_bytes=VMEM)
    anywhere = pl.BlockSpec(memory_space=pl.ANY)

    def units_of(rows):
        return rows.reshape(own, units, UNIT).transpose(1, 0, 2)

    both = pl.pallas_call(
        pack_kernel,
        out_shape=jax.ShapeDtypeStruct((devices, 2 * UNITS, own, UNIT), noise.dtype),
        in_specs=[anywhere, anywhere],
        out_specs=anywhere,
        scratch_shapes=[
            pltpu.VMEM((UNITS * devices - units, own, UNIT), noise.dtype),
            pltpu.SemaphoreType.DMA((4 * UNITS,)),
        ],
        compiler_params=params,
    )(units_of(noise), units_of(data))
    both = both.transpose(0, 2, 1, 3).reshape(devices, own, 2 * ent)
    both = lax.all_to_all(both, AXES, split_axis=0, concat_axis=0)

    pieces = jax.ShapeDtypeStruct((devices, 4, LANES), jnp.float32)
    parts, data_ent = pl.pallas_call(
        gram_kernel,
        out_shape=(pieces, jax.ShapeDtypeStruct((BATCH, ent), data.dtype)),
        compiler_params=params,
    )(both)
    parts = lax.all_to_all(parts, AXES, split_axis=0, concat_axis=0)
    total = pl.pallas_call(sum_kernel, out_shape=pieces, compiler_params=params)(parts)
    total = lax.all_to_all(total, AXES, split_axis=0, concat_axis=0)

    moved, pots = pl.pallas_call(
        sweep_kernel,
        out_shape=(
            jax.ShapeDtypeStruct((devices, own, ent), jnp.bfloat16),
            jax.ShapeDtypeStruct((2, BATCH), jnp.float32),
        ),
        scratch_shapes=[
            pltpu.VMEM((BATCH, BATCH), jnp.float32),
            pltpu.VMEM((BATCH, BATCH), jnp.float32),
            pltpu.VMEM((1, BATCH), jnp.float32),
            pltpu.VMEM((BATCH, 1), jnp.float32),
            pltpu.VMEM((1, BATCH), jnp.float32),
            pltpu.VMEM((BATCH, 1), jnp.float32),
        ],
        compiler_params=params,
    )(total, data_ent)
    moved = lax.all_to_all(moved, AXES, split_axis=0, concat_axis=0)
    moved = moved.reshape(devices, own, UNITS, UNIT).transpose(0, 2, 1, 3)
    targets = pl.pallas_call(
        unpack_kernel,
        out_shape=jax.ShapeDtypeStruct((units, own, UNIT), moved.dtype),
        in_specs=[anywhere],
        out_specs=anywhere,
        scratch_shapes=[pltpu.SemaphoreType.DMA((UNITS,))],
        compiler_params=params,
    )(moved)
    targets = targets.transpose(1, 0, 2).reshape(own, LATENT)

    offset = lax.axis_index(AXES) * own
    mine = lax.dynamic_slice_in_dim(pots, offset, own, 1)
    wide = noise.astype(jnp.float32)
    noise_sq = jnp.sum(wide * wide, axis=1)
    return (targets, mine[0] + noise_sq / LATENT, mine[1])


def solution(mesh):
    return jax.shard_map(
        on_device,
        mesh=mesh,
        in_specs=(P(AXES, None), P(AXES, None)),
        out_specs=(P(AXES, None), P(AXES), P(AXES)),
        check_vma=False,
    )
```

```python
import math

import jax
import jax.numpy as jnp
from jax import lax
from jax.experimental import pallas as pl
from jax.experimental.pallas import tpu as pltpu
from jax.sharding import PartitionSpec as P

SWEEPS = 20
LATENT = 324480
BATCH = 256
AXES = ("dp", "dim")
LANES = 128
TEMPER = 0.25 / math.sqrt(LATENT)
BIT = TEMPER * math.log(2.0)
DRIFT = 2.0**40
VMEM = 24 * 1024 * 1024
UNITS = 4
UNIT = 640


def pack_kernel(noise_ref, data_ref, out_ref, zeros, sems):
    devices, units = out_ref.shape[0], noise_ref.shape[0]
    zeros[...] = jnp.zeros_like(zeros)
    copies = []
    for kind, ref in enumerate((noise_ref, data_ref)):
        for q in range(UNITS):
            slot = kind * UNITS + q
            start = q * devices
            count = min(devices, units - start)
            copies.append((ref.at[pl.ds(start, count)], out_ref.at[pl.ds(0, count), slot]))
            if count < devices:
                copies.append((zeros, out_ref.at[pl.ds(count, devices - count), slot]))
    copies = [pltpu.make_async_copy(src, dst, sems.at[n]) for n, (src, dst) in enumerate(copies)]
    for copy in copies:
        copy.start()
    for copy in copies:
        copy.wait()


def unpack_kernel(moved_ref, out_ref, sems):
    devices, units = moved_ref.shape[0], out_ref.shape[0]
    copies = []
    for q in range(UNITS):
        start = q * devices
        count = min(devices, units - start)
        copies.append(
            pltpu.make_async_copy(
                moved_ref.at[pl.ds(0, count), q], out_ref.at[pl.ds(start, count)], sems.at[q]
            )
        )
    for copy in copies:
        copy.start()
    for copy in copies:
        copy.wait()


def pieces_of(value, pieces_ref):
    for piece in range(BATCH * 2 // 4):
        row, half = 4 * (piece // 2), LANES * (piece % 2)
        pieces_ref[piece] = value[row : row + 4, half : half + LANES]


def whole_of(pieces_ref):
    rows = []
    for row in range(BATCH // 4):
        rows.append(jnp.concatenate([pieces_ref[2 * row], pieces_ref[2 * row + 1]], axis=1))
    return jnp.concatenate(rows, axis=0)


def gram_kernel(both_ref, out_ref, data_ref):
    ent = data_ref.shape[1]
    noise = both_ref[:, :, :ent].reshape(data_ref.shape)
    data = both_ref[:, :, ent:].reshape(data_ref.shape)
    data_ref[...] = data
    gram = lax.dot_general(
        data, noise, (((1,), (1,)), ((), ())), preferred_element_type=jnp.float32
    )
    wide = data.astype(jnp.float32)
    data_sq = jnp.sum(wide * wide, axis=1, keepdims=True)
    pieces_of(data_sq - 2.0 * gram, out_ref)


def sum_kernel(parts_ref, out_ref):
    total = jnp.sum(parts_ref[...], axis=0)
    out_ref[...] = jnp.broadcast_to(total[None], out_ref.shape)


def sweep_kernel(cost_ref, data_ref, out_ref, pots_ref, bias, kern, row_pot, col_pot, col_fac):
    bias[...] = whole_of(cost_ref) * (-1.0 / (LATENT * BIT))
    col_pot[...] = jnp.zeros_like(col_pot)

    def log_sweep():
        scaled = bias[...] + col_pot[...]
        top = jnp.max(scaled, axis=0, keepdims=True)
        row = -(top + jnp.log2(jnp.sum(jnp.exp2(scaled - top), axis=0, keepdims=True)))
        scaled = bias[...] + row
        top = jnp.max(scaled, axis=1, keepdims=True)
        col = -(top + jnp.log2(jnp.sum(jnp.exp2(scaled - top), axis=1, keepdims=True)))
        row_pot[...] = row
        col_pot[...] = col
        kern[...] = jnp.exp2(scaled + col)

    log_sweep()
    col_fac[...] = jnp.ones_like(col_fac)

    tile = (8, LANES)
    blocks = [pl.ds(start, 8) for start in range(0, BATCH, 8)]
    halves = [pl.ds(start, LANES) for start in range(0, BATCH, LANES)]

    def sweep(step, carry):
        low, high, _ = carry
        sums = [[jnp.zeros(tile, jnp.float32) for _ in halves] for _ in range(2)]
        for n, block in enumerate(blocks):
            factor = col_fac[block, :]
            for h, half in enumerate(halves):
                sums[n % 2][h] += kern[block, half] * factor
        rows = []
        for first, second in zip(*sums):
            total = jnp.broadcast_to(jnp.sum(first + second, axis=0, keepdims=True), tile)
            low, high = jnp.minimum(low, total), jnp.maximum(high, total)
            rows.append(1.0 / total)
        for block in blocks:
            total = sum(kern[block, half] * row for half, row in zip(halves, rows))
            total = jnp.broadcast_to(jnp.sum(total, axis=1, keepdims=True), tile)
            low, high = jnp.minimum(low, total), jnp.maximum(high, total)
            col_fac[block, :] = 1.0 / total
        return (low, high, tuple(rows))

    ones = jnp.ones(tile, jnp.float32)
    low, high, rows = lax.fori_loop(1, SWEEPS, sweep, (ones, ones, (ones, ones)))
    near = (jnp.min(low) >= 1.0 / DRIFT) & (jnp.max(high) <= DRIFT)

    @pl.when(near)
    def _():
        factor = col_fac[...]
        row_pot[...] += jnp.log2(jnp.concatenate([row[:1] for row in rows], axis=1))
        col_pot[...] += jnp.log2(factor[:, :1])
        kern[...] *= jnp.concatenate([factor, factor], axis=1)

    @pl.when(jnp.logical_not(near))
    def _():
        col_pot[...] = jnp.zeros_like(col_pot)

        def again(step, carry):
            log_sweep()
            return carry

        lax.fori_loop(0, SWEEPS, again, 0)

    near = jnp.min(jnp.sum(kern[...], axis=0, keepdims=True)) >= 1.0 / DRIFT

    @pl.when(jnp.logical_not(near))
    def _():
        scaled = bias[...] + col_pot[...]
        kern[...] = jnp.exp2(scaled - jnp.max(scaled, axis=0, keepdims=True))

    scaled = kern[...]
    weights = (scaled / jnp.sum(scaled, axis=0, keepdims=True)).astype(jnp.bfloat16)
    moved = lax.dot_general(
        weights, data_ref[...], (((0,), (0,)), ((), ())), preferred_element_type=jnp.float32
    )
    out_ref[...] = moved.astype(jnp.bfloat16).reshape(out_ref.shape)
    pots_ref[0:1, :] = row_pot[...] * BIT
    pots_ref[1:2, :] = jnp.transpose(col_pot[...] * BIT)


def on_device(noise, data):
    devices = lax.axis_size(AXES)
    own = noise.shape[0]
    ent = UNITS * UNIT
    units = LATENT // UNIT
    params = pltpu.CompilerParams(vmem_limit_bytes=VMEM)
    anywhere = pl.BlockSpec(memory_space=pl.ANY)

    def units_of(rows):
        return rows.reshape(own, units, UNIT).transpose(1, 0, 2)

    both = pl.pallas_call(
        pack_kernel,
        out_shape=jax.ShapeDtypeStruct((devices, 2 * UNITS, own, UNIT), noise.dtype),
        in_specs=[anywhere, anywhere],
        out_specs=anywhere,
        scratch_shapes=[
            pltpu.VMEM((UNITS * devices - units, own, UNIT), noise.dtype),
            pltpu.SemaphoreType.DMA((4 * UNITS,)),
        ],
        compiler_params=params,
    )(units_of(noise), units_of(data))
    both = both.transpose(0, 2, 1, 3).reshape(devices, own, 2 * ent)
    both = lax.all_to_all(both, AXES, split_axis=0, concat_axis=0)

    pieces = jax.ShapeDtypeStruct((devices, 4, LANES), jnp.float32)
    parts, data_ent = pl.pallas_call(
        gram_kernel,
        out_shape=(pieces, jax.ShapeDtypeStruct((BATCH, ent), data.dtype)),
        compiler_params=params,
    )(both)
    parts = lax.all_to_all(parts, AXES, split_axis=0, concat_axis=0)
    total = pl.pallas_call(sum_kernel, out_shape=pieces, compiler_params=params)(parts)
    total = lax.all_to_all(total, AXES, split_axis=0, concat_axis=0)

    moved, pots = pl.pallas_call(
        sweep_kernel,
        out_shape=(
            jax.ShapeDtypeStruct((devices, own, ent), jnp.bfloat16),
            jax.ShapeDtypeStruct((2, BATCH), jnp.float32),
        ),
        scratch_shapes=[
            pltpu.VMEM((BATCH, BATCH), jnp.float32),
            pltpu.VMEM((BATCH, BATCH), jnp.float32),
            pltpu.VMEM((1, BATCH), jnp.float32),
            pltpu.VMEM((BATCH, 1), jnp.float32),
            pltpu.VMEM((BATCH, LANES), jnp.float32),
        ],
        compiler_params=params,
    )(total, data_ent)
    moved = lax.all_to_all(moved, AXES, split_axis=0, concat_axis=0)
    moved = moved.reshape(devices, own, UNITS, UNIT).transpose(0, 2, 1, 3)
    targets = pl.pallas_call(
        unpack_kernel,
        out_shape=jax.ShapeDtypeStruct((units, own, UNIT), moved.dtype),
        in_specs=[anywhere],
        out_specs=anywhere,
        scratch_shapes=[pltpu.SemaphoreType.DMA((UNITS,))],
        compiler_params=params,
    )(moved)
    targets = targets.transpose(1, 0, 2).reshape(own, LATENT)

    offset = lax.axis_index(AXES) * own
    mine = lax.dynamic_slice_in_dim(pots, offset, own, 1)
    wide = noise.astype(jnp.float32)
    noise_sq = jnp.sum(wide * wide, axis=1)
    return (targets, mine[0] + noise_sq / LATENT, mine[1])


def solution(mesh):
    return jax.shard_map(
        on_device,
        mesh=mesh,
        in_specs=(P(AXES, None), P(AXES, None)),
        out_specs=(P(AXES, None), P(AXES), P(AXES)),
        check_vma=False,
    )
```

```python
import math

import jax
import jax.numpy as jnp
from jax import lax
from jax.experimental import pallas as pl
from jax.experimental.pallas import tpu as pltpu
from jax.sharding import PartitionSpec as P

SWEEPS = 20
LATENT = 324480
BATCH = 256
AXES = ("dp", "dim")
LANES = 128
TEMPER = 0.25 / math.sqrt(LATENT)
BIT = TEMPER * math.log(2.0)
DRIFT = 2.0**40
VMEM = 24 * 1024 * 1024
UNITS = 4
UNIT = 640


def pack_kernel(noise_ref, data_ref, out_ref, zeros, sems):
    devices, units = out_ref.shape[0], noise_ref.shape[0]
    zeros[...] = jnp.zeros_like(zeros)
    copies = []
    for kind, ref in enumerate((noise_ref, data_ref)):
        for q in range(UNITS):
            slot = kind * UNITS + q
            start = q * devices
            count = min(devices, units - start)
            copies.append((ref.at[pl.ds(start, count)], out_ref.at[pl.ds(0, count), slot]))
            if count < devices:
                copies.append((zeros, out_ref.at[pl.ds(count, devices - count), slot]))
    copies = [pltpu.make_async_copy(src, dst, sems.at[n]) for n, (src, dst) in enumerate(copies)]
    for copy in copies:
        copy.start()
    for copy in copies:
        copy.wait()


def square_kernel(noise_ref, after_ref, out_ref):
    units = noise_ref.shape[1] // UNIT

    def add(n, total):
        unit = noise_ref[:, pl.ds(pl.multiple_of(n * UNIT, UNIT), UNIT)].astype(jnp.float32)
        return total + unit * unit

    total = jnp.zeros((noise_ref.shape[0], UNIT), jnp.float32)
    total = lax.fori_loop(0, units, add, total, unroll=13)
    total = jnp.sum(total, axis=1, keepdims=True)
    out_ref[...] = jnp.broadcast_to(total, out_ref.shape)


def unpack_kernel(moved_ref, pots_ref, noise_sq_ref, out_ref, row_ref, col_ref, sems):
    devices, units = moved_ref.shape[0], out_ref.shape[0]
    copies = []
    for q in range(UNITS):
        start = q * devices
        count = min(devices, units - start)
        copies.append(
            pltpu.make_async_copy(
                moved_ref.at[pl.ds(0, count), q], out_ref.at[pl.ds(start, count)], sems.at[q]
            )
        )
    for copy in copies:
        copy.start()
    own = out_ref.shape[1]
    first = (lax.axis_index("dp") * lax.axis_size("dim") + lax.axis_index("dim")) * own
    lane = lax.broadcasted_iota(jnp.int32, (1, BATCH), 1)
    for n in range(own):
        mine = lane == first + n
        row = jnp.sum(jnp.where(mine, pots_ref[0:1, :], 0.0))
        row_ref[n] = row + jnp.max(noise_sq_ref[n : n + 1, :]) / LATENT
        col_ref[n] = jnp.sum(jnp.where(mine, pots_ref[1:2, :], 0.0))
    for copy in copies:
        copy.wait()


def pieces_of(value, pieces_ref):
    for piece in range(BATCH * 2 // 4):
        row, half = 4 * (piece // 2), LANES * (piece % 2)
        pieces_ref[piece] = value[row : row + 4, half : half + LANES]


def whole_of(pieces_ref):
    rows = []
    for row in range(BATCH // 4):
        rows.append(jnp.concatenate([pieces_ref[2 * row], pieces_ref[2 * row + 1]], axis=1))
    return jnp.concatenate(rows, axis=0)


def gram_kernel(both_ref, out_ref, data_ref):
    ent = data_ref.shape[1]
    noise = both_ref[:, :, :ent].reshape(data_ref.shape)
    data = both_ref[:, :, ent:].reshape(data_ref.shape)
    data_ref[...] = data
    gram = lax.dot_general(
        data, noise, (((1,), (1,)), ((), ())), preferred_element_type=jnp.float32
    )
    wide = data.astype(jnp.float32)
    data_sq = jnp.sum(wide * wide, axis=1, keepdims=True)
    pieces_of(data_sq - 2.0 * gram, out_ref)


def sum_kernel(parts_ref, before_ref, out_ref):
    total = jnp.sum(parts_ref[...], axis=0)
    out_ref[...] = jnp.broadcast_to(total[None], out_ref.shape)


def sweep_kernel(cost_ref, data_ref, out_ref, pots_ref, bias, kern, row_pot, col_pot, col_fac):
    bias[...] = whole_of(cost_ref) * (-1.0 / (LATENT * BIT))
    col_pot[...] = jnp.zeros_like(col_pot)

    def log_sweep():
        scaled = bias[...] + col_pot[...]
        top = jnp.max(scaled, axis=0, keepdims=True)
        row = -(top + jnp.log2(jnp.sum(jnp.exp2(scaled - top), axis=0, keepdims=True)))
        scaled = bias[...] + row
        top = jnp.max(scaled, axis=1, keepdims=True)
        col = -(top + jnp.log2(jnp.sum(jnp.exp2(scaled - top), axis=1, keepdims=True)))
        row_pot[...] = row
        col_pot[...] = col
        kern[...] = jnp.exp2(scaled + col)

    log_sweep()
    col_fac[...] = jnp.ones_like(col_fac)

    tile = (8, LANES)
    blocks = [pl.ds(start, 8) for start in range(0, BATCH, 8)]
    halves = [pl.ds(start, LANES) for start in range(0, BATCH, LANES)]

    def sweep(step, carry):
        low, high, _ = carry
        sums = [[jnp.zeros(tile, jnp.float32) for _ in halves] for _ in range(2)]
        for n, block in enumerate(blocks):
            factor = col_fac[block, :]
            for h, half in enumerate(halves):
                sums[n % 2][h] += kern[block, half] * factor
        rows = []
        for first, second in zip(*sums):
            total = jnp.broadcast_to(jnp.sum(first + second, axis=0, keepdims=True), tile)
            low, high = jnp.minimum(low, total), jnp.maximum(high, total)
            rows.append(1.0 / total)
        for block in blocks:
            total = sum(kern[block, half] * row for half, row in zip(halves, rows))
            total = jnp.broadcast_to(jnp.sum(total, axis=1, keepdims=True), tile)
            low, high = jnp.minimum(low, total), jnp.maximum(high, total)
            col_fac[block, :] = 1.0 / total
        return (low, high, tuple(rows))

    ones = jnp.ones(tile, jnp.float32)
    low, high, rows = lax.fori_loop(1, SWEEPS, sweep, (ones, ones, (ones, ones)))
    near = (jnp.min(low) >= 1.0 / DRIFT) & (jnp.max(high) <= DRIFT)

    @pl.when(near)
    def _():
        factor = col_fac[...]
        row_pot[...] += jnp.log2(jnp.concatenate([row[:1] for row in rows], axis=1))
        col_pot[...] += jnp.log2(factor[:, :1])
        kern[...] *= jnp.concatenate([factor, factor], axis=1)

    @pl.when(jnp.logical_not(near))
    def _():
        col_pot[...] = jnp.zeros_like(col_pot)

        def again(step, carry):
            log_sweep()
            return carry

        lax.fori_loop(0, SWEEPS, again, 0)

    near = jnp.min(jnp.sum(kern[...], axis=0, keepdims=True)) >= 1.0 / DRIFT

    @pl.when(jnp.logical_not(near))
    def _():
        scaled = bias[...] + col_pot[...]
        kern[...] = jnp.exp2(scaled - jnp.max(scaled, axis=0, keepdims=True))

    scaled = kern[...]
    weights = (scaled / jnp.sum(scaled, axis=0, keepdims=True)).astype(jnp.bfloat16)
    moved = lax.dot_general(
        weights, data_ref[...], (((0,), (0,)), ((), ())), preferred_element_type=jnp.float32
    )
    out_ref[...] = moved.astype(jnp.bfloat16).reshape(out_ref.shape)
    pots_ref[0:1, :] = row_pot[...] * BIT
    pots_ref[1:2, :] = jnp.transpose(col_pot[...] * BIT)


def on_device(noise, data):
    devices = lax.axis_size(AXES)
    own = noise.shape[0]
    ent = UNITS * UNIT
    units = LATENT // UNIT
    params = pltpu.CompilerParams(vmem_limit_bytes=VMEM)
    anywhere = pl.BlockSpec(memory_space=pl.ANY)

    def units_of(rows):
        return rows.reshape(own, units, UNIT).transpose(1, 0, 2)

    both = pl.pallas_call(
        pack_kernel,
        out_shape=jax.ShapeDtypeStruct((devices, 2 * UNITS, own, UNIT), noise.dtype),
        in_specs=[pl.BlockSpec(memory_space=pltpu.HBM)] * 2,
        out_specs=anywhere,
        scratch_shapes=[
            pltpu.VMEM((UNITS * devices - units, own, UNIT), noise.dtype),
            pltpu.SemaphoreType.DMA((4 * UNITS,)),
        ],
        compiler_params=params,
    )(*[pltpu.with_memory_space_constraint(units_of(rows), pltpu.HBM) for rows in (noise, data)])
    both = both.transpose(0, 2, 1, 3).reshape(devices, own, 2 * ent)
    both = lax.all_to_all(both, AXES, split_axis=0, concat_axis=0)

    pieces = jax.ShapeDtypeStruct((devices, 4, LANES), jnp.float32)
    parts, data_ent = pl.pallas_call(
        gram_kernel,
        out_shape=(pieces, jax.ShapeDtypeStruct((BATCH, ent), data.dtype)),
        compiler_params=params,
    )(both)
    whole = pl.BlockSpec(memory_space=pltpu.VMEM)
    noise_sq = pl.pallas_call(
        square_kernel,
        out_shape=jax.ShapeDtypeStruct((own, LANES), jnp.float32),
        in_specs=[whole, anywhere],
        out_specs=whole,
        compiler_params=params,
    )(noise, parts)
    parts = lax.all_to_all(parts, AXES, split_axis=0, concat_axis=0)
    total = pl.pallas_call(
        sum_kernel,
        out_shape=pieces,
        in_specs=[whole, anywhere],
        out_specs=whole,
        compiler_params=params,
    )(parts, noise_sq)
    total = lax.all_to_all(total, AXES, split_axis=0, concat_axis=0)

    moved, pots = pl.pallas_call(
        sweep_kernel,
        out_shape=(
            jax.ShapeDtypeStruct((devices, own, ent), jnp.bfloat16),
            jax.ShapeDtypeStruct((2, BATCH), jnp.float32),
        ),
        scratch_shapes=[
            pltpu.VMEM((BATCH, BATCH), jnp.float32),
            pltpu.VMEM((BATCH, BATCH), jnp.float32),
            pltpu.VMEM((1, BATCH), jnp.float32),
            pltpu.VMEM((BATCH, 1), jnp.float32),
            pltpu.VMEM((BATCH, LANES), jnp.float32),
        ],
        compiler_params=params,
    )(total, data_ent)
    moved = lax.all_to_all(moved, AXES, split_axis=0, concat_axis=0)
    moved = moved.reshape(devices, own, UNITS, UNIT).transpose(0, 2, 1, 3)
    scalars = pl.BlockSpec(memory_space=pltpu.SMEM)
    targets, row, col = pl.pallas_call(
        unpack_kernel,
        out_shape=(
            jax.ShapeDtypeStruct((units, own, UNIT), moved.dtype),
            jax.ShapeDtypeStruct((own,), jnp.float32),
            jax.ShapeDtypeStruct((own,), jnp.float32),
        ),
        in_specs=[anywhere, whole, whole],
        out_specs=(anywhere, scalars, scalars),
        scratch_shapes=[pltpu.SemaphoreType.DMA((UNITS,))],
        compiler_params=params,
    )(moved, pots, noise_sq)
    return (targets.transpose(1, 0, 2).reshape(own, LATENT), row, col)


def solution(mesh):
    return jax.shard_map(
        on_device,
        mesh=mesh,
        in_specs=(P(AXES, None), P(AXES, None)),
        out_specs=(P(AXES, None), P(AXES), P(AXES)),
        check_vma=False,
    )
```

```python
import math

import jax
import jax.numpy as jnp
from jax import lax
from jax.experimental import pallas as pl
from jax.experimental.pallas import tpu as pltpu
from jax.sharding import PartitionSpec as P

SWEEPS = 20
LATENT = 324480
BATCH = 256
AXES = ("dp", "dim")
LANES = 128
TEMPER = 0.25 / math.sqrt(LATENT)
BIT = TEMPER * math.log(2.0)
DRIFT = 2.0**40
VMEM = 24 * 1024 * 1024
UNITS = 4
UNIT = 640


def pack_kernel(noise_ref, data_ref, out_ref, zeros, sems):
    devices, units = out_ref.shape[0], noise_ref.shape[0]
    zeros[...] = jnp.zeros_like(zeros)
    copies = []
    for kind, ref in enumerate((noise_ref, data_ref)):
        for q in range(UNITS):
            slot = kind * UNITS + q
            start = q * devices
            count = min(devices, units - start)
            copies.append((ref.at[pl.ds(start, count)], out_ref.at[pl.ds(0, count), slot]))
            if count < devices:
                copies.append((zeros, out_ref.at[pl.ds(count, devices - count), slot]))
    copies = [pltpu.make_async_copy(src, dst, sems.at[n]) for n, (src, dst) in enumerate(copies)]
    for copy in copies:
        copy.start()
    for copy in copies:
        copy.wait()


def unpack_kernel(moved_ref, pots_ref, noise_ref, out_ref, row_ref, col_ref, row, col, sems):
    devices, units = moved_ref.shape[0], out_ref.shape[0]
    own = out_ref.shape[1]
    copies = []
    for q in range(UNITS):
        start = q * devices
        count = min(devices, units - start)
        copies.append((moved_ref.at[pl.ds(0, count), q], out_ref.at[pl.ds(start, count)]))
    copies.extend([(row, row_ref), (col, col_ref)])
    copies = [pltpu.make_async_copy(src, dst, sems.at[n]) for n, (src, dst) in enumerate(copies)]
    for copy in copies[:UNITS]:
        copy.start()

    def add(n, total):
        unit = noise_ref[:, pl.ds(pl.multiple_of(n * UNIT, UNIT), UNIT)].astype(jnp.float32)
        return total + unit * unit

    noise_sq = jnp.zeros((own, UNIT), jnp.float32)
    noise_sq = lax.fori_loop(0, units, add, noise_sq, unroll=13)
    noise_sq = jnp.sum(noise_sq, axis=1, keepdims=True)
    first = (lax.axis_index("dp") * lax.axis_size("dim") + lax.axis_index("dim")) * own
    lane = lax.broadcasted_iota(jnp.int32, (1, BATCH), 1)
    for n in range(own):
        mine = lane == first + n
        row_pot = jnp.sum(jnp.where(mine, pots_ref[0:1, :], 0.0))
        row[n] = row_pot + jnp.sum(noise_sq[n : n + 1, :]) / LATENT
        col[n] = jnp.sum(jnp.where(mine, pots_ref[1:2, :], 0.0))
    for copy in copies[UNITS:]:
        copy.start()
    for copy in copies:
        copy.wait()


def pieces_of(value, pieces_ref):
    for piece in range(BATCH * 2 // 4):
        row, half = 4 * (piece // 2), LANES * (piece % 2)
        pieces_ref[piece] = value[row : row + 4, half : half + LANES]


def whole_of(pieces_ref):
    rows = []
    for row in range(BATCH // 4):
        rows.append(jnp.concatenate([pieces_ref[2 * row], pieces_ref[2 * row + 1]], axis=1))
    return jnp.concatenate(rows, axis=0)


def gram_kernel(both_ref, out_ref, data_ref):
    ent = data_ref.shape[1]
    noise = both_ref[:, :, :ent].reshape(data_ref.shape)
    data = both_ref[:, :, ent:].reshape(data_ref.shape)
    data_ref[...] = data
    gram = lax.dot_general(
        data, noise, (((1,), (1,)), ((), ())), preferred_element_type=jnp.float32
    )
    wide = data.astype(jnp.float32)
    data_sq = jnp.sum(wide * wide, axis=1, keepdims=True)
    pieces_of(data_sq - 2.0 * gram, out_ref)


def sum_kernel(parts_ref, out_ref):
    total = jnp.sum(parts_ref[...], axis=0)
    out_ref[...] = jnp.broadcast_to(total[None], out_ref.shape)


def sweep_kernel(cost_ref, data_ref, out_ref, pots_ref, bias, kern, row_pot, col_pot, col_fac):
    bias[...] = whole_of(cost_ref) * (-1.0 / (LATENT * BIT))
    col_pot[...] = jnp.zeros_like(col_pot)

    def log_sweep():
        scaled = bias[...] + col_pot[...]
        top = jnp.max(scaled, axis=0, keepdims=True)
        row = -(top + jnp.log2(jnp.sum(jnp.exp2(scaled - top), axis=0, keepdims=True)))
        scaled = bias[...] + row
        top = jnp.max(scaled, axis=1, keepdims=True)
        col = -(top + jnp.log2(jnp.sum(jnp.exp2(scaled - top), axis=1, keepdims=True)))
        row_pot[...] = row
        col_pot[...] = col
        kern[...] = jnp.exp2(scaled + col)

    log_sweep()
    col_fac[...] = jnp.ones_like(col_fac)

    tile = (8, LANES)
    blocks = [pl.ds(start, 8) for start in range(0, BATCH, 8)]
    halves = [pl.ds(start, LANES) for start in range(0, BATCH, LANES)]

    def sweep(step, carry):
        low, high, _ = carry
        sums = [[jnp.zeros(tile, jnp.float32) for _ in halves] for _ in range(2)]
        for n, block in enumerate(blocks):
            factor = col_fac[block, :]
            for h, half in enumerate(halves):
                sums[n % 2][h] += kern[block, half] * factor
        rows = []
        for first, second in zip(*sums):
            total = jnp.broadcast_to(jnp.sum(first + second, axis=0, keepdims=True), tile)
            low, high = jnp.minimum(low, total), jnp.maximum(high, total)
            rows.append(1.0 / total)
        for block in blocks:
            total = sum(kern[block, half] * row for half, row in zip(halves, rows))
            total = jnp.broadcast_to(jnp.sum(total, axis=1, keepdims=True), tile)
            low, high = jnp.minimum(low, total), jnp.maximum(high, total)
            col_fac[block, :] = 1.0 / total
        return (low, high, tuple(rows))

    ones = jnp.ones(tile, jnp.float32)
    low, high, rows = lax.fori_loop(1, SWEEPS, sweep, (ones, ones, (ones, ones)))
    near = (jnp.min(low) >= 1.0 / DRIFT) & (jnp.max(high) <= DRIFT)

    @pl.when(near)
    def _():
        factor = col_fac[...]
        row_pot[...] += jnp.log2(jnp.concatenate([row[:1] for row in rows], axis=1))
        col_pot[...] += jnp.log2(factor[:, :1])
        kern[...] *= jnp.concatenate([factor, factor], axis=1)

    @pl.when(jnp.logical_not(near))
    def _():
        col_pot[...] = jnp.zeros_like(col_pot)

        def again(step, carry):
            log_sweep()
            return carry

        lax.fori_loop(0, SWEEPS, again, 0)

    near = jnp.min(jnp.sum(kern[...], axis=0, keepdims=True)) >= 1.0 / DRIFT

    @pl.when(jnp.logical_not(near))
    def _():
        scaled = bias[...] + col_pot[...]
        kern[...] = jnp.exp2(scaled - jnp.max(scaled, axis=0, keepdims=True))

    scaled = kern[...]
    weights = (scaled / jnp.sum(scaled, axis=0, keepdims=True)).astype(jnp.bfloat16)
    moved = lax.dot_general(
        weights, data_ref[...], (((0,), (0,)), ((), ())), preferred_element_type=jnp.float32
    )
    out_ref[...] = moved.astype(jnp.bfloat16).reshape(out_ref.shape)
    pots_ref[0:1, :] = row_pot[...] * BIT
    pots_ref[1:2, :] = jnp.transpose(col_pot[...] * BIT)


def on_device(noise, data):
    devices = lax.axis_size(AXES)
    own = noise.shape[0]
    ent = UNITS * UNIT
    units = LATENT // UNIT
    params = pltpu.CompilerParams(vmem_limit_bytes=VMEM)
    anywhere = pl.BlockSpec(memory_space=pl.ANY)

    def units_of(rows):
        return rows.reshape(own, units, UNIT).transpose(1, 0, 2)

    both = pl.pallas_call(
        pack_kernel,
        out_shape=jax.ShapeDtypeStruct((devices, 2 * UNITS, own, UNIT), noise.dtype),
        in_specs=[pl.BlockSpec(memory_space=pltpu.HBM)] * 2,
        out_specs=anywhere,
        scratch_shapes=[
            pltpu.VMEM((UNITS * devices - units, own, UNIT), noise.dtype),
            pltpu.SemaphoreType.DMA((4 * UNITS,)),
        ],
        compiler_params=params,
    )(*[pltpu.with_memory_space_constraint(units_of(rows), pltpu.HBM) for rows in (noise, data)])
    both = both.transpose(0, 2, 1, 3).reshape(devices, own, 2 * ent)
    both = lax.all_to_all(both, AXES, split_axis=0, concat_axis=0)

    pieces = jax.ShapeDtypeStruct((devices, 4, LANES), jnp.float32)
    parts, data_ent = pl.pallas_call(
        gram_kernel,
        out_shape=(pieces, jax.ShapeDtypeStruct((BATCH, ent), data.dtype)),
        compiler_params=params,
    )(both)
    parts = lax.all_to_all(parts, AXES, split_axis=0, concat_axis=0)
    total = pl.pallas_call(sum_kernel, out_shape=pieces, compiler_params=params)(parts)
    total = lax.all_to_all(total, AXES, split_axis=0, concat_axis=0)

    moved, pots = pl.pallas_call(
        sweep_kernel,
        out_shape=(
            jax.ShapeDtypeStruct((devices, own, ent), jnp.bfloat16),
            jax.ShapeDtypeStruct((2, BATCH), jnp.float32),
        ),
        scratch_shapes=[
            pltpu.VMEM((BATCH, BATCH), jnp.float32),
            pltpu.VMEM((BATCH, BATCH), jnp.float32),
            pltpu.VMEM((1, BATCH), jnp.float32),
            pltpu.VMEM((BATCH, 1), jnp.float32),
            pltpu.VMEM((BATCH, LANES), jnp.float32),
        ],
        compiler_params=params,
    )(total, data_ent)
    moved = lax.all_to_all(moved, AXES, split_axis=0, concat_axis=0)
    moved = moved.reshape(devices, own, UNITS, UNIT).transpose(0, 2, 1, 3)
    whole = pl.BlockSpec(memory_space=pltpu.VMEM)
    targets, row, col = pl.pallas_call(
        unpack_kernel,
        out_shape=(
            jax.ShapeDtypeStruct((units, own, UNIT), moved.dtype),
            jax.ShapeDtypeStruct((own,), jnp.float32),
            jax.ShapeDtypeStruct((own,), jnp.float32),
        ),
        in_specs=[anywhere, whole, whole],
        out_specs=(anywhere, anywhere, anywhere),
        scratch_shapes=[
            pltpu.SMEM((own,), jnp.float32),
            pltpu.SMEM((own,), jnp.float32),
            pltpu.SemaphoreType.DMA((UNITS + 2,)),
        ],
        compiler_params=params,
    )(moved, pots, noise)
    return (targets.transpose(1, 0, 2).reshape(own, LATENT), row, col)


def solution(mesh):
    return jax.shard_map(
        on_device,
        mesh=mesh,
        in_specs=(P(AXES, None), P(AXES, None)),
        out_specs=(P(AXES, None), P(AXES), P(AXES)),
        check_vma=False,
    )
```

```python
import math

import jax
import jax.numpy as jnp
from jax import lax
from jax.experimental import pallas as pl
from jax.experimental.pallas import tpu as pltpu
from jax.sharding import PartitionSpec as P

SWEEPS = 20
LATENT = 324480
BATCH = 256
AXES = ("dp", "dim")
LANES = 128
TEMPER = 0.25 / math.sqrt(LATENT)
BIT = TEMPER * math.log(2.0)
DRIFT = 2.0**40
VMEM = 24 * 1024 * 1024
UNITS = 4
UNIT = 640


def pack_kernel(noise_ref, data_ref, out_ref, zeros, sems):
    devices, units = out_ref.shape[0], noise_ref.shape[0]
    zeros[...] = jnp.zeros_like(zeros)
    copies = []
    for kind, ref in enumerate((noise_ref, data_ref)):
        for q in range(UNITS):
            slot = kind * UNITS + q
            start = q * devices
            count = min(devices, units - start)
            copies.append((ref.at[pl.ds(start, count)], out_ref.at[pl.ds(0, count), slot]))
            if count < devices:
                copies.append((zeros, out_ref.at[pl.ds(count, devices - count), slot]))
    copies = [pltpu.make_async_copy(src, dst, sems.at[n]) for n, (src, dst) in enumerate(copies)]
    for copy in copies:
        copy.start()
    for copy in copies:
        copy.wait()


def unpack_kernel(moved_ref, pots_ref, noise_ref, out_ref, row_ref, col_ref, row, col, sems):
    devices, units = moved_ref.shape[0], out_ref.shape[0]
    own = out_ref.shape[1]
    copies = []
    for q in range(UNITS):
        start = q * devices
        count = min(devices, units - start)
        copies.append((moved_ref.at[pl.ds(0, count), q], out_ref.at[pl.ds(start, count)]))
    copies.extend([(row, row_ref), (col, col_ref)])
    copies = [pltpu.make_async_copy(src, dst, sems.at[n]) for n, (src, dst) in enumerate(copies)]
    for copy in copies[:UNITS]:
        copy.start()

    def add(n, total):
        unit = noise_ref[:, pl.ds(pl.multiple_of(n * UNIT, UNIT), UNIT)].astype(jnp.float32)
        return total + unit * unit

    noise_sq = jnp.zeros((own, UNIT), jnp.float32)
    noise_sq = lax.fori_loop(0, units, add, noise_sq, unroll=13)
    noise_sq = jnp.sum(noise_sq, axis=1, keepdims=True)
    first = (lax.axis_index("dp") * lax.axis_size("dim") + lax.axis_index("dim")) * own
    lane = lax.broadcasted_iota(jnp.int32, (1, BATCH), 1)
    for n in range(own):
        mine = lane == first + n
        row_pot = jnp.sum(jnp.where(mine, pots_ref[0:1, :], 0.0))
        row[n] = row_pot + jnp.sum(noise_sq[n : n + 1, :]) / LATENT
        col[n] = jnp.sum(jnp.where(mine, pots_ref[1:2, :], 0.0))
    for copy in copies[UNITS:]:
        copy.start()
    for copy in copies:
        copy.wait()


def pieces_of(value, pieces_ref):
    for piece in range(BATCH * 2 // 4):
        row, half = 4 * (piece // 2), LANES * (piece % 2)
        pieces_ref[piece] = value[row : row + 4, half : half + LANES]


def whole_of(pieces_ref):
    rows = []
    for row in range(BATCH // 4):
        rows.append(jnp.concatenate([pieces_ref[2 * row], pieces_ref[2 * row + 1]], axis=1))
    return jnp.concatenate(rows, axis=0)


def gram_kernel(both_ref, out_ref, data_ref):
    ent = data_ref.shape[1]
    noise = both_ref[:, :, :ent].reshape(data_ref.shape)
    data = both_ref[:, :, ent:].reshape(data_ref.shape)
    data_ref[...] = data
    gram = lax.dot_general(
        data, noise, (((1,), (1,)), ((), ())), preferred_element_type=jnp.float32
    )
    wide = data.astype(jnp.float32)
    data_sq = jnp.sum(wide * wide, axis=1, keepdims=True)
    pieces_of(data_sq - 2.0 * gram, out_ref)


def sum_kernel(parts_ref, out_ref):
    total = jnp.sum(parts_ref[...], axis=0)
    out_ref[...] = jnp.broadcast_to(total[None], out_ref.shape)


def sweep_kernel(cost_ref, data_ref, out_ref, pots_ref, bias, kern, row_pot, col_pot, row_sum):
    bias[...] = whole_of(cost_ref) * (-1.0 / (LATENT * BIT))
    col_pot[...] = jnp.zeros_like(col_pot)

    def log_sweep():
        scaled = bias[...] + col_pot[...]
        top = jnp.max(scaled, axis=0, keepdims=True)
        row = -(top + jnp.log2(jnp.sum(jnp.exp2(scaled - top), axis=0, keepdims=True)))
        scaled = bias[...] + row
        top = jnp.max(scaled, axis=1, keepdims=True)
        scaled = jnp.exp2(scaled - top)
        total = jnp.sum(scaled, axis=1, keepdims=True)
        row_pot[...] = row
        col_pot[...] = -(top + jnp.log2(total))
        kern[...] = scaled * (1.0 / total)

    log_sweep()

    tile = (8, LANES)
    blocks = [pl.ds(start, 8) for start in range(0, BATCH, 8)]
    halves = [pl.ds(start, LANES) for start in range(0, BATCH, LANES)]

    def over_columns(low, high, rows, use):
        sums = [[jnp.zeros(tile, jnp.float32) for _ in halves] for _ in range(2)]
        for n, block in enumerate(blocks):
            parts = [kern[block, half] for half in halves]
            if rows is not None:
                total = sum(part * row for part, row in zip(parts, rows))
                total = jnp.broadcast_to(jnp.sum(total, axis=1, keepdims=True), tile)
                low, high = jnp.minimum(low, total), jnp.maximum(high, total)
                factor = 1.0 / total
                parts = [part * factor for part in parts]
                if use is not None:
                    use(block, factor, parts)
            for h, part in enumerate(parts):
                sums[n % 2][h] += part
        totals = []
        for first, second in zip(*sums):
            total = jnp.broadcast_to(jnp.sum(first + second, axis=0, keepdims=True), tile)
            low = jnp.minimum(low, total)
            totals.append(total)
        return low, high, totals

    def sweep(step, carry):
        low, high, rows = carry
        low, high, totals = over_columns(low, high, rows, None)
        for total in totals:
            high = jnp.maximum(high, total)
        return (low, high, tuple(1.0 / total for total in totals))

    def finish(block, factor, parts):
        col_pot[block, :] += jnp.log2(factor[:, :1])
        for half, part in zip(halves, parts):
            kern[block, half] = part

    ones = jnp.ones(tile, jnp.float32)
    carry = sweep(0, (ones, ones, None))
    low, high, rows = lax.fori_loop(2, SWEEPS, sweep, carry)
    low, high, totals = over_columns(low, high, rows, finish)
    row_pot[...] += jnp.log2(jnp.concatenate([row[:1] for row in rows], axis=1))
    row_sum[...] = jnp.concatenate([total[:1] for total in totals], axis=1)
    near = jnp.min(jnp.where((low >= 1.0 / DRIFT) & (high <= DRIFT), 1.0, 0.0)) > 0.5

    @pl.when(jnp.logical_not(near))
    def _():
        col_pot[...] = jnp.zeros_like(col_pot)

        def again(step, carry):
            log_sweep()
            return carry

        lax.fori_loop(0, SWEEPS, again, 0)
        scaled = bias[...] + col_pot[...]
        scaled = jnp.exp2(scaled - jnp.max(scaled, axis=0, keepdims=True))
        kern[...] = scaled
        row_sum[...] = jnp.sum(scaled, axis=0, keepdims=True)

    weights = (kern[...] * (1.0 / row_sum[...])).astype(jnp.bfloat16)
    moved = lax.dot_general(
        weights, data_ref[...], (((0,), (0,)), ((), ())), preferred_element_type=jnp.float32
    )
    out_ref[...] = moved.astype(jnp.bfloat16).reshape(out_ref.shape)
    pots_ref[0:1, :] = row_pot[...] * BIT
    pots_ref[1:2, :] = jnp.transpose(col_pot[...] * BIT)


def on_device(noise, data):
    devices = lax.axis_size(AXES)
    own = noise.shape[0]
    ent = UNITS * UNIT
    units = LATENT // UNIT
    params = pltpu.CompilerParams(vmem_limit_bytes=VMEM)
    anywhere = pl.BlockSpec(memory_space=pl.ANY)

    def units_of(rows):
        return rows.reshape(own, units, UNIT).transpose(1, 0, 2)

    both = pl.pallas_call(
        pack_kernel,
        out_shape=jax.ShapeDtypeStruct((devices, 2 * UNITS, own, UNIT), noise.dtype),
        in_specs=[pl.BlockSpec(memory_space=pltpu.HBM)] * 2,
        out_specs=anywhere,
        scratch_shapes=[
            pltpu.VMEM((UNITS * devices - units, own, UNIT), noise.dtype),
            pltpu.SemaphoreType.DMA((4 * UNITS,)),
        ],
        compiler_params=params,
    )(*[pltpu.with_memory_space_constraint(units_of(rows), pltpu.HBM) for rows in (noise, data)])
    both = both.transpose(0, 2, 1, 3).reshape(devices, own, 2 * ent)
    both = lax.all_to_all(both, AXES, split_axis=0, concat_axis=0)

    pieces = jax.ShapeDtypeStruct((devices, 4, LANES), jnp.float32)
    parts, data_ent = pl.pallas_call(
        gram_kernel,
        out_shape=(pieces, jax.ShapeDtypeStruct((BATCH, ent), data.dtype)),
        compiler_params=params,
    )(both)
    parts = lax.all_to_all(parts, AXES, split_axis=0, concat_axis=0)
    total = pl.pallas_call(sum_kernel, out_shape=pieces, compiler_params=params)(parts)
    total = lax.all_to_all(total, AXES, split_axis=0, concat_axis=0)

    moved, pots = pl.pallas_call(
        sweep_kernel,
        out_shape=(
            jax.ShapeDtypeStruct((devices, own, ent), jnp.bfloat16),
            jax.ShapeDtypeStruct((2, BATCH), jnp.float32),
        ),
        scratch_shapes=[
            pltpu.VMEM((BATCH, BATCH), jnp.float32),
            pltpu.VMEM((BATCH, BATCH), jnp.float32),
            pltpu.VMEM((1, BATCH), jnp.float32),
            pltpu.VMEM((BATCH, 1), jnp.float32),
            pltpu.VMEM((1, BATCH), jnp.float32),
        ],
        compiler_params=params,
    )(total, data_ent)
    moved = lax.all_to_all(moved, AXES, split_axis=0, concat_axis=0)
    moved = moved.reshape(devices, own, UNITS, UNIT).transpose(0, 2, 1, 3)
    whole = pl.BlockSpec(memory_space=pltpu.VMEM)
    targets, row, col = pl.pallas_call(
        unpack_kernel,
        out_shape=(
            jax.ShapeDtypeStruct((units, own, UNIT), moved.dtype),
            jax.ShapeDtypeStruct((own,), jnp.float32),
            jax.ShapeDtypeStruct((own,), jnp.float32),
        ),
        in_specs=[anywhere, whole, whole],
        out_specs=(anywhere, anywhere, anywhere),
        scratch_shapes=[
            pltpu.SMEM((own,), jnp.float32),
            pltpu.SMEM((own,), jnp.float32),
            pltpu.SemaphoreType.DMA((UNITS + 2,)),
        ],
        compiler_params=params,
    )(moved, pots, noise)
    return (targets.transpose(1, 0, 2).reshape(own, LATENT), row, col)


def solution(mesh):
    return jax.shard_map(
        on_device,
        mesh=mesh,
        in_specs=(P(AXES, None), P(AXES, None)),
        out_specs=(P(AXES, None), P(AXES), P(AXES)),
        check_vma=False,
    )
```

```python
import math

import jax
import jax.numpy as jnp
from jax import lax
from jax.experimental import pallas as pl
from jax.experimental.pallas import tpu as pltpu
from jax.sharding import PartitionSpec as P

SWEEPS = 20
LATENT = 324480
BATCH = 256
AXES = ("dp", "dim")
LANES = 128
TEMPER = 0.25 / math.sqrt(LATENT)
BIT = TEMPER * math.log(2.0)
DRIFT = 2.0**40
VMEM = 24 * 1024 * 1024
UNITS = 4
UNIT = 640


def pack_kernel(noise_ref, data_ref, out_ref, noise_sq_ref, sems):
    devices, units = out_ref.shape[0], noise_ref.shape[0]
    copies = []
    for kind, ref in enumerate((noise_ref, data_ref)):
        for q in range(UNITS):
            slot = kind * UNITS + q
            start = q * devices
            count = min(devices, units - start)
            copies.append(
                pltpu.make_async_copy(
                    ref.at[pl.ds(start, count)], out_ref.at[pl.ds(0, count), slot], sems.at[slot]
                )
            )
    for copy in copies:
        copy.start()
    rest = UNITS * devices - units
    for kind in range(2):
        slot = kind * UNITS + UNITS - 1
        out_ref[devices - rest :, slot] = jnp.zeros((rest,) + out_ref.shape[2:], out_ref.dtype)
    for copy in copies[:UNITS]:
        copy.wait()

    def add(n, total):
        for q in range(UNITS):
            unit = out_ref[n, q].astype(jnp.float32)
            total = total + unit * unit
        return total

    total = jnp.zeros(out_ref.shape[2:], jnp.float32)
    total = lax.fori_loop(0, devices, add, total, unroll=8)
    total = jnp.sum(total, axis=1, keepdims=True)
    noise_sq_ref[...] = jnp.broadcast_to(total, noise_sq_ref.shape)
    for copy in copies[UNITS:]:
        copy.wait()


def unpack_kernel(moved_ref, out_ref, sems):
    devices, units = moved_ref.shape[0], out_ref.shape[0]
    copies = []
    for q in range(UNITS):
        start = q * devices
        count = min(devices, units - start)
        copies.append(
            pltpu.make_async_copy(
                moved_ref.at[pl.ds(0, count), q], out_ref.at[pl.ds(start, count)], sems.at[q]
            )
        )
    for copy in copies:
        copy.start()
    for copy in copies:
        copy.wait()


def pieces_of(value, pieces_ref):
    for piece in range(BATCH * 2 // 4):
        row, half = 4 * (piece // 2), LANES * (piece % 2)
        pieces_ref[piece] = value[row : row + 4, half : half + LANES]


def whole_of(pieces_ref):
    rows = []
    for row in range(BATCH // 4):
        rows.append(jnp.concatenate([pieces_ref[2 * row], pieces_ref[2 * row + 1]], axis=1))
    return jnp.concatenate(rows, axis=0)


def gram_kernel(both_ref, out_ref, data_ref):
    ent = data_ref.shape[1]
    noise = both_ref[:, :, :ent].reshape(data_ref.shape)
    data = both_ref[:, :, ent:].reshape(data_ref.shape)
    data_ref[...] = data
    gram = lax.dot_general(
        data, noise, (((1,), (1,)), ((), ())), preferred_element_type=jnp.float32
    )
    wide = data.astype(jnp.float32)
    data_sq = jnp.sum(wide * wide, axis=1, keepdims=True)
    pieces_of(data_sq - 2.0 * gram, out_ref)


def sum_kernel(parts_ref, out_ref):
    total = jnp.sum(parts_ref[...], axis=0)
    out_ref[...] = jnp.broadcast_to(total[None], out_ref.shape)


def sweep_kernel(
    cost_ref, data_ref, noise_sq_ref, out_ref, row_ref, col_ref,
    bias, kern, row_pot, col_pot, row_sum, row_own, col_own, sems,
):
    bias[...] = whole_of(cost_ref) * (-1.0 / (LATENT * BIT))
    col_pot[...] = jnp.zeros_like(col_pot)

    def log_sweep():
        scaled = bias[...] + col_pot[...]
        top = jnp.max(scaled, axis=0, keepdims=True)
        row = -(top + jnp.log2(jnp.sum(jnp.exp2(scaled - top), axis=0, keepdims=True)))
        scaled = bias[...] + row
        top = jnp.max(scaled, axis=1, keepdims=True)
        scaled = jnp.exp2(scaled - top)
        total = jnp.sum(scaled, axis=1, keepdims=True)
        row_pot[...] = row
        col_pot[...] = -(top + jnp.log2(total))
        kern[...] = scaled * (1.0 / total)

    log_sweep()

    tile = (8, LANES)
    blocks = [pl.ds(start, 8) for start in range(0, BATCH, 8)]
    halves = [pl.ds(start, LANES) for start in range(0, BATCH, LANES)]

    def over_columns(low, high, rows, use):
        sums = [[jnp.zeros(tile, jnp.float32) for _ in halves] for _ in range(2)]
        for n, block in enumerate(blocks):
            parts = [kern[block, half] for half in halves]
            if rows is not None:
                total = sum(part * row for part, row in zip(parts, rows))
                total = jnp.broadcast_to(jnp.sum(total, axis=1, keepdims=True), tile)
                low, high = jnp.minimum(low, total), jnp.maximum(high, total)
                factor = 1.0 / total
                parts = [part * factor for part in parts]
                if use is not None:
                    use(block, factor, parts)
            for h, part in enumerate(parts):
                sums[n % 2][h] += part
        totals = []
        for first, second in zip(*sums):
            total = jnp.broadcast_to(jnp.sum(first + second, axis=0, keepdims=True), tile)
            low = jnp.minimum(low, total)
            totals.append(total)
        return low, high, totals

    def sweep(step, carry):
        low, high, rows = carry
        low, high, totals = over_columns(low, high, rows, None)
        for total in totals:
            high = jnp.maximum(high, total)
        return (low, high, tuple(1.0 / total for total in totals))

    def finish(block, factor, parts):
        col_pot[block, :] += jnp.log2(factor[:, :1])
        for half, part in zip(halves, parts):
            kern[block, half] = part

    ones = jnp.ones(tile, jnp.float32)
    carry = sweep(0, (ones, ones, None))
    low, high, rows = lax.fori_loop(2, SWEEPS, sweep, carry)
    low, high, totals = over_columns(low, high, rows, finish)
    row_pot[...] += jnp.log2(jnp.concatenate([row[:1] for row in rows], axis=1))
    row_sum[...] = jnp.concatenate([total[:1] for total in totals], axis=1)
    near = jnp.min(jnp.where((low >= 1.0 / DRIFT) & (high <= DRIFT), 1.0, 0.0)) > 0.5

    @pl.when(jnp.logical_not(near))
    def _():
        col_pot[...] = jnp.zeros_like(col_pot)

        def again(step, carry):
            log_sweep()
            return carry

        lax.fori_loop(0, SWEEPS, again, 0)
        scaled = bias[...] + col_pot[...]
        scaled = jnp.exp2(scaled - jnp.max(scaled, axis=0, keepdims=True))
        kern[...] = scaled
        row_sum[...] = jnp.sum(scaled, axis=0, keepdims=True)

    own = out_ref.shape[1]
    first = (lax.axis_index("dp") * lax.axis_size("dim") + lax.axis_index("dim")) * own
    place = lax.broadcasted_iota(jnp.int32, (1, BATCH), 1)
    rows = row_pot[...]
    cols = jnp.transpose(col_pot[...])
    for n in range(own):
        mine = place == first + n
        row = jnp.sum(jnp.where(mine, rows, 0.0)) * BIT
        row_own[n] = row + jnp.max(noise_sq_ref[n : n + 1, :]) / LATENT
        col_own[n] = jnp.sum(jnp.where(mine, cols, 0.0)) * BIT
    copies = [(row_own, row_ref), (col_own, col_ref)]
    copies = [pltpu.make_async_copy(src, dst, sems.at[n]) for n, (src, dst) in enumerate(copies)]
    for copy in copies:
        copy.start()

    weights = (kern[...] * (1.0 / row_sum[...])).astype(jnp.bfloat16)
    moved = lax.dot_general(
        weights, data_ref[...], (((0,), (0,)), ((), ())), preferred_element_type=jnp.float32
    )
    out_ref[...] = moved.astype(jnp.bfloat16).reshape(out_ref.shape)
    for copy in copies:
        copy.wait()


def on_device(noise, data):
    devices = lax.axis_size(AXES)
    own = noise.shape[0]
    ent = UNITS * UNIT
    units = LATENT // UNIT
    params = pltpu.CompilerParams(vmem_limit_bytes=VMEM)
    anywhere = pl.BlockSpec(memory_space=pl.ANY)
    whole = pl.BlockSpec(memory_space=pltpu.VMEM)

    def units_of(rows):
        return rows.reshape(own, units, UNIT).transpose(1, 0, 2)

    both, noise_sq = pl.pallas_call(
        pack_kernel,
        out_shape=(
            jax.ShapeDtypeStruct((devices, 2 * UNITS, own, UNIT), noise.dtype),
            jax.ShapeDtypeStruct((own, LANES), jnp.float32),
        ),
        in_specs=[anywhere, anywhere],
        out_specs=(whole, whole),
        scratch_shapes=[pltpu.SemaphoreType.DMA((2 * UNITS,))],
        compiler_params=params,
    )(*[pltpu.with_memory_space_constraint(units_of(rows), pltpu.HBM) for rows in (noise, data)])
    both = both.transpose(0, 2, 1, 3).reshape(devices, own, 2 * ent)
    both = lax.all_to_all(both, AXES, split_axis=0, concat_axis=0)

    pieces = jax.ShapeDtypeStruct((devices, 4, LANES), jnp.float32)
    parts, data_ent = pl.pallas_call(
        gram_kernel,
        out_shape=(pieces, jax.ShapeDtypeStruct((BATCH, ent), data.dtype)),
        compiler_params=params,
    )(both)
    parts = lax.all_to_all(parts, AXES, split_axis=0, concat_axis=0)
    total = pl.pallas_call(sum_kernel, out_shape=pieces, compiler_params=params)(parts)
    total = lax.all_to_all(total, AXES, split_axis=0, concat_axis=0)

    scalars = jax.ShapeDtypeStruct((own,), jnp.float32)
    moved, row, col = pl.pallas_call(
        sweep_kernel,
        out_shape=(jax.ShapeDtypeStruct((devices, own, ent), jnp.bfloat16), scalars, scalars),
        in_specs=[whole, whole, whole],
        out_specs=(whole, anywhere, anywhere),
        scratch_shapes=[
            pltpu.VMEM((BATCH, BATCH), jnp.float32),
            pltpu.VMEM((BATCH, BATCH), jnp.float32),
            pltpu.VMEM((1, BATCH), jnp.float32),
            pltpu.VMEM((BATCH, 1), jnp.float32),
            pltpu.VMEM((1, BATCH), jnp.float32),
            pltpu.SMEM((own,), jnp.float32),
            pltpu.SMEM((own,), jnp.float32),
            pltpu.SemaphoreType.DMA((2,)),
        ],
        compiler_params=params,
    )(total, data_ent, noise_sq)
    moved = lax.all_to_all(moved, AXES, split_axis=0, concat_axis=0)
    moved = moved.reshape(devices, own, UNITS, UNIT).transpose(0, 2, 1, 3)
    targets = pl.pallas_call(
        unpack_kernel,
        out_shape=jax.ShapeDtypeStruct((units, own, UNIT), moved.dtype),
        in_specs=[anywhere],
        out_specs=anywhere,
        scratch_shapes=[pltpu.SemaphoreType.DMA((UNITS,))],
        compiler_params=params,
    )(moved)
    return (targets.transpose(1, 0, 2).reshape(own, LATENT), row, col)


def solution(mesh):
    return jax.shard_map(
        on_device,
        mesh=mesh,
        in_specs=(P(AXES, None), P(AXES, None)),
        out_specs=(P(AXES, None), P(AXES), P(AXES)),
        check_vma=False,
    )
```

```python
import math

import jax
import jax.numpy as jnp
from jax import lax
from jax.experimental import pallas as pl
from jax.experimental.pallas import tpu as pltpu
from jax.sharding import PartitionSpec as P

SWEEPS = 20
LATENT = 324480
BATCH = 256
AXES = ("dp", "dim")
LANES = 128
TEMPER = 0.25 / math.sqrt(LATENT)
BIT = TEMPER * math.log(2.0)
DRIFT = 2.0**40
VMEM = 24 * 1024 * 1024
UNITS = 4
UNIT = 640


def pack_kernel(noise_ref, data_ref, out_ref, zeros, sems):
    devices, units = out_ref.shape[0], noise_ref.shape[0]
    zeros[...] = jnp.zeros_like(zeros)
    copies = []
    for kind, ref in enumerate((noise_ref, data_ref)):
        for q in range(UNITS):
            slot = kind * UNITS + q
            start = q * devices
            count = min(devices, units - start)
            copies.append((ref.at[pl.ds(start, count)], out_ref.at[pl.ds(0, count), slot]))
            if count < devices:
                copies.append((zeros, out_ref.at[pl.ds(count, devices - count), slot]))
    copies = [pltpu.make_async_copy(src, dst, sems.at[n]) for n, (src, dst) in enumerate(copies)]
    for copy in copies:
        copy.start()
    for copy in copies:
        copy.wait()


def unpack_kernel(moved_ref, pots_ref, noise_sq_ref, out_ref, row_ref, col_ref, row, col, sems):
    devices, units = moved_ref.shape[0], out_ref.shape[0]
    own = out_ref.shape[1]
    copies = []
    for q in range(UNITS):
        start = q * devices
        count = min(devices, units - start)
        copies.append((moved_ref.at[pl.ds(0, count), q], out_ref.at[pl.ds(start, count)]))
    copies.extend([(row, row_ref), (col, col_ref)])
    copies = [pltpu.make_async_copy(src, dst, sems.at[n]) for n, (src, dst) in enumerate(copies)]
    for copy in copies[:UNITS]:
        copy.start()

    first = (lax.axis_index("dp") * lax.axis_size("dim") + lax.axis_index("dim")) * own
    lane = lax.broadcasted_iota(jnp.int32, (1, BATCH), 1)
    for n in range(own):
        mine = lane == first + n
        row_pot = jnp.sum(jnp.where(mine, pots_ref[0:1, :], 0.0))
        row[n] = row_pot + jnp.max(noise_sq_ref[n : n + 1, :]) / LATENT
        col[n] = jnp.sum(jnp.where(mine, pots_ref[1:2, :], 0.0))
    for copy in copies[UNITS:]:
        copy.start()
    for copy in copies:
        copy.wait()


def pieces_of(value, pieces_ref):
    for piece in range(BATCH * 2 // 4):
        row, half = 4 * (piece // 2), LANES * (piece % 2)
        pieces_ref[piece] = value[row : row + 4, half : half + LANES]


def whole_of(pieces_ref):
    rows = []
    for row in range(BATCH // 4):
        rows.append(jnp.concatenate([pieces_ref[2 * row], pieces_ref[2 * row + 1]], axis=1))
    return jnp.concatenate(rows, axis=0)


def gram_kernel(both_ref, out_ref, data_ref):
    ent = data_ref.shape[1]
    noise = both_ref[:, :, :ent].reshape(data_ref.shape)
    data = both_ref[:, :, ent:].reshape(data_ref.shape)
    data_ref[...] = data
    gram = lax.dot_general(
        data, noise, (((1,), (1,)), ((), ())), preferred_element_type=jnp.float32
    )
    wide = data.astype(jnp.float32)
    data_sq = jnp.sum(wide * wide, axis=1, keepdims=True)
    pieces_of(data_sq - 2.0 * gram, out_ref)


def sum_kernel(parts_ref, out_ref):
    total = jnp.sum(parts_ref[...], axis=0)
    out_ref[...] = jnp.broadcast_to(total[None], out_ref.shape)


def sweep_kernel(
    cost_ref, data_ref, noise_ref, out_ref, pots_ref, noise_sq_ref,
    bias, kern, row_pot, col_pot, row_sum,
):
    bias[...] = whole_of(cost_ref) * (-1.0 / (LATENT * BIT))
    col_pot[...] = jnp.zeros_like(col_pot)

    def log_sweep():
        scaled = bias[...] + col_pot[...]
        top = jnp.max(scaled, axis=0, keepdims=True)
        row = -(top + jnp.log2(jnp.sum(jnp.exp2(scaled - top), axis=0, keepdims=True)))
        scaled = bias[...] + row
        top = jnp.max(scaled, axis=1, keepdims=True)
        scaled = jnp.exp2(scaled - top)
        total = jnp.sum(scaled, axis=1, keepdims=True)
        row_pot[...] = row
        col_pot[...] = -(top + jnp.log2(total))
        kern[...] = scaled * (1.0 / total)

    log_sweep()

    tile = (8, LANES)
    blocks = [pl.ds(start, 8) for start in range(0, BATCH, 8)]
    halves = [pl.ds(start, LANES) for start in range(0, BATCH, LANES)]

    def over_columns(low, high, rows, use):
        sums = [[jnp.zeros(tile, jnp.float32) for _ in halves] for _ in range(2)]
        for n, block in enumerate(blocks):
            parts = [kern[block, half] for half in halves]
            if rows is not None:
                total = sum(part * row for part, row in zip(parts, rows))
                total = jnp.broadcast_to(jnp.sum(total, axis=1, keepdims=True), tile)
                low, high = jnp.minimum(low, total), jnp.maximum(high, total)
                factor = 1.0 / total
                parts = [part * factor for part in parts]
                if use is not None:
                    use(block, factor, parts)
            for h, part in enumerate(parts):
                sums[n % 2][h] += part
        totals = []
        for first, second in zip(*sums):
            total = jnp.broadcast_to(jnp.sum(first + second, axis=0, keepdims=True), tile)
            low = jnp.minimum(low, total)
            totals.append(total)
        return low, high, totals

    units = noise_ref.shape[1] // UNIT
    share = units // (SWEEPS - 2)

    def squares(first, count, total):
        for n in range(count):
            start = pl.multiple_of((first + n) * UNIT, LANES)
            unit = noise_ref[:, pl.ds(start, UNIT)].astype(jnp.float32)
            total = total + unit * unit
        return total

    def sweep(step, carry):
        low, high, rows, noise_sq = carry
        low, high, totals = over_columns(low, high, rows, None)
        for total in totals:
            high = jnp.maximum(high, total)
        if rows is not None:
            noise_sq = squares((step - 2) * share, share, noise_sq)
        return (low, high, tuple(1.0 / total for total in totals), noise_sq)

    def finish(block, factor, parts):
        col_pot[block, :] += jnp.log2(factor[:, :1])
        for half, part in zip(halves, parts):
            kern[block, half] = part

    ones = jnp.ones(tile, jnp.float32)
    carry = sweep(0, (ones, ones, None, jnp.zeros((noise_ref.shape[0], UNIT), jnp.float32)))
    low, high, rows, noise_sq = lax.fori_loop(2, SWEEPS, sweep, carry)
    done = (SWEEPS - 2) * share
    noise_sq = jnp.sum(squares(done, units - done, noise_sq), axis=1, keepdims=True)
    noise_sq_ref[...] = jnp.broadcast_to(noise_sq, noise_sq_ref.shape)
    low, high, totals = over_columns(low, high, rows, finish)
    row_pot[...] += jnp.log2(jnp.concatenate([row[:1] for row in rows], axis=1))
    row_sum[...] = jnp.concatenate([total[:1] for total in totals], axis=1)
    near = jnp.min(jnp.where((low >= 1.0 / DRIFT) & (high <= DRIFT), 1.0, 0.0)) > 0.5

    @pl.when(jnp.logical_not(near))
    def _():
        col_pot[...] = jnp.zeros_like(col_pot)

        def again(step, carry):
            log_sweep()
            return carry

        lax.fori_loop(0, SWEEPS, again, 0)
        scaled = bias[...] + col_pot[...]
        scaled = jnp.exp2(scaled - jnp.max(scaled, axis=0, keepdims=True))
        kern[...] = scaled
        row_sum[...] = jnp.sum(scaled, axis=0, keepdims=True)

    weights = (kern[...] * (1.0 / row_sum[...])).astype(jnp.bfloat16)
    moved = lax.dot_general(
        weights, data_ref[...], (((0,), (0,)), ((), ())), preferred_element_type=jnp.float32
    )
    out_ref[...] = moved.astype(jnp.bfloat16).reshape(out_ref.shape)
    pots_ref[0:1, :] = row_pot[...] * BIT
    pots_ref[1:2, :] = jnp.transpose(col_pot[...] * BIT)


def on_device(noise, data):
    devices = lax.axis_size(AXES)
    own = noise.shape[0]
    ent = UNITS * UNIT
    units = LATENT // UNIT
    params = pltpu.CompilerParams(vmem_limit_bytes=VMEM)
    anywhere = pl.BlockSpec(memory_space=pl.ANY)

    def units_of(rows):
        return rows.reshape(own, units, UNIT).transpose(1, 0, 2)

    both = pl.pallas_call(
        pack_kernel,
        out_shape=jax.ShapeDtypeStruct((devices, 2 * UNITS, own, UNIT), noise.dtype),
        in_specs=[pl.BlockSpec(memory_space=pltpu.HBM)] * 2,
        out_specs=anywhere,
        scratch_shapes=[
            pltpu.VMEM((UNITS * devices - units, own, UNIT), noise.dtype),
            pltpu.SemaphoreType.DMA((4 * UNITS,)),
        ],
        compiler_params=params,
    )(*[pltpu.with_memory_space_constraint(units_of(rows), pltpu.HBM) for rows in (noise, data)])
    both = both.transpose(0, 2, 1, 3).reshape(devices, own, 2 * ent)
    both = lax.all_to_all(both, AXES, split_axis=0, concat_axis=0)

    pieces = jax.ShapeDtypeStruct((devices, 4, LANES), jnp.float32)
    parts, data_ent = pl.pallas_call(
        gram_kernel,
        out_shape=(pieces, jax.ShapeDtypeStruct((BATCH, ent), data.dtype)),
        compiler_params=params,
    )(both)
    parts = lax.all_to_all(parts, AXES, split_axis=0, concat_axis=0)
    total = pl.pallas_call(sum_kernel, out_shape=pieces, compiler_params=params)(parts)
    total = lax.all_to_all(total, AXES, split_axis=0, concat_axis=0)

    moved, pots, noise_sq = pl.pallas_call(
        sweep_kernel,
        out_shape=(
            jax.ShapeDtypeStruct((devices, own, ent), jnp.bfloat16),
            jax.ShapeDtypeStruct((2, BATCH), jnp.float32),
            jax.ShapeDtypeStruct((own, LANES), jnp.float32),
        ),
        scratch_shapes=[
            pltpu.VMEM((BATCH, BATCH), jnp.float32),
            pltpu.VMEM((BATCH, BATCH), jnp.float32),
            pltpu.VMEM((1, BATCH), jnp.float32),
            pltpu.VMEM((BATCH, 1), jnp.float32),
            pltpu.VMEM((1, BATCH), jnp.float32),
        ],
        compiler_params=params,
    )(total, data_ent, noise)
    moved = lax.all_to_all(moved, AXES, split_axis=0, concat_axis=0)
    moved = moved.reshape(devices, own, UNITS, UNIT).transpose(0, 2, 1, 3)
    whole = pl.BlockSpec(memory_space=pltpu.VMEM)
    targets, row, col = pl.pallas_call(
        unpack_kernel,
        out_shape=(
            jax.ShapeDtypeStruct((units, own, UNIT), moved.dtype),
            jax.ShapeDtypeStruct((own,), jnp.float32),
            jax.ShapeDtypeStruct((own,), jnp.float32),
        ),
        in_specs=[anywhere, whole, whole],
        out_specs=(anywhere, anywhere, anywhere),
        scratch_shapes=[
            pltpu.SMEM((own,), jnp.float32),
            pltpu.SMEM((own,), jnp.float32),
            pltpu.SemaphoreType.DMA((UNITS + 2,)),
        ],
        compiler_params=params,
    )(moved, pots, noise_sq)
    return (targets.transpose(1, 0, 2).reshape(own, LATENT), row, col)


def solution(mesh):
    return jax.shard_map(
        on_device,
        mesh=mesh,
        in_specs=(P(AXES, None), P(AXES, None)),
        out_specs=(P(AXES, None), P(AXES), P(AXES)),
        check_vma=False,
    )
```

```python
import math

import jax
import jax.numpy as jnp
from jax import lax
from jax.experimental import pallas as pl
from jax.experimental.pallas import tpu as pltpu
from jax.sharding import PartitionSpec as P

SWEEPS = 20
LATENT = 324480
BATCH = 256
AXES = ("dp", "dim")
LANES = 128
TEMPER = 0.25 / math.sqrt(LATENT)
BIT = TEMPER * math.log(2.0)
DRIFT = 2.0**40
VMEM = 24 * 1024 * 1024
UNITS = 4
UNIT = 640


def pack_kernel(noise_ref, data_ref, out_ref, zeros, sems):
    devices, units = out_ref.shape[0], noise_ref.shape[0]
    zeros[...] = jnp.zeros_like(zeros)
    copies = []
    for kind, ref in enumerate((noise_ref, data_ref)):
        for q in range(UNITS):
            slot = kind * UNITS + q
            start = q * devices
            count = min(devices, units - start)
            copies.append((ref.at[pl.ds(start, count)], out_ref.at[pl.ds(0, count), slot]))
            if count < devices:
                copies.append((zeros, out_ref.at[pl.ds(count, devices - count), slot]))
    copies = [pltpu.make_async_copy(src, dst, sems.at[n]) for n, (src, dst) in enumerate(copies)]
    for copy in copies:
        copy.start()
    for copy in copies:
        copy.wait()


def unpack_kernel(moved_ref, pots_ref, noise_sq_ref, out_ref, row_ref, col_ref, row, col, sems):
    devices, units = moved_ref.shape[0], out_ref.shape[0]
    own = out_ref.shape[1]
    copies = []
    for q in range(UNITS):
        start = q * devices
        count = min(devices, units - start)
        copies.append((moved_ref.at[pl.ds(0, count), q], out_ref.at[pl.ds(start, count)]))
    copies.extend([(row, row_ref), (col, col_ref)])
    copies = [pltpu.make_async_copy(src, dst, sems.at[n]) for n, (src, dst) in enumerate(copies)]
    for copy in copies[:UNITS]:
        copy.start()

    first = (lax.axis_index("dp") * lax.axis_size("dim") + lax.axis_index("dim")) * own
    lane = lax.broadcasted_iota(jnp.int32, (1, BATCH), 1)
    for n in range(own):
        mine = lane == first + n
        row_pot = jnp.sum(jnp.where(mine, pots_ref[0:1, :], 0.0))
        row[n] = row_pot + jnp.max(noise_sq_ref[n : n + 1, :]) / LATENT
        col[n] = jnp.sum(jnp.where(mine, pots_ref[1:2, :], 0.0))
    for copy in copies[UNITS:]:
        copy.start()
    for copy in copies:
        copy.wait()


def pieces_of(value, pieces_ref):
    for piece in range(BATCH * 2 // 4):
        row, half = 4 * (piece // 2), LANES * (piece % 2)
        pieces_ref[piece] = value[row : row + 4, half : half + LANES]


def whole_of(pieces_ref):
    rows = []
    for row in range(BATCH // 4):
        rows.append(jnp.concatenate([pieces_ref[2 * row], pieces_ref[2 * row + 1]], axis=1))
    return jnp.concatenate(rows, axis=0)


def gram_kernel(both_ref, out_ref, data_ref):
    ent = data_ref.shape[1]
    noise = both_ref[:, :, :ent].reshape(data_ref.shape)
    data = both_ref[:, :, ent:].reshape(data_ref.shape)
    data_ref[...] = data
    gram = lax.dot_general(
        data, noise, (((1,), (1,)), ((), ())), preferred_element_type=jnp.float32
    )
    data_sq = jnp.zeros((BATCH, LANES), jnp.float32)
    for start in range(0, ent, LANES):
        wide = data_ref[:, start : start + LANES].astype(jnp.float32)
        data_sq = data_sq + wide * wide
    data_sq = jnp.sum(data_sq, axis=1, keepdims=True)
    pieces_of(data_sq - 2.0 * gram, out_ref)


def sum_kernel(parts_ref, out_ref):
    total = jnp.sum(parts_ref[...], axis=0)
    out_ref[...] = jnp.broadcast_to(total[None], out_ref.shape)


def sweep_kernel(
    cost_ref, data_ref, noise_ref, out_ref, pots_ref, noise_sq_ref,
    bias, kern, row_pot, col_pot, row_sum,
):
    bias[...] = whole_of(cost_ref) * (-1.0 / (LATENT * BIT))
    col_pot[...] = jnp.zeros_like(col_pot)

    def log_sweep():
        scaled = bias[...] + col_pot[...]
        top = jnp.max(scaled, axis=0, keepdims=True)
        row = -(top + jnp.log2(jnp.sum(jnp.exp2(scaled - top), axis=0, keepdims=True)))
        scaled = bias[...] + row
        top = jnp.max(scaled, axis=1, keepdims=True)
        scaled = jnp.exp2(scaled - top)
        total = jnp.sum(scaled, axis=1, keepdims=True)
        row_pot[...] = row
        col_pot[...] = -(top + jnp.log2(total))
        kern[...] = scaled * (1.0 / total)

    log_sweep()

    tile = (8, LANES)
    blocks = [pl.ds(start, 8) for start in range(0, BATCH, 8)]
    halves = [pl.ds(start, LANES) for start in range(0, BATCH, LANES)]

    def over_columns(low, high, rows, use):
        sums = [[jnp.zeros(tile, jnp.float32) for _ in halves] for _ in range(2)]
        for n, block in enumerate(blocks):
            parts = [kern[block, half] for half in halves]
            if rows is not None:
                total = sum(part * row for part, row in zip(parts, rows))
                total = jnp.broadcast_to(jnp.sum(total, axis=1, keepdims=True), tile)
                low, high = jnp.minimum(low, total), jnp.maximum(high, total)
                factor = 1.0 / total
                parts = [part * factor for part in parts]
                if use is not None:
                    use(block, factor, parts)
            for h, part in enumerate(parts):
                sums[n % 2][h] += part
        totals = []
        for first, second in zip(*sums):
            total = jnp.broadcast_to(jnp.sum(first + second, axis=0, keepdims=True), tile)
            low = jnp.minimum(low, total)
            totals.append(total)
        return low, high, totals

    units = noise_ref.shape[1] // UNIT
    share = units // (SWEEPS - 2)

    def squares(first, count, total):
        for n in range(count):
            start = pl.multiple_of((first + n) * UNIT, LANES)
            unit = noise_ref[:, pl.ds(start, UNIT)].astype(jnp.float32)
            total = total + unit * unit
        return total

    def sweep(step, carry):
        low, high, rows, noise_sq = carry
        low, high, totals = over_columns(low, high, rows, None)
        for total in totals:
            high = jnp.maximum(high, total)
        if rows is not None:
            noise_sq = squares((step - 2) * share, share, noise_sq)
        return (low, high, tuple(1.0 / total for total in totals), noise_sq)

    def finish(block, factor, parts):
        col_pot[block, :] += jnp.log2(factor[:, :1])
        for half, part in zip(halves, parts):
            kern[block, half] = part

    ones = jnp.ones(tile, jnp.float32)
    carry = sweep(0, (ones, ones, None, jnp.zeros((noise_ref.shape[0], UNIT), jnp.float32)))
    low, high, rows, noise_sq = lax.fori_loop(2, SWEEPS, sweep, carry)
    done = (SWEEPS - 2) * share
    noise_sq = jnp.sum(squares(done, units - done, noise_sq), axis=1, keepdims=True)
    noise_sq_ref[...] = jnp.broadcast_to(noise_sq, noise_sq_ref.shape)
    low, high, totals = over_columns(low, high, rows, finish)
    row_pot[...] += jnp.log2(jnp.concatenate([row[:1] for row in rows], axis=1))
    row_sum[...] = jnp.concatenate([total[:1] for total in totals], axis=1)
    near = jnp.min(jnp.where((low >= 1.0 / DRIFT) & (high <= DRIFT), 1.0, 0.0)) > 0.5

    @pl.when(jnp.logical_not(near))
    def _():
        col_pot[...] = jnp.zeros_like(col_pot)

        def again(step, carry):
            log_sweep()
            return carry

        lax.fori_loop(0, SWEEPS, again, 0)
        scaled = bias[...] + col_pot[...]
        scaled = jnp.exp2(scaled - jnp.max(scaled, axis=0, keepdims=True))
        kern[...] = scaled
        row_sum[...] = jnp.sum(scaled, axis=0, keepdims=True)

    weights = (kern[...] * (1.0 / row_sum[...])).astype(jnp.bfloat16)
    moved = lax.dot_general(
        weights, data_ref[...], (((0,), (0,)), ((), ())), preferred_element_type=jnp.float32
    )
    out_ref[...] = moved.astype(jnp.bfloat16).reshape(out_ref.shape)
    pots_ref[0:1, :] = row_pot[...] * BIT
    pots_ref[1:2, :] = jnp.transpose(col_pot[...] * BIT)


def on_device(noise, data):
    devices = lax.axis_size(AXES)
    own = noise.shape[0]
    ent = UNITS * UNIT
    units = LATENT // UNIT
    params = pltpu.CompilerParams(vmem_limit_bytes=VMEM)
    anywhere = pl.BlockSpec(memory_space=pl.ANY)

    def units_of(rows):
        return rows.reshape(own, units, UNIT).transpose(1, 0, 2)

    both = pl.pallas_call(
        pack_kernel,
        out_shape=jax.ShapeDtypeStruct((devices, 2 * UNITS, own, UNIT), noise.dtype),
        in_specs=[pl.BlockSpec(memory_space=pltpu.HBM)] * 2,
        out_specs=anywhere,
        scratch_shapes=[
            pltpu.VMEM((UNITS * devices - units, own, UNIT), noise.dtype),
            pltpu.SemaphoreType.DMA((4 * UNITS,)),
        ],
        compiler_params=params,
    )(*[pltpu.with_memory_space_constraint(units_of(rows), pltpu.HBM) for rows in (noise, data)])
    both = both.transpose(0, 2, 1, 3).reshape(devices, own, 2 * ent)
    both = lax.all_to_all(both, AXES, split_axis=0, concat_axis=0)

    pieces = jax.ShapeDtypeStruct((devices, 4, LANES), jnp.float32)
    parts, data_ent = pl.pallas_call(
        gram_kernel,
        out_shape=(pieces, jax.ShapeDtypeStruct((BATCH, ent), data.dtype)),
        compiler_params=params,
    )(both)
    parts = lax.all_to_all(parts, AXES, split_axis=0, concat_axis=0)
    total = pl.pallas_call(sum_kernel, out_shape=pieces, compiler_params=params)(parts)
    total = lax.all_to_all(total, AXES, split_axis=0, concat_axis=0)

    moved, pots, noise_sq = pl.pallas_call(
        sweep_kernel,
        out_shape=(
            jax.ShapeDtypeStruct((devices, own, ent), jnp.bfloat16),
            jax.ShapeDtypeStruct((2, BATCH), jnp.float32),
            jax.ShapeDtypeStruct((own, LANES), jnp.float32),
        ),
        scratch_shapes=[
            pltpu.VMEM((BATCH, BATCH), jnp.float32),
            pltpu.VMEM((BATCH, BATCH), jnp.float32),
            pltpu.VMEM((1, BATCH), jnp.float32),
            pltpu.VMEM((BATCH, 1), jnp.float32),
            pltpu.VMEM((1, BATCH), jnp.float32),
        ],
        compiler_params=params,
    )(total, data_ent, noise)
    moved = lax.all_to_all(moved, AXES, split_axis=0, concat_axis=0)
    moved = moved.reshape(devices, own, UNITS, UNIT).transpose(0, 2, 1, 3)
    whole = pl.BlockSpec(memory_space=pltpu.VMEM)
    targets, row, col = pl.pallas_call(
        unpack_kernel,
        out_shape=(
            jax.ShapeDtypeStruct((units, own, UNIT), moved.dtype),
            jax.ShapeDtypeStruct((own,), jnp.float32),
            jax.ShapeDtypeStruct((own,), jnp.float32),
        ),
        in_specs=[anywhere, whole, whole],
        out_specs=(anywhere, anywhere, anywhere),
        scratch_shapes=[
            pltpu.SMEM((own,), jnp.float32),
            pltpu.SMEM((own,), jnp.float32),
            pltpu.SemaphoreType.DMA((UNITS + 2,)),
        ],
        compiler_params=params,
    )(moved, pots, noise_sq)
    return (targets.transpose(1, 0, 2).reshape(own, LATENT), row, col)


def solution(mesh):
    return jax.shard_map(
        on_device,
        mesh=mesh,
        in_specs=(P(AXES, None), P(AXES, None)),
        out_specs=(P(AXES, None), P(AXES), P(AXES)),
        check_vma=False,
    )
```

```python
import math

import jax
import jax.numpy as jnp
from jax import lax
from jax.experimental import pallas as pl
from jax.experimental.pallas import tpu as pltpu
from jax.sharding import PartitionSpec as P

SWEEPS = 20
LATENT = 324480
BATCH = 256
AXES = ("dp", "dim")
LANES = 128
TEMPER = 0.25 / math.sqrt(LATENT)
BIT = TEMPER * math.log(2.0)
DRIFT = 2.0**40
VMEM = 24 * 1024 * 1024
UNITS = 4
UNIT = 640


def pack_kernel(noise_ref, data_ref, out_ref, zeros, sems):
    devices, units = out_ref.shape[0], noise_ref.shape[0]
    zeros[...] = jnp.zeros_like(zeros)
    copies = []
    for kind, ref in enumerate((noise_ref, data_ref)):
        for q in range(UNITS):
            slot = kind * UNITS + q
            start = q * devices
            count = min(devices, units - start)
            copies.append((ref.at[pl.ds(start, count)], out_ref.at[pl.ds(0, count), slot]))
            if count < devices:
                copies.append((zeros, out_ref.at[pl.ds(count, devices - count), slot]))
    copies = [pltpu.make_async_copy(src, dst, sems.at[n]) for n, (src, dst) in enumerate(copies)]
    for copy in copies:
        copy.start()
    for copy in copies:
        copy.wait()


def unpack_kernel(moved_ref, pots_ref, noise_sq_ref, out_ref, row_ref, col_ref, row, col, sems):
    devices, units = moved_ref.shape[0], out_ref.shape[0]
    own = out_ref.shape[1]
    copies = []
    for q in range(UNITS):
        start = q * devices
        count = min(devices, units - start)
        copies.append((moved_ref.at[pl.ds(0, count), q], out_ref.at[pl.ds(start, count)]))
    copies.extend([(row, row_ref), (col, col_ref)])
    copies = [pltpu.make_async_copy(src, dst, sems.at[n]) for n, (src, dst) in enumerate(copies)]
    for copy in copies[:UNITS]:
        copy.start()

    first = (lax.axis_index("dp") * lax.axis_size("dim") + lax.axis_index("dim")) * own
    lane = lax.broadcasted_iota(jnp.int32, (1, BATCH), 1)
    for n in range(own):
        mine = lane == first + n
        row_pot = jnp.sum(jnp.where(mine, pots_ref[0:1, :], 0.0))
        row[n] = row_pot + jnp.max(noise_sq_ref[n : n + 1, :]) / LATENT
        col[n] = jnp.sum(jnp.where(mine, pots_ref[1:2, :], 0.0))
    for copy in copies[UNITS:]:
        copy.start()
    for copy in copies:
        copy.wait()


def tiles():
    for tile in range(BATCH * BATCH // (8 * LANES)):
        row, half = 8 * (tile // 2), LANES * (tile % 2)
        yield tile, slice(row, row + 8), slice(half, half + LANES)


def gram_kernel(both_ref, out_ref, data_ref):
    ent = data_ref.shape[1]
    noise = both_ref[:, :, :ent].reshape(data_ref.shape)
    data = both_ref[:, :, ent:].reshape(data_ref.shape)
    data_ref[...] = data
    gram = lax.dot_general(
        data, noise, (((1,), (1,)), ((), ())), preferred_element_type=jnp.float32
    )
    data_sq = jnp.zeros((BATCH, LANES), jnp.float32)
    for start in range(0, ent, LANES):
        wide = data_ref[:, start : start + LANES].astype(jnp.float32)
        data_sq = data_sq + wide * wide
    data_sq = jnp.sum(data_sq, axis=1, keepdims=True)
    parts = data_sq - 2.0 * gram
    for tile, rows, half in tiles():
        out_ref[tile] = parts[rows, half]


def sum_kernel(parts_ref, out_ref):
    total = jnp.sum(parts_ref[...], axis=0)
    total = total[:4] + total[4:]
    total = jnp.concatenate([total, total], axis=0)
    out_ref[...] = jnp.broadcast_to(total[None], out_ref.shape)


def sweep_kernel(
    cost_ref, data_ref, noise_ref, out_ref, pots_ref, noise_sq_ref,
    bias, kern, row_pot, col_pot, row_sum,
):
    for tile, rows, half in tiles():
        bias[rows, half] = cost_ref[tile] * (-1.0 / (LATENT * BIT))
    col_pot[...] = jnp.zeros_like(col_pot)

    def log_sweep():
        scaled = bias[...] + col_pot[...]
        top = jnp.max(scaled, axis=0, keepdims=True)
        row = -(top + jnp.log2(jnp.sum(jnp.exp2(scaled - top), axis=0, keepdims=True)))
        scaled = bias[...] + row
        top = jnp.max(scaled, axis=1, keepdims=True)
        scaled = jnp.exp2(scaled - top)
        total = jnp.sum(scaled, axis=1, keepdims=True)
        row_pot[...] = row
        col_pot[...] = -(top + jnp.log2(total))
        kern[...] = scaled * (1.0 / total)

    log_sweep()

    tile = (8, LANES)
    blocks = [pl.ds(start, 8) for start in range(0, BATCH, 8)]
    halves = [pl.ds(start, LANES) for start in range(0, BATCH, LANES)]

    def over_columns(low, high, rows, use):
        sums = [[jnp.zeros(tile, jnp.float32) for _ in halves] for _ in range(2)]
        for n, block in enumerate(blocks):
            parts = [kern[block, half] for half in halves]
            if rows is not None:
                total = sum(part * row for part, row in zip(parts, rows))
                total = jnp.broadcast_to(jnp.sum(total, axis=1, keepdims=True), tile)
                low, high = jnp.minimum(low, total), jnp.maximum(high, total)
                factor = 1.0 / total
                parts = [part * factor for part in parts]
                if use is not None:
                    use(block, factor, parts)
            for h, part in enumerate(parts):
                sums[n % 2][h] += part
        totals = []
        for first, second in zip(*sums):
            total = jnp.broadcast_to(jnp.sum(first + second, axis=0, keepdims=True), tile)
            low = jnp.minimum(low, total)
            totals.append(total)
        return low, high, totals

    units = noise_ref.shape[1] // UNIT
    share = units // (SWEEPS - 2)

    def squares(first, count, total):
        for n in range(count):
            start = pl.multiple_of((first + n) * UNIT, LANES)
            unit = noise_ref[:, pl.ds(start, UNIT)].astype(jnp.float32)
            total = total + unit * unit
        return total

    def sweep(step, carry):
        low, high, rows, noise_sq = carry
        low, high, totals = over_columns(low, high, rows, None)
        for total in totals:
            high = jnp.maximum(high, total)
        if rows is not None:
            noise_sq = squares((step - 2) * share, share, noise_sq)
        return (low, high, tuple(1.0 / total for total in totals), noise_sq)

    def finish(block, factor, parts):
        col_pot[block, :] += jnp.log2(factor[:, :1])
        for half, part in zip(halves, parts):
            kern[block, half] = part

    ones = jnp.ones(tile, jnp.float32)
    carry = sweep(0, (ones, ones, None, jnp.zeros((noise_ref.shape[0], UNIT), jnp.float32)))
    low, high, rows, noise_sq = lax.fori_loop(2, SWEEPS, sweep, carry)
    done = (SWEEPS - 2) * share
    noise_sq = jnp.sum(squares(done, units - done, noise_sq), axis=1, keepdims=True)
    noise_sq_ref[...] = jnp.broadcast_to(noise_sq, noise_sq_ref.shape)
    low, high, totals = over_columns(low, high, rows, finish)
    row_pot[...] += jnp.log2(jnp.concatenate([row[:1] for row in rows], axis=1))
    row_sum[...] = jnp.concatenate([total[:1] for total in totals], axis=1)
    near = jnp.min(jnp.where((low >= 1.0 / DRIFT) & (high <= DRIFT), 1.0, 0.0)) > 0.5

    @pl.when(jnp.logical_not(near))
    def _():
        col_pot[...] = jnp.zeros_like(col_pot)

        def again(step, carry):
            log_sweep()
            return carry

        lax.fori_loop(0, SWEEPS, again, 0)
        scaled = bias[...] + col_pot[...]
        scaled = jnp.exp2(scaled - jnp.max(scaled, axis=0, keepdims=True))
        kern[...] = scaled
        row_sum[...] = jnp.sum(scaled, axis=0, keepdims=True)

    weights = (kern[...] * (1.0 / row_sum[...])).astype(jnp.bfloat16)
    moved = lax.dot_general(
        weights, data_ref[...], (((0,), (0,)), ((), ())), preferred_element_type=jnp.float32
    )
    out_ref[...] = moved.astype(jnp.bfloat16).reshape(out_ref.shape)
    pots_ref[0:1, :] = row_pot[...] * BIT
    pots_ref[1:2, :] = jnp.transpose(col_pot[...] * BIT)


def on_device(noise, data):
    devices = lax.axis_size(AXES)
    own = noise.shape[0]
    ent = UNITS * UNIT
    units = LATENT // UNIT
    params = pltpu.CompilerParams(vmem_limit_bytes=VMEM)
    anywhere = pl.BlockSpec(memory_space=pl.ANY)

    def units_of(rows):
        return rows.reshape(own, units, UNIT).transpose(1, 0, 2)

    both = pl.pallas_call(
        pack_kernel,
        out_shape=jax.ShapeDtypeStruct((devices, 2 * UNITS, own, UNIT), noise.dtype),
        in_specs=[pl.BlockSpec(memory_space=pltpu.HBM)] * 2,
        out_specs=anywhere,
        scratch_shapes=[
            pltpu.VMEM((UNITS * devices - units, own, UNIT), noise.dtype),
            pltpu.SemaphoreType.DMA((4 * UNITS,)),
        ],
        compiler_params=params,
    )(*[pltpu.with_memory_space_constraint(units_of(rows), pltpu.HBM) for rows in (noise, data)])
    both = both.transpose(0, 2, 1, 3).reshape(devices, own, 2 * ent)
    both = lax.all_to_all(both, AXES, split_axis=0, concat_axis=0)

    whole = jax.ShapeDtypeStruct((devices // 2, 8, LANES), jnp.float32)

    def exchange(parts):
        parts = parts.reshape(devices, 4, LANES)
        return lax.all_to_all(parts, AXES, split_axis=0, concat_axis=0).reshape(whole.shape)

    parts, data_ent = pl.pallas_call(
        gram_kernel,
        out_shape=(whole, jax.ShapeDtypeStruct((BATCH, ent), data.dtype)),
        compiler_params=params,
    )(both)
    total = pl.pallas_call(sum_kernel, out_shape=whole, compiler_params=params)(exchange(parts))
    total = exchange(total)

    moved, pots, noise_sq = pl.pallas_call(
        sweep_kernel,
        out_shape=(
            jax.ShapeDtypeStruct((devices, own, ent), jnp.bfloat16),
            jax.ShapeDtypeStruct((2, BATCH), jnp.float32),
            jax.ShapeDtypeStruct((own, LANES), jnp.float32),
        ),
        scratch_shapes=[
            pltpu.VMEM((BATCH, BATCH), jnp.float32),
            pltpu.VMEM((BATCH, BATCH), jnp.float32),
            pltpu.VMEM((1, BATCH), jnp.float32),
            pltpu.VMEM((BATCH, 1), jnp.float32),
            pltpu.VMEM((1, BATCH), jnp.float32),
        ],
        compiler_params=params,
    )(total, data_ent, noise)
    moved = lax.all_to_all(moved, AXES, split_axis=0, concat_axis=0)
    moved = moved.reshape(devices, own, UNITS, UNIT).transpose(0, 2, 1, 3)
    in_vmem = pl.BlockSpec(memory_space=pltpu.VMEM)
    targets, row, col = pl.pallas_call(
        unpack_kernel,
        out_shape=(
            jax.ShapeDtypeStruct((units, own, UNIT), moved.dtype),
            jax.ShapeDtypeStruct((own,), jnp.float32),
            jax.ShapeDtypeStruct((own,), jnp.float32),
        ),
        in_specs=[anywhere, in_vmem, in_vmem],
        out_specs=(anywhere, anywhere, anywhere),
        scratch_shapes=[
            pltpu.SMEM((own,), jnp.float32),
            pltpu.SMEM((own,), jnp.float32),
            pltpu.SemaphoreType.DMA((UNITS + 2,)),
        ],
        compiler_params=params,
    )(moved, pots, noise_sq)
    return (targets.transpose(1, 0, 2).reshape(own, LATENT), row, col)


def solution(mesh):
    return jax.shard_map(
        on_device,
        mesh=mesh,
        in_specs=(P(AXES, None), P(AXES, None)),
        out_specs=(P(AXES, None), P(AXES), P(AXES)),
        check_vma=False,
    )
```

```python
import math

import jax
import jax.numpy as jnp
from jax import lax
from jax.experimental import pallas as pl
from jax.experimental.pallas import tpu as pltpu
from jax.sharding import PartitionSpec as P

SWEEPS = 20
LATENT = 324480
BATCH = 256
AXES = ("dp", "dim")
LANES = 128
TEMPER = 0.25 / math.sqrt(LATENT)
BIT = TEMPER * math.log(2.0)
DRIFT = 2.0**40
VMEM = 24 * 1024 * 1024
UNITS = 4
UNIT = 640


def pack_kernel(noise_ref, data_ref, out_ref, zeros, sems):
    devices, units = out_ref.shape[0], noise_ref.shape[0]
    zeros[...] = jnp.zeros_like(zeros)
    copies = []
    for kind, ref in enumerate((noise_ref, data_ref)):
        for q in range(UNITS):
            slot = kind * UNITS + q
            start = q * devices
            count = min(devices, units - start)
            copies.append((ref.at[pl.ds(start, count)], out_ref.at[pl.ds(0, count), slot]))
            if count < devices:
                copies.append((zeros, out_ref.at[pl.ds(count, devices - count), slot]))
    copies = [pltpu.make_async_copy(src, dst, sems.at[n]) for n, (src, dst) in enumerate(copies)]
    for copy in copies:
        copy.start()
    for copy in copies:
        copy.wait()


def unpack_kernel(moved_ref, pots_ref, noise_sq_ref, out_ref, row_ref, col_ref, row, col, sems):
    devices, units = moved_ref.shape[0], out_ref.shape[0]
    own = out_ref.shape[1]
    copies = []
    for q in range(UNITS):
        start = q * devices
        count = min(devices, units - start)
        copies.append((moved_ref.at[pl.ds(0, count), q], out_ref.at[pl.ds(start, count)]))
    copies.extend([(row, row_ref), (col, col_ref)])
    copies = [pltpu.make_async_copy(src, dst, sems.at[n]) for n, (src, dst) in enumerate(copies)]
    for copy in copies[:UNITS]:
        copy.start()

    first = (lax.axis_index("dp") * lax.axis_size("dim") + lax.axis_index("dim")) * own
    lane = lax.broadcasted_iota(jnp.int32, (1, BATCH), 1)
    for n in range(own):
        mine = lane == first + n
        row_pot = jnp.sum(jnp.where(mine, pots_ref[0:1, :], 0.0))
        row[n] = row_pot + jnp.max(noise_sq_ref[n : n + 1, :]) / LATENT
        col[n] = jnp.sum(jnp.where(mine, pots_ref[1:2, :], 0.0))
    for copy in copies[UNITS:]:
        copy.start()
    for copy in copies:
        copy.wait()


def tiles(rows):
    for tile in range(rows * BATCH // (8 * LANES)):
        row, half = 8 * (tile // 2), LANES * (tile % 2)
        yield tile, slice(row, row + 8), slice(half, half + LANES)


def core():
    return lax.rem(lax.axis_index("dim"), 2)


def half_of(both_ref, noise, part, data_ref, out_ref):
    rows, ent = data_ref.shape
    pairs = rows // both_ref.shape[1]
    data = both_ref[pl.ds(pl.multiple_of(part * pairs, pairs), pairs), :, ent:].reshape(rows, ent)
    data_ref[...] = data
    gram = lax.dot_general(
        data, noise, (((1,), (1,)), ((), ())), preferred_element_type=jnp.float32
    )
    data_sq = jnp.zeros((rows, LANES), jnp.float32)
    for start in range(0, ent, LANES):
        wide = data_ref[:, start : start + LANES].astype(jnp.float32)
        data_sq = data_sq + wide * wide
    data_sq = jnp.sum(data_sq, axis=1, keepdims=True)
    parts = data_sq - 2.0 * gram
    for tile, span, half in tiles(rows):
        out_ref[tile] = parts[span, half]


def sent_kernel(both_ref, out_ref, noise_ref, data_ref):
    noise_ref[...] = both_ref[:, :, : noise_ref.shape[1]].reshape(noise_ref.shape)
    half_of(both_ref, noise_ref[...], 1 - core(), data_ref, out_ref)


def kept_kernel(both_ref, noise_ref, other_ref, out_ref, data_ref, own):
    rows = own.shape[0]
    half_of(both_ref, noise_ref[...], core(), own, out_ref)
    data_ref[pl.ds(pl.multiple_of(core() * rows, rows), rows), :] = own[...]
    data_ref[pl.ds(pl.multiple_of((1 - core()) * rows, rows), rows), :] = other_ref[...]


def add_kernel(first_ref, second_ref, out_ref):
    out_ref[...] = first_ref[...] + second_ref[...]


def sum_kernel(parts_ref, out_ref):
    total = jnp.sum(parts_ref[...], axis=0)
    total = total[:4] + total[4:]
    total = jnp.concatenate([total, total], axis=0)
    out_ref[...] = jnp.broadcast_to(total[None], out_ref.shape)


def sweep_kernel(
    cost_ref, other_ref, data_ref, noise_ref, out_ref, pots_ref, noise_sq_ref,
    bias, kern, row_pot, col_pot, row_sum,
):
    for part, ref in ((core(), cost_ref), (1 - core(), other_ref)):
        first = part * (BATCH // 2)
        for tile, span, half in tiles(BATCH // 2):
            rows = pl.ds(pl.multiple_of(first + span.start, 8), 8)
            bias[rows, half] = ref[tile] * (-1.0 / (LATENT * BIT))
    col_pot[...] = jnp.zeros_like(col_pot)

    def log_sweep():
        scaled = bias[...] + col_pot[...]
        top = jnp.max(scaled, axis=0, keepdims=True)
        row = -(top + jnp.log2(jnp.sum(jnp.exp2(scaled - top), axis=0, keepdims=True)))
        scaled = bias[...] + row
        top = jnp.max(scaled, axis=1, keepdims=True)
        scaled = jnp.exp2(scaled - top)
        total = jnp.sum(scaled, axis=1, keepdims=True)
        row_pot[...] = row
        col_pot[...] = -(top + jnp.log2(total))
        kern[...] = scaled * (1.0 / total)

    log_sweep()

    tile = (8, LANES)
    blocks = [pl.ds(start, 8) for start in range(0, BATCH, 8)]
    halves = [pl.ds(start, LANES) for start in range(0, BATCH, LANES)]

    def over_columns(low, high, rows, use):
        sums = [[jnp.zeros(tile, jnp.float32) for _ in halves] for _ in range(2)]
        for n, block in enumerate(blocks):
            parts = [kern[block, half] for half in halves]
            if rows is not None:
                total = sum(part * row for part, row in zip(parts, rows))
                total = jnp.broadcast_to(jnp.sum(total, axis=1, keepdims=True), tile)
                low, high = jnp.minimum(low, total), jnp.maximum(high, total)
                factor = 1.0 / total
                parts = [part * factor for part in parts]
                if use is not None:
                    use(block, factor, parts)
            for h, part in enumerate(parts):
                sums[n % 2][h] += part
        totals = []
        for first, second in zip(*sums):
            total = jnp.broadcast_to(jnp.sum(first + second, axis=0, keepdims=True), tile)
            low = jnp.minimum(low, total)
            totals.append(total)
        return low, high, totals

    units = noise_ref.shape[1] // UNIT
    share = units // (SWEEPS - 2)

    def squares(first, count, total):
        for n in range(count):
            start = pl.multiple_of((first + n) * UNIT, LANES)
            unit = noise_ref[:, pl.ds(start, UNIT)].astype(jnp.float32)
            total = total + unit * unit
        return total

    def sweep(step, carry):
        low, high, rows, noise_sq = carry
        low, high, totals = over_columns(low, high, rows, None)
        for total in totals:
            high = jnp.maximum(high, total)
        if rows is not None:
            noise_sq = squares((step - 2) * share, share, noise_sq)
        return (low, high, tuple(1.0 / total for total in totals), noise_sq)

    def finish(block, factor, parts):
        col_pot[block, :] += jnp.log2(factor[:, :1])
        for half, part in zip(halves, parts):
            kern[block, half] = part

    ones = jnp.ones(tile, jnp.float32)
    carry = sweep(0, (ones, ones, None, jnp.zeros((noise_ref.shape[0], UNIT), jnp.float32)))
    low, high, rows, noise_sq = lax.fori_loop(2, SWEEPS, sweep, carry)
    done = (SWEEPS - 2) * share
    noise_sq = jnp.sum(squares(done, units - done, noise_sq), axis=1, keepdims=True)
    noise_sq_ref[...] = jnp.broadcast_to(noise_sq, noise_sq_ref.shape)
    low, high, totals = over_columns(low, high, rows, finish)
    row_pot[...] += jnp.log2(jnp.concatenate([row[:1] for row in rows], axis=1))
    row_sum[...] = jnp.concatenate([total[:1] for total in totals], axis=1)
    near = jnp.min(jnp.where((low >= 1.0 / DRIFT) & (high <= DRIFT), 1.0, 0.0)) > 0.5

    @pl.when(jnp.logical_not(near))
    def _():
        col_pot[...] = jnp.zeros_like(col_pot)

        def again(step, carry):
            log_sweep()
            return carry

        lax.fori_loop(0, SWEEPS, again, 0)
        scaled = bias[...] + col_pot[...]
        scaled = jnp.exp2(scaled - jnp.max(scaled, axis=0, keepdims=True))
        kern[...] = scaled
        row_sum[...] = jnp.sum(scaled, axis=0, keepdims=True)

    weights = (kern[...] * (1.0 / row_sum[...])).astype(jnp.bfloat16)
    moved = lax.dot_general(
        weights, data_ref[...], (((0,), (0,)), ((), ())), preferred_element_type=jnp.float32
    )
    out_ref[...] = moved.astype(jnp.bfloat16).reshape(out_ref.shape)
    pots_ref[0:1, :] = row_pot[...] * BIT
    pots_ref[1:2, :] = jnp.transpose(col_pot[...] * BIT)


def on_device(noise, data):
    devices = lax.axis_size(AXES)
    own = noise.shape[0]
    ent = UNITS * UNIT
    units = LATENT // UNIT
    params = pltpu.CompilerParams(vmem_limit_bytes=VMEM)
    anywhere = pl.BlockSpec(memory_space=pl.ANY)

    def units_of(rows):
        return rows.reshape(own, units, UNIT).transpose(1, 0, 2)

    both = pl.pallas_call(
        pack_kernel,
        out_shape=jax.ShapeDtypeStruct((devices, 2 * UNITS, own, UNIT), noise.dtype),
        in_specs=[pl.BlockSpec(memory_space=pltpu.HBM)] * 2,
        out_specs=anywhere,
        scratch_shapes=[
            pltpu.VMEM((UNITS * devices - units, own, UNIT), noise.dtype),
            pltpu.SemaphoreType.DMA((4 * UNITS,)),
        ],
        compiler_params=params,
    )(*[pltpu.with_memory_space_constraint(units_of(rows), pltpu.HBM) for rows in (noise, data)])
    both = both.transpose(0, 2, 1, 3).reshape(devices, own, 2 * ent)
    both = lax.all_to_all(both, AXES, split_axis=0, concat_axis=0)

    part = jax.ShapeDtypeStruct((devices // 4, 8, LANES), jnp.float32)
    data_half = jax.ShapeDtypeStruct((BATCH // 2, ent), data.dtype)
    data_whole = jax.ShapeDtypeStruct((BATCH, ent), data.dtype)

    def exchange(parts):
        parts = parts.reshape(devices, 2, LANES)
        return lax.all_to_all(parts, AXES, split_axis=0, concat_axis=0).reshape(part.shape)

    def other_core(parts):
        return lax.ppermute(parts, "dim", [(k, k ^ 1) for k in range(lax.axis_size("dim"))])

    sent, noise_ent, data_other = pl.pallas_call(
        sent_kernel, out_shape=(part, data_whole, data_half), compiler_params=params
    )(both)
    got = other_core(sent)
    kept, data_ent = pl.pallas_call(
        kept_kernel,
        out_shape=(part, data_whole),
        scratch_shapes=[pltpu.VMEM(data_half.shape, data_half.dtype)],
        compiler_params=params,
        cost_estimate=pl.CostEstimate(
            flops=BATCH * BATCH * ent, bytes_accessed=6 * BATCH * ent, transcendentals=0
        ),
    )(both, noise_ent, data_other)
    parts = pl.pallas_call(add_kernel, out_shape=part, compiler_params=params)(kept, got)
    total = pl.pallas_call(sum_kernel, out_shape=part, compiler_params=params)(exchange(parts))
    total = exchange(total)

    moved, pots, noise_sq = pl.pallas_call(
        sweep_kernel,
        out_shape=(
            jax.ShapeDtypeStruct((devices, own, ent), jnp.bfloat16),
            jax.ShapeDtypeStruct((2, BATCH), jnp.float32),
            jax.ShapeDtypeStruct((own, LANES), jnp.float32),
        ),
        scratch_shapes=[
            pltpu.VMEM((BATCH, BATCH), jnp.float32),
            pltpu.VMEM((BATCH, BATCH), jnp.float32),
            pltpu.VMEM((1, BATCH), jnp.float32),
            pltpu.VMEM((BATCH, 1), jnp.float32),
            pltpu.VMEM((1, BATCH), jnp.float32),
        ],
        compiler_params=params,
    )(total, other_core(total), data_ent, noise)
    moved = lax.all_to_all(moved, AXES, split_axis=0, concat_axis=0)
    moved = moved.reshape(devices, own, UNITS, UNIT).transpose(0, 2, 1, 3)
    in_vmem = pl.BlockSpec(memory_space=pltpu.VMEM)
    targets, row, col = pl.pallas_call(
        unpack_kernel,
        out_shape=(
            jax.ShapeDtypeStruct((units, own, UNIT), moved.dtype),
            jax.ShapeDtypeStruct((own,), jnp.float32),
            jax.ShapeDtypeStruct((own,), jnp.float32),
        ),
        in_specs=[anywhere, in_vmem, in_vmem],
        out_specs=(anywhere, anywhere, anywhere),
        scratch_shapes=[
            pltpu.SMEM((own,), jnp.float32),
            pltpu.SMEM((own,), jnp.float32),
            pltpu.SemaphoreType.DMA((UNITS + 2,)),
        ],
        compiler_params=params,
    )(moved, pots, noise_sq)
    return (targets.transpose(1, 0, 2).reshape(own, LATENT), row, col)


def solution(mesh):
    return jax.shard_map(
        on_device,
        mesh=mesh,
        in_specs=(P(AXES, None), P(AXES, None)),
        out_specs=(P(AXES, None), P(AXES), P(AXES)),
        check_vma=False,
    )
```

```python
import math

import jax
import jax.numpy as jnp
from jax import lax
from jax.experimental import pallas as pl
from jax.experimental.pallas import tpu as pltpu
from jax.sharding import PartitionSpec as P

SWEEPS = 20
LATENT = 324480
BATCH = 256
AXES = ("dp", "dim")
LANES = 128
TEMPER = 0.25 / math.sqrt(LATENT)
BIT = TEMPER * math.log(2.0)
DRIFT = 2.0**40
VMEM = 24 * 1024 * 1024
UNITS = 4
UNIT = 640


def pack_kernel(noise_ref, data_ref, out_ref, zeros, sems):
    devices, units = out_ref.shape[0], noise_ref.shape[0]
    zeros[...] = jnp.zeros_like(zeros)
    copies = []
    for kind, ref in enumerate((noise_ref, data_ref)):
        for q in range(UNITS):
            slot = kind * UNITS + q
            start = q * devices
            count = min(devices, units - start)
            copies.append((ref.at[pl.ds(start, count)], out_ref.at[pl.ds(0, count), slot]))
            if count < devices:
                copies.append((zeros, out_ref.at[pl.ds(count, devices - count), slot]))
    copies = [pltpu.make_async_copy(src, dst, sems.at[n]) for n, (src, dst) in enumerate(copies)]
    for copy in copies:
        copy.start()
    for copy in copies:
        copy.wait()


def unpack_kernel(moved_ref, pots_ref, noise_sq_ref, out_ref, row_ref, col_ref, row, col, sems):
    devices, units = moved_ref.shape[0], out_ref.shape[0]
    own = out_ref.shape[1]
    copies = []
    for q in range(UNITS):
        start = q * devices
        count = min(devices, units - start)
        copies.append((moved_ref.at[pl.ds(0, count), q], out_ref.at[pl.ds(start, count)]))
    copies.extend([(row, row_ref), (col, col_ref)])
    copies = [pltpu.make_async_copy(src, dst, sems.at[n]) for n, (src, dst) in enumerate(copies)]
    for copy in copies[:UNITS]:
        copy.start()

    first = (lax.axis_index("dp") * lax.axis_size("dim") + lax.axis_index("dim")) * own
    lane = lax.broadcasted_iota(jnp.int32, (1, BATCH), 1)
    for n in range(own):
        mine = lane == first + n
        row_pot = jnp.sum(jnp.where(mine, pots_ref[0:1, :], 0.0))
        row[n] = row_pot + jnp.max(noise_sq_ref[n : n + 1, :]) / LATENT
        col[n] = jnp.sum(jnp.where(mine, pots_ref[1:2, :], 0.0))
    for copy in copies[UNITS:]:
        copy.start()
    for copy in copies:
        copy.wait()


def tiles(rows):
    for tile in range(rows * BATCH // (8 * LANES)):
        row, half = 8 * (tile // 2), LANES * (tile % 2)
        yield tile, slice(row, row + 8), slice(half, half + LANES)


def core():
    return lax.rem(lax.axis_index("dim"), 2)


def half_of(both_ref, noise, part, data, out_ref):
    rows, ent = data.shape
    data[...] = both_ref[:, part, :, ent:].reshape(rows, ent)
    gram = lax.dot_general(
        data[...], noise, (((1,), (1,)), ((), ())), preferred_element_type=jnp.float32
    )
    data_sq = jnp.zeros((rows, LANES), jnp.float32)
    for start in range(0, ent, LANES):
        wide = data[:, start : start + LANES].astype(jnp.float32)
        data_sq = data_sq + wide * wide
    data_sq = jnp.sum(data_sq, axis=1, keepdims=True)
    parts = data_sq - 2.0 * gram
    for tile, span, half in tiles(rows):
        out_ref[tile] = parts[span, half]


def sent_kernel(both_ref, out_ref, noise_ref, data):
    noise_ref[...] = both_ref[:, :, :, : noise_ref.shape[1]].reshape(noise_ref.shape)
    half_of(both_ref, noise_ref[...], 1 - core(), data, out_ref)


def kept_kernel(both_ref, noise_ref, out_ref, data_ref, data):
    half_of(both_ref, noise_ref[...], core(), data, out_ref)
    data_ref[...] = both_ref[:, :, :, noise_ref.shape[1] :].reshape(data_ref.shape)


def add_kernel(first_ref, second_ref, out_ref):
    out_ref[...] = first_ref[...] + second_ref[...]


def sum_kernel(parts_ref, out_ref):
    total = jnp.sum(parts_ref[...], axis=0)
    total = total[:4] + total[4:]
    total = jnp.concatenate([total, total], axis=0)
    out_ref[...] = jnp.broadcast_to(total[None], out_ref.shape)


def sweep_kernel(
    cost_ref, data_ref, noise_ref, out_ref, pots_ref, noise_sq_ref,
    bias, kern, row_pot, col_pot, row_sum,
):
    for tile, rows, half in tiles(BATCH):
        block, side = tile // 2, tile % 2
        place = 4 * (block // 2) + 2 * side + block % 2
        bias[rows, half] = cost_ref[place] * (-1.0 / (LATENT * BIT))
    col_pot[...] = jnp.zeros_like(col_pot)

    def log_sweep():
        scaled = bias[...] + col_pot[...]
        top = jnp.max(scaled, axis=0, keepdims=True)
        row = -(top + jnp.log2(jnp.sum(jnp.exp2(scaled - top), axis=0, keepdims=True)))
        scaled = bias[...] + row
        top = jnp.max(scaled, axis=1, keepdims=True)
        scaled = jnp.exp2(scaled - top)
        total = jnp.sum(scaled, axis=1, keepdims=True)
        row_pot[...] = row
        col_pot[...] = -(top + jnp.log2(total))
        kern[...] = scaled * (1.0 / total)

    log_sweep()

    tile = (8, LANES)
    blocks = [pl.ds(start, 8) for start in range(0, BATCH, 8)]
    halves = [pl.ds(start, LANES) for start in range(0, BATCH, LANES)]

    def over_columns(low, high, rows, use):
        sums = [[jnp.zeros(tile, jnp.float32) for _ in halves] for _ in range(2)]
        for n, block in enumerate(blocks):
            parts = [kern[block, half] for half in halves]
            if rows is not None:
                total = sum(part * row for part, row in zip(parts, rows))
                total = jnp.broadcast_to(jnp.sum(total, axis=1, keepdims=True), tile)
                low, high = jnp.minimum(low, total), jnp.maximum(high, total)
                factor = 1.0 / total
                parts = [part * factor for part in parts]
                if use is not None:
                    use(block, factor, parts)
            for h, part in enumerate(parts):
                sums[n % 2][h] += part
        totals = []
        for first, second in zip(*sums):
            total = jnp.broadcast_to(jnp.sum(first + second, axis=0, keepdims=True), tile)
            low = jnp.minimum(low, total)
            totals.append(total)
        return low, high, totals

    units = noise_ref.shape[1] // UNIT
    share = units // (SWEEPS - 2)

    def squares(first, count, total):
        for n in range(count):
            start = pl.multiple_of((first + n) * UNIT, LANES)
            unit = noise_ref[:, pl.ds(start, UNIT)].astype(jnp.float32)
            total = total + unit * unit
        return total

    def sweep(step, carry):
        low, high, rows, noise_sq = carry
        low, high, totals = over_columns(low, high, rows, None)
        for total in totals:
            high = jnp.maximum(high, total)
        if rows is not None:
            noise_sq = squares((step - 2) * share, share, noise_sq)
        return (low, high, tuple(1.0 / total for total in totals), noise_sq)

    def finish(block, factor, parts):
        col_pot[block, :] += jnp.log2(factor[:, :1])
        for half, part in zip(halves, parts):
            kern[block, half] = part

    ones = jnp.ones(tile, jnp.float32)
    carry = sweep(0, (ones, ones, None, jnp.zeros((noise_ref.shape[0], UNIT), jnp.float32)))
    low, high, rows, noise_sq = lax.fori_loop(2, SWEEPS, sweep, carry)
    done = (SWEEPS - 2) * share
    noise_sq = jnp.sum(squares(done, units - done, noise_sq), axis=1, keepdims=True)
    noise_sq_ref[...] = jnp.broadcast_to(noise_sq, noise_sq_ref.shape)
    low, high, totals = over_columns(low, high, rows, finish)
    row_pot[...] += jnp.log2(jnp.concatenate([row[:1] for row in rows], axis=1))
    row_sum[...] = jnp.concatenate([total[:1] for total in totals], axis=1)
    near = jnp.min(jnp.where((low >= 1.0 / DRIFT) & (high <= DRIFT), 1.0, 0.0)) > 0.5

    @pl.when(jnp.logical_not(near))
    def _():
        col_pot[...] = jnp.zeros_like(col_pot)

        def again(step, carry):
            log_sweep()
            return carry

        lax.fori_loop(0, SWEEPS, again, 0)
        scaled = bias[...] + col_pot[...]
        scaled = jnp.exp2(scaled - jnp.max(scaled, axis=0, keepdims=True))
        kern[...] = scaled
        row_sum[...] = jnp.sum(scaled, axis=0, keepdims=True)

    weights = (kern[...] * (1.0 / row_sum[...])).astype(jnp.bfloat16)
    moved = lax.dot_general(
        weights, data_ref[...], (((0,), (0,)), ((), ())), preferred_element_type=jnp.float32
    )
    out_ref[...] = moved.astype(jnp.bfloat16).reshape(out_ref.shape)
    pots_ref[0:1, :] = row_pot[...] * BIT
    pots_ref[1:2, :] = jnp.transpose(col_pot[...] * BIT)


def on_device(noise, data):
    devices = lax.axis_size(AXES)
    own = noise.shape[0]
    ent = UNITS * UNIT
    units = LATENT // UNIT
    params = pltpu.CompilerParams(vmem_limit_bytes=VMEM)
    anywhere = pl.BlockSpec(memory_space=pl.ANY)

    def units_of(rows):
        return rows.reshape(own, units, UNIT).transpose(1, 0, 2)

    both = pl.pallas_call(
        pack_kernel,
        out_shape=jax.ShapeDtypeStruct((devices, 2 * UNITS, own, UNIT), noise.dtype),
        in_specs=[pl.BlockSpec(memory_space=pltpu.HBM)] * 2,
        out_specs=anywhere,
        scratch_shapes=[
            pltpu.VMEM((UNITS * devices - units, own, UNIT), noise.dtype),
            pltpu.SemaphoreType.DMA((4 * UNITS,)),
        ],
        compiler_params=params,
    )(*[pltpu.with_memory_space_constraint(units_of(rows), pltpu.HBM) for rows in (noise, data)])
    both = both.transpose(0, 2, 1, 3).reshape(devices, own, 2 * ent)
    both = lax.all_to_all(both, AXES, split_axis=0, concat_axis=0)

    part = jax.ShapeDtypeStruct((devices // 4, 8, LANES), jnp.float32)
    whole = jax.ShapeDtypeStruct((devices // 2, 8, LANES), jnp.float32)
    data_whole = jax.ShapeDtypeStruct((BATCH, ent), data.dtype)
    data_half = pltpu.VMEM((BATCH // 2, ent), data.dtype)

    def exchange(parts):
        shape = parts.shape
        parts = parts.reshape(devices, -1, LANES)
        return lax.all_to_all(parts, AXES, split_axis=0, concat_axis=0).reshape(shape)

    both = both.reshape(devices // 2, 2, own, 2 * ent)
    sent, noise_ent = pl.pallas_call(
        sent_kernel, out_shape=(part, data_whole), scratch_shapes=[data_half], compiler_params=params
    )(both)
    got = lax.ppermute(sent, "dim", [(k, k ^ 1) for k in range(lax.axis_size("dim"))])
    kept, data_ent = pl.pallas_call(
        kept_kernel,
        out_shape=(part, data_whole),
        scratch_shapes=[data_half],
        compiler_params=params,
        cost_estimate=pl.CostEstimate(
            flops=BATCH * BATCH * ent, bytes_accessed=6 * BATCH * ent, transcendentals=0
        ),
    )(both, noise_ent)
    parts = pl.pallas_call(add_kernel, out_shape=part, compiler_params=params)(kept, got)
    total = pl.pallas_call(sum_kernel, out_shape=whole, compiler_params=params)(exchange(parts))
    total = exchange(total)

    moved, pots, noise_sq = pl.pallas_call(
        sweep_kernel,
        out_shape=(
            jax.ShapeDtypeStruct((devices, own, ent), jnp.bfloat16),
            jax.ShapeDtypeStruct((2, BATCH), jnp.float32),
            jax.ShapeDtypeStruct((own, LANES), jnp.float32),
        ),
        scratch_shapes=[
            pltpu.VMEM((BATCH, BATCH), jnp.float32),
            pltpu.VMEM((BATCH, BATCH), jnp.float32),
            pltpu.VMEM((1, BATCH), jnp.float32),
            pltpu.VMEM((BATCH, 1), jnp.float32),
            pltpu.VMEM((1, BATCH), jnp.float32),
        ],
        compiler_params=params,
    )(total, data_ent, noise)
    moved = lax.all_to_all(moved, AXES, split_axis=0, concat_axis=0)
    moved = moved.reshape(devices, own, UNITS, UNIT).transpose(0, 2, 1, 3)
    in_vmem = pl.BlockSpec(memory_space=pltpu.VMEM)
    targets, row, col = pl.pallas_call(
        unpack_kernel,
        out_shape=(
            jax.ShapeDtypeStruct((units, own, UNIT), moved.dtype),
            jax.ShapeDtypeStruct((own,), jnp.float32),
            jax.ShapeDtypeStruct((own,), jnp.float32),
        ),
        in_specs=[anywhere, in_vmem, in_vmem],
        out_specs=(anywhere, anywhere, anywhere),
        scratch_shapes=[
            pltpu.SMEM((own,), jnp.float32),
            pltpu.SMEM((own,), jnp.float32),
            pltpu.SemaphoreType.DMA((UNITS + 2,)),
        ],
        compiler_params=params,
    )(moved, pots, noise_sq)
    return (targets.transpose(1, 0, 2).reshape(own, LATENT), row, col)


def solution(mesh):
    return jax.shard_map(
        on_device,
        mesh=mesh,
        in_specs=(P(AXES, None), P(AXES, None)),
        out_specs=(P(AXES, None), P(AXES), P(AXES)),
        check_vma=False,
    )
```

```python
import math

import jax
import jax.numpy as jnp
from jax import lax
from jax.experimental import pallas as pl
from jax.experimental.pallas import tpu as pltpu
from jax.sharding import PartitionSpec as P

SWEEPS = 20
LATENT = 324480
BATCH = 256
AXES = ("dp", "dim")
LANES = 128
TEMPER = 0.25 / math.sqrt(LATENT)
BIT = TEMPER * math.log(2.0)
DRIFT = 2.0**40
VMEM = 24 * 1024 * 1024
UNITS = 4
UNIT = 640


def pack_kernel(noise_ref, data_ref, out_ref, zeros, sems):
    devices, units = out_ref.shape[0], noise_ref.shape[0]
    zeros[...] = jnp.zeros_like(zeros)
    copies = []
    for kind, ref in enumerate((noise_ref, data_ref)):
        for q in range(UNITS):
            slot = kind * UNITS + q
            start = q * devices
            count = min(devices, units - start)
            copies.append((ref.at[pl.ds(start, count)], out_ref.at[pl.ds(0, count), slot]))
            if count < devices:
                copies.append((zeros, out_ref.at[pl.ds(count, devices - count), slot]))
    copies = [pltpu.make_async_copy(src, dst, sems.at[n]) for n, (src, dst) in enumerate(copies)]
    for copy in copies:
        copy.start()
    for copy in copies:
        copy.wait()


def unpack_kernel(moved_ref, pots_ref, noise_sq_ref, out_ref, row_ref, col_ref, row, col, sems):
    devices, units = moved_ref.shape[0], out_ref.shape[0]
    own = out_ref.shape[1]
    copies = []
    for q in range(UNITS):
        start = q * devices
        count = min(devices, units - start)
        copies.append((moved_ref.at[pl.ds(0, count), q], out_ref.at[pl.ds(start, count)]))
    copies.extend([(row, row_ref), (col, col_ref)])
    copies = [pltpu.make_async_copy(src, dst, sems.at[n]) for n, (src, dst) in enumerate(copies)]
    for copy in copies[:UNITS]:
        copy.start()

    first = (lax.axis_index("dp") * lax.axis_size("dim") + lax.axis_index("dim")) * own
    lane = lax.broadcasted_iota(jnp.int32, (1, BATCH), 1)
    for n in range(own):
        mine = lane == first + n
        row_pot = jnp.sum(jnp.where(mine, pots_ref[0:1, :], 0.0))
        row[n] = row_pot + jnp.max(noise_sq_ref[n : n + 1, :]) / LATENT
        col[n] = jnp.sum(jnp.where(mine, pots_ref[1:2, :], 0.0))
    for copy in copies[UNITS:]:
        copy.start()
    for copy in copies:
        copy.wait()


def tiles():
    for tile in range(BATCH * BATCH // (8 * LANES)):
        row, half = 8 * (tile // 2), LANES * (tile % 2)
        yield tile, slice(row, row + 8), slice(half, half + LANES)


def gram_kernel(both_ref, out_ref, data_ref):
    ent = data_ref.shape[1]
    noise = both_ref[:, :, :ent].reshape(data_ref.shape)
    data = both_ref[:, :, ent:].reshape(data_ref.shape)
    data_ref[...] = data
    gram = lax.dot_general(
        data, noise, (((1,), (1,)), ((), ())), preferred_element_type=jnp.float32
    )
    data_sq = jnp.zeros((BATCH, LANES), jnp.float32)
    for start in range(0, ent, LANES):
        wide = data_ref[:, start : start + LANES].astype(jnp.float32)
        data_sq = data_sq + wide * wide
    data_sq = jnp.sum(data_sq, axis=1, keepdims=True)
    parts = data_sq - 2.0 * gram
    for tile, rows, half in tiles():
        out_ref[tile] = parts[rows, half]


def sum_kernel(parts_ref, out_ref):
    total = jnp.sum(parts_ref[...], axis=0)
    total = total[:4] + total[4:]
    total = jnp.concatenate([total, total], axis=0)
    out_ref[...] = jnp.broadcast_to(total[None], out_ref.shape)


def sweep_kernel(
    cost_ref, data_ref, noise_ref, out_ref, pots_ref, noise_sq_ref,
    bias, kern, row_pot, col_pot, row_sum,
):
    for tile, rows, half in tiles():
        bias[rows, half] = cost_ref[tile] * (-1.0 / (LATENT * BIT))

    def log_sweep(scaled):
        top = jnp.max(scaled, axis=0, keepdims=True)
        row = -(top + jnp.log2(jnp.sum(jnp.exp2(scaled - top), axis=0, keepdims=True)))
        scaled = bias[...] + row
        top = jnp.max(scaled, axis=1, keepdims=True)
        scaled = jnp.exp2(scaled - top)
        total = jnp.sum(scaled, axis=1, keepdims=True)
        row_pot[...] = row
        col_pot[...] = -(top + jnp.log2(total))
        scaled = scaled * (1.0 / total)
        kern[...] = scaled
        return jnp.sum(scaled, axis=0, keepdims=True)

    total = log_sweep(bias[...])

    tile = (8, LANES)
    blocks = [pl.ds(start, 8) for start in range(0, BATCH, 8)]
    halves = [pl.ds(start, LANES) for start in range(0, BATCH, LANES)]

    def over_columns(low, high, rows, use):
        sums = [[jnp.zeros(tile, jnp.float32) for _ in halves] for _ in range(2)]
        for n, block in enumerate(blocks):
            parts = [kern[block, half] for half in halves]
            total = sum(part * row for part, row in zip(parts, rows))
            total = jnp.broadcast_to(jnp.sum(total, axis=1, keepdims=True), tile)
            low, high = jnp.minimum(low, total), jnp.maximum(high, total)
            factor = 1.0 / total
            parts = [part * factor for part in parts]
            if use is not None:
                use(block, factor, parts)
            for h, part in enumerate(parts):
                sums[n % 2][h] += part
        totals = []
        for first, second in zip(*sums):
            total = jnp.broadcast_to(jnp.sum(first + second, axis=0, keepdims=True), tile)
            low = jnp.minimum(low, total)
            totals.append(total)
        return low, high, totals

    units = noise_ref.shape[1] // UNIT
    share = units // (SWEEPS - 2)

    def squares(first, count, total):
        for n in range(count):
            start = pl.multiple_of((first + n) * UNIT, LANES)
            unit = noise_ref[:, pl.ds(start, UNIT)].astype(jnp.float32)
            total = total + unit * unit
        return total

    def sweep(step, carry):
        low, high, rows, noise_sq = carry
        low, high, totals = over_columns(low, high, rows, None)
        for total in totals:
            high = jnp.maximum(high, total)
        noise_sq = squares((step - 2) * share, share, noise_sq)
        return (low, high, tuple(1.0 / total for total in totals), noise_sq)

    def finish(block, factor, parts):
        col_pot[block, :] += jnp.log2(factor[:, :1])
        for half, part in zip(halves, parts):
            kern[block, half] = part

    totals = [jnp.broadcast_to(total[:, half.start : half.start + LANES], tile) for half in halves]
    low, high = jnp.minimum(*totals), jnp.maximum(*totals)
    noise_sq = jnp.zeros((noise_ref.shape[0], UNIT), jnp.float32)
    carry = (low, high, tuple(1.0 / total for total in totals), noise_sq)
    low, high, rows, noise_sq = lax.fori_loop(2, SWEEPS, sweep, carry)
    done = (SWEEPS - 2) * share
    noise_sq = jnp.sum(squares(done, units - done, noise_sq), axis=1, keepdims=True)
    noise_sq_ref[...] = jnp.broadcast_to(noise_sq, noise_sq_ref.shape)
    low, high, totals = over_columns(low, high, rows, finish)
    row_pot[...] += jnp.log2(jnp.concatenate([row[:1] for row in rows], axis=1))
    row_sum[...] = jnp.concatenate([total[:1] for total in totals], axis=1)
    near = jnp.min(jnp.where((low >= 1.0 / DRIFT) & (high <= DRIFT), 1.0, 0.0)) > 0.5

    @pl.when(jnp.logical_not(near))
    def _():
        col_pot[...] = jnp.zeros_like(col_pot)

        def again(step, carry):
            log_sweep(bias[...] + col_pot[...])
            return carry

        lax.fori_loop(0, SWEEPS, again, 0)
        scaled = bias[...] + col_pot[...]
        scaled = jnp.exp2(scaled - jnp.max(scaled, axis=0, keepdims=True))
        kern[...] = scaled
        row_sum[...] = jnp.sum(scaled, axis=0, keepdims=True)

    weights = (kern[...] * (1.0 / row_sum[...])).astype(jnp.bfloat16)
    moved = lax.dot_general(
        weights, data_ref[...], (((0,), (0,)), ((), ())), preferred_element_type=jnp.float32
    )
    out_ref[...] = moved.astype(jnp.bfloat16).reshape(out_ref.shape)
    pots_ref[0:1, :] = row_pot[...] * BIT
    pots_ref[1:2, :] = jnp.transpose(col_pot[...] * BIT)


def on_device(noise, data):
    devices = lax.axis_size(AXES)
    own = noise.shape[0]
    ent = UNITS * UNIT
    units = LATENT // UNIT
    params = pltpu.CompilerParams(vmem_limit_bytes=VMEM)
    anywhere = pl.BlockSpec(memory_space=pl.ANY)

    def units_of(rows):
        return rows.reshape(own, units, UNIT).transpose(1, 0, 2)

    both = pl.pallas_call(
        pack_kernel,
        out_shape=jax.ShapeDtypeStruct((devices, 2 * UNITS, own, UNIT), noise.dtype),
        in_specs=[pl.BlockSpec(memory_space=pltpu.HBM)] * 2,
        out_specs=anywhere,
        scratch_shapes=[
            pltpu.VMEM((UNITS * devices - units, own, UNIT), noise.dtype),
            pltpu.SemaphoreType.DMA((4 * UNITS,)),
        ],
        compiler_params=params,
    )(*[pltpu.with_memory_space_constraint(units_of(rows), pltpu.HBM) for rows in (noise, data)])
    both = both.transpose(0, 2, 1, 3).reshape(devices, own, 2 * ent)
    both = lax.all_to_all(both, AXES, split_axis=0, concat_axis=0)

    whole = jax.ShapeDtypeStruct((devices // 2, 8, LANES), jnp.float32)

    def exchange(parts):
        parts = parts.reshape(devices, 4, LANES)
        return lax.all_to_all(parts, AXES, split_axis=0, concat_axis=0).reshape(whole.shape)

    parts, data_ent = pl.pallas_call(
        gram_kernel,
        out_shape=(whole, jax.ShapeDtypeStruct((BATCH, ent), data.dtype)),
        compiler_params=params,
    )(both)
    total = pl.pallas_call(sum_kernel, out_shape=whole, compiler_params=params)(exchange(parts))
    total = exchange(total)

    moved, pots, noise_sq = pl.pallas_call(
        sweep_kernel,
        out_shape=(
            jax.ShapeDtypeStruct((devices, own, ent), jnp.bfloat16),
            jax.ShapeDtypeStruct((2, BATCH), jnp.float32),
            jax.ShapeDtypeStruct((own, LANES), jnp.float32),
        ),
        scratch_shapes=[
            pltpu.VMEM((BATCH, BATCH), jnp.float32),
            pltpu.VMEM((BATCH, BATCH), jnp.float32),
            pltpu.VMEM((1, BATCH), jnp.float32),
            pltpu.VMEM((BATCH, 1), jnp.float32),
            pltpu.VMEM((1, BATCH), jnp.float32),
        ],
        compiler_params=params,
    )(total, data_ent, noise)
    moved = lax.all_to_all(moved, AXES, split_axis=0, concat_axis=0)
    moved = moved.reshape(devices, own, UNITS, UNIT).transpose(0, 2, 1, 3)
    in_vmem = pl.BlockSpec(memory_space=pltpu.VMEM)
    targets, row, col = pl.pallas_call(
        unpack_kernel,
        out_shape=(
            jax.ShapeDtypeStruct((units, own, UNIT), moved.dtype),
            jax.ShapeDtypeStruct((own,), jnp.float32),
            jax.ShapeDtypeStruct((own,), jnp.float32),
        ),
        in_specs=[anywhere, in_vmem, in_vmem],
        out_specs=(anywhere, anywhere, anywhere),
        scratch_shapes=[
            pltpu.SMEM((own,), jnp.float32),
            pltpu.SMEM((own,), jnp.float32),
            pltpu.SemaphoreType.DMA((UNITS + 2,)),
        ],
        compiler_params=params,
    )(moved, pots, noise_sq)
    return (targets.transpose(1, 0, 2).reshape(own, LATENT), row, col)


def solution(mesh):
    return jax.shard_map(
        on_device,
        mesh=mesh,
        in_specs=(P(AXES, None), P(AXES, None)),
        out_specs=(P(AXES, None), P(AXES), P(AXES)),
        check_vma=False,
    )
```

```python
import math

import jax
import jax.numpy as jnp
from jax import lax
from jax.experimental import pallas as pl
from jax.experimental.pallas import tpu as pltpu
from jax.sharding import PartitionSpec as P

SWEEPS = 20
LATENT = 324480
BATCH = 256
AXES = ("dp", "dim")
LANES = 128
TEMPER = 0.25 / math.sqrt(LATENT)
BIT = TEMPER * math.log(2.0)
DRIFT = 2.0**40
VMEM = 24 * 1024 * 1024
UNITS = 4
UNIT = 640


def pack_kernel(noise_ref, data_ref, out_ref, zeros, sems):
    devices, units = out_ref.shape[0], noise_ref.shape[0]
    zeros[...] = jnp.zeros_like(zeros)
    copies = []
    for kind, ref in enumerate((noise_ref, data_ref)):
        for q in range(UNITS):
            slot = kind * UNITS + q
            start = q * devices
            count = min(devices, units - start)
            copies.append((ref.at[pl.ds(start, count)], out_ref.at[pl.ds(0, count), slot]))
            if count < devices:
                copies.append((zeros, out_ref.at[pl.ds(count, devices - count), slot]))
    copies = [pltpu.make_async_copy(src, dst, sems.at[n]) for n, (src, dst) in enumerate(copies)]
    for copy in copies:
        copy.start()
    for copy in copies:
        copy.wait()


def unpack_kernel(moved_ref, pots_ref, noise_sq_ref, out_ref, row_ref, col_ref, row, col, sems):
    devices, units = moved_ref.shape[0], out_ref.shape[0]
    own = out_ref.shape[1]
    copies = []
    for q in range(UNITS):
        start = q * devices
        count = min(devices, units - start)
        copies.append((moved_ref.at[pl.ds(0, count), q], out_ref.at[pl.ds(start, count)]))
    copies.extend([(row, row_ref), (col, col_ref)])
    copies = [pltpu.make_async_copy(src, dst, sems.at[n]) for n, (src, dst) in enumerate(copies)]
    for copy in copies[:UNITS]:
        copy.start()

    first = (lax.axis_index("dp") * lax.axis_size("dim") + lax.axis_index("dim")) * own
    lane = lax.broadcasted_iota(jnp.int32, (1, BATCH), 1)
    for n in range(own):
        mine = lane == first + n
        row_pot = jnp.sum(jnp.where(mine, pots_ref[0:1, :], 0.0))
        row[n] = row_pot + jnp.max(noise_sq_ref[n : n + 1, :]) / LATENT
        col[n] = jnp.sum(jnp.where(mine, pots_ref[1:2, :], 0.0))
    for copy in copies[UNITS:]:
        copy.start()
    for copy in copies:
        copy.wait()


def tiles():
    for tile in range(BATCH * BATCH // (8 * LANES)):
        row, half = 8 * (tile // 2), LANES * (tile % 2)
        yield tile, slice(row, row + 8), slice(half, half + LANES)


def gram_kernel(both_ref, out_ref, data_ref):
    ent = data_ref.shape[1]
    noise = jnp.transpose(both_ref[:, :, :ent].reshape(data_ref.shape))
    data = both_ref[:, :, ent:].reshape(data_ref.shape)
    data_ref[...] = data
    gram = jnp.dot(data, noise, preferred_element_type=jnp.float32)
    data_sq = jnp.zeros((BATCH, LANES), jnp.float32)
    for start in range(0, ent, LANES):
        wide = data_ref[:, start : start + LANES].astype(jnp.float32)
        data_sq = data_sq + wide * wide
    data_sq = jnp.sum(data_sq, axis=1, keepdims=True)
    parts = data_sq - 2.0 * gram
    for tile, rows, half in tiles():
        out_ref[tile] = parts[rows, half]


def sum_kernel(parts_ref, out_ref):
    total = jnp.sum(parts_ref[...], axis=0)
    total = total[:4] + total[4:]
    total = jnp.concatenate([total, total], axis=0)
    out_ref[...] = jnp.broadcast_to(total[None], out_ref.shape)


def sweep_kernel(
    cost_ref, data_ref, noise_ref, out_ref, pots_ref, noise_sq_ref,
    bias, kern, row_pot, col_pot, row_sum,
):
    for tile, rows, half in tiles():
        bias[rows, half] = cost_ref[tile] * (-1.0 / (LATENT * BIT))

    def log_sweep(scaled):
        top = jnp.max(scaled, axis=0, keepdims=True)
        row = -(top + jnp.log2(jnp.sum(jnp.exp2(scaled - top), axis=0, keepdims=True)))
        scaled = bias[...] + row
        top = jnp.max(scaled, axis=1, keepdims=True)
        scaled = jnp.exp2(scaled - top)
        total = jnp.sum(scaled, axis=1, keepdims=True)
        row_pot[...] = row
        col_pot[...] = -(top + jnp.log2(total))
        scaled = scaled * (1.0 / total)
        kern[...] = scaled
        return jnp.sum(scaled, axis=0, keepdims=True)

    total = log_sweep(bias[...])

    tile = (8, LANES)
    blocks = [pl.ds(start, 8) for start in range(0, BATCH, 8)]
    halves = [pl.ds(start, LANES) for start in range(0, BATCH, LANES)]

    def over_columns(low, high, rows, use):
        sums = [[jnp.zeros(tile, jnp.float32) for _ in halves] for _ in range(2)]
        for n, block in enumerate(blocks):
            parts = [kern[block, half] for half in halves]
            total = sum(part * row for part, row in zip(parts, rows))
            total = jnp.broadcast_to(jnp.sum(total, axis=1, keepdims=True), tile)
            low, high = jnp.minimum(low, total), jnp.maximum(high, total)
            factor = 1.0 / total
            parts = [part * factor for part in parts]
            if use is not None:
                use(block, factor, parts)
            for h, part in enumerate(parts):
                sums[n % 2][h] += part
        totals = []
        for first, second in zip(*sums):
            total = jnp.broadcast_to(jnp.sum(first + second, axis=0, keepdims=True), tile)
            low = jnp.minimum(low, total)
            totals.append(total)
        return low, high, totals

    units = noise_ref.shape[1] // UNIT
    share = units // (SWEEPS - 2)

    def squares(first, count, total):
        for n in range(count):
            start = pl.multiple_of((first + n) * UNIT, LANES)
            unit = noise_ref[:, pl.ds(start, UNIT)].astype(jnp.float32)
            total = total + unit * unit
        return total

    def sweep(step, carry):
        low, high, rows, noise_sq = carry
        low, high, totals = over_columns(low, high, rows, None)
        for total in totals:
            high = jnp.maximum(high, total)
        noise_sq = squares((step - 2) * share, share, noise_sq)
        return (low, high, tuple(1.0 / total for total in totals), noise_sq)

    def finish(block, factor, parts):
        col_pot[block, :] += jnp.log2(factor[:, :1])
        for half, part in zip(halves, parts):
            kern[block, half] = part

    totals = [jnp.broadcast_to(total[:, half.start : half.start + LANES], tile) for half in halves]
    low, high = jnp.minimum(*totals), jnp.maximum(*totals)
    noise_sq = jnp.zeros((noise_ref.shape[0], UNIT), jnp.float32)
    carry = (low, high, tuple(1.0 / total for total in totals), noise_sq)
    low, high, rows, noise_sq = lax.fori_loop(2, SWEEPS, sweep, carry)
    done = (SWEEPS - 2) * share
    noise_sq = jnp.sum(squares(done, units - done, noise_sq), axis=1, keepdims=True)
    noise_sq_ref[...] = jnp.broadcast_to(noise_sq, noise_sq_ref.shape)
    low, high, totals = over_columns(low, high, rows, finish)
    row_pot[...] += jnp.log2(jnp.concatenate([row[:1] for row in rows], axis=1))
    row_sum[...] = jnp.concatenate([total[:1] for total in totals], axis=1)
    near = jnp.min(jnp.where((low >= 1.0 / DRIFT) & (high <= DRIFT), 1.0, 0.0)) > 0.5

    def targets():
        weights = (kern[...] * (1.0 / row_sum[...])).astype(jnp.bfloat16)
        moved = lax.dot_general(
            weights, data_ref[...], (((0,), (0,)), ((), ())), preferred_element_type=jnp.float32
        )
        out_ref[...] = moved.astype(jnp.bfloat16).reshape(out_ref.shape)

    targets()

    @pl.when(jnp.logical_not(near))
    def _():
        col_pot[...] = jnp.zeros_like(col_pot)

        def again(step, carry):
            log_sweep(bias[...] + col_pot[...])
            return carry

        lax.fori_loop(0, SWEEPS, again, 0)
        scaled = bias[...] + col_pot[...]
        scaled = jnp.exp2(scaled - jnp.max(scaled, axis=0, keepdims=True))
        kern[...] = scaled
        row_sum[...] = jnp.sum(scaled, axis=0, keepdims=True)
        targets()

    pots_ref[0:1, :] = row_pot[...] * BIT
    pots_ref[1:2, :] = jnp.transpose(col_pot[...] * BIT)


def on_device(noise, data):
    devices = lax.axis_size(AXES)
    own = noise.shape[0]
    ent = UNITS * UNIT
    units = LATENT // UNIT
    params = pltpu.CompilerParams(vmem_limit_bytes=VMEM)
    anywhere = pl.BlockSpec(memory_space=pl.ANY)

    def units_of(rows):
        return rows.reshape(own, units, UNIT).transpose(1, 0, 2)

    both = pl.pallas_call(
        pack_kernel,
        out_shape=jax.ShapeDtypeStruct((devices, 2 * UNITS, own, UNIT), noise.dtype),
        in_specs=[pl.BlockSpec(memory_space=pltpu.HBM)] * 2,
        out_specs=anywhere,
        scratch_shapes=[
            pltpu.VMEM((UNITS * devices - units, own, UNIT), noise.dtype),
            pltpu.SemaphoreType.DMA((4 * UNITS,)),
        ],
        compiler_params=params,
    )(*[pltpu.with_memory_space_constraint(units_of(rows), pltpu.HBM) for rows in (noise, data)])
    both = both.transpose(0, 2, 1, 3).reshape(devices, own, 2 * ent)
    both = lax.all_to_all(both, AXES, split_axis=0, concat_axis=0)

    whole = jax.ShapeDtypeStruct((devices // 2, 8, LANES), jnp.float32)

    def exchange(parts):
        parts = parts.reshape(devices, 4, LANES)
        return lax.all_to_all(parts, AXES, split_axis=0, concat_axis=0).reshape(whole.shape)

    parts, data_ent = pl.pallas_call(
        gram_kernel,
        out_shape=(whole, jax.ShapeDtypeStruct((BATCH, ent), data.dtype)),
        compiler_params=params,
    )(both)
    total = pl.pallas_call(sum_kernel, out_shape=whole, compiler_params=params)(exchange(parts))
    total = exchange(total)

    moved, pots, noise_sq = pl.pallas_call(
        sweep_kernel,
        out_shape=(
            jax.ShapeDtypeStruct((devices, own, ent), jnp.bfloat16),
            jax.ShapeDtypeStruct((2, BATCH), jnp.float32),
            jax.ShapeDtypeStruct((own, LANES), jnp.float32),
        ),
        scratch_shapes=[
            pltpu.VMEM((BATCH, BATCH), jnp.float32),
            pltpu.VMEM((BATCH, BATCH), jnp.float32),
            pltpu.VMEM((1, BATCH), jnp.float32),
            pltpu.VMEM((BATCH, 1), jnp.float32),
            pltpu.VMEM((1, BATCH), jnp.float32),
        ],
        compiler_params=params,
    )(total, data_ent, noise)
    moved = lax.all_to_all(moved, AXES, split_axis=0, concat_axis=0)
    moved = moved.reshape(devices, own, UNITS, UNIT).transpose(0, 2, 1, 3)
    in_vmem = pl.BlockSpec(memory_space=pltpu.VMEM)
    targets, row, col = pl.pallas_call(
        unpack_kernel,
        out_shape=(
            jax.ShapeDtypeStruct((units, own, UNIT), moved.dtype),
            jax.ShapeDtypeStruct((own,), jnp.float32),
            jax.ShapeDtypeStruct((own,), jnp.float32),
        ),
        in_specs=[anywhere, in_vmem, in_vmem],
        out_specs=(anywhere, anywhere, anywhere),
        scratch_shapes=[
            pltpu.SMEM((own,), jnp.float32),
            pltpu.SMEM((own,), jnp.float32),
            pltpu.SemaphoreType.DMA((UNITS + 2,)),
        ],
        compiler_params=params,
    )(moved, pots, noise_sq)
    return (targets.transpose(1, 0, 2).reshape(own, LATENT), row, col)


def solution(mesh):
    return jax.shard_map(
        on_device,
        mesh=mesh,
        in_specs=(P(AXES, None), P(AXES, None)),
        out_specs=(P(AXES, None), P(AXES), P(AXES)),
        check_vma=False,
    )
```

```python
import math

import jax
import jax.numpy as jnp
from jax import lax
from jax.experimental import pallas as pl
from jax.experimental.pallas import tpu as pltpu
from jax.sharding import PartitionSpec as P

SWEEPS = 20
LATENT = 324480
BATCH = 256
AXES = ("dp", "dim")
LANES = 128
TEMPER = 0.25 / math.sqrt(LATENT)
BIT = TEMPER * math.log(2.0)
DRIFT = 2.0**40
VMEM = 24 * 1024 * 1024
UNITS = 4
UNIT = 640


def pack_kernel(noise_ref, data_ref, out_ref, zeros, sems):
    devices, units = out_ref.shape[0], noise_ref.shape[0]
    zeros[...] = jnp.zeros_like(zeros)
    copies = []
    for kind, ref in enumerate((noise_ref, data_ref)):
        for q in range(UNITS):
            slot = kind * UNITS + q
            start = q * devices
            count = min(devices, units - start)
            copies.append((ref.at[pl.ds(start, count)], out_ref.at[pl.ds(0, count), slot]))
            if count < devices:
                copies.append((zeros, out_ref.at[pl.ds(count, devices - count), slot]))
    copies = [pltpu.make_async_copy(src, dst, sems.at[n]) for n, (src, dst) in enumerate(copies)]
    for copy in copies:
        copy.start()
    for copy in copies:
        copy.wait()


def unpack_kernel(moved_ref, pots_ref, noise_sq_ref, out_ref, row_ref, col_ref, row, col, sems):
    devices, units = moved_ref.shape[0], out_ref.shape[0]
    own = out_ref.shape[1]
    copies = []
    for q in range(UNITS):
        start = q * devices
        count = min(devices, units - start)
        copies.append((moved_ref.at[pl.ds(0, count), q], out_ref.at[pl.ds(start, count)]))
    copies.extend([(row, row_ref), (col, col_ref)])
    copies = [pltpu.make_async_copy(src, dst, sems.at[n]) for n, (src, dst) in enumerate(copies)]
    for copy in copies[:UNITS]:
        copy.start()

    first = (lax.axis_index("dp") * lax.axis_size("dim") + lax.axis_index("dim")) * own
    lane = lax.broadcasted_iota(jnp.int32, (1, BATCH), 1)
    for n in range(own):
        mine = lane == first + n
        row_pot = jnp.sum(jnp.where(mine, pots_ref[0:1, :], 0.0))
        row[n] = row_pot + jnp.max(noise_sq_ref[n : n + 1, :]) / LATENT
        col[n] = jnp.sum(jnp.where(mine, pots_ref[1:2, :], 0.0))
    for copy in copies[UNITS:]:
        copy.start()
    for copy in copies:
        copy.wait()


def tiles():
    for tile in range(BATCH * BATCH // (8 * LANES)):
        row, half = 8 * (tile // 2), LANES * (tile % 2)
        yield tile, slice(row, row + 8), slice(half, half + LANES)


def gram_kernel(both_ref, out_ref, data_ref):
    ent = data_ref.shape[1]
    noise = jnp.transpose(both_ref[:, :, :ent].reshape(data_ref.shape))
    data_ref[...] = both_ref[:, :, ent:].reshape(data_ref.shape)
    gram = jnp.dot(data_ref[...], noise, preferred_element_type=jnp.float32)
    data_sq = jnp.zeros((BATCH, LANES), jnp.float32)
    for start in range(0, ent, LANES):
        wide = data_ref[:, start : start + LANES].astype(jnp.float32)
        data_sq = data_sq + wide * wide
    data_sq = jnp.sum(data_sq, axis=1, keepdims=True)
    parts = data_sq - 2.0 * gram
    for tile, rows, half in tiles():
        out_ref[tile] = parts[rows, half]


def sum_kernel(parts_ref, out_ref):
    total = jnp.sum(parts_ref[...], axis=0)
    total = total[:4] + total[4:]
    total = jnp.concatenate([total, total], axis=0)
    out_ref[...] = jnp.broadcast_to(total[None], out_ref.shape)


def sweep_kernel(
    cost_ref, data_ref, noise_ref, out_ref, pots_ref, noise_sq_ref,
    bias, kern, row_pot, col_pot, row_sum,
):
    for tile, rows, half in tiles():
        bias[rows, half] = cost_ref[tile] * (-1.0 / (LATENT * BIT))

    def log_sweep(scaled):
        top = jnp.max(scaled, axis=0, keepdims=True)
        row = -(top + jnp.log2(jnp.sum(jnp.exp2(scaled - top), axis=0, keepdims=True)))
        scaled = bias[...] + row
        top = jnp.max(scaled, axis=1, keepdims=True)
        scaled = jnp.exp2(scaled - top)
        total = jnp.sum(scaled, axis=1, keepdims=True)
        row_pot[...] = row
        col_pot[...] = -(top + jnp.log2(total))
        scaled = scaled * (1.0 / total)
        kern[...] = scaled
        return jnp.sum(scaled, axis=0, keepdims=True)

    total = log_sweep(bias[...])

    tile = (8, LANES)
    blocks = [pl.ds(start, 8) for start in range(0, BATCH, 8)]
    halves = [pl.ds(start, LANES) for start in range(0, BATCH, LANES)]

    def over_columns(low, high, rows, use):
        sums = [[jnp.zeros(tile, jnp.float32) for _ in halves] for _ in range(2)]
        for n, block in enumerate(blocks):
            parts = [kern[block, half] for half in halves]
            total = sum(part * row for part, row in zip(parts, rows))
            total = jnp.broadcast_to(jnp.sum(total, axis=1, keepdims=True), tile)
            low, high = jnp.minimum(low, total), jnp.maximum(high, total)
            factor = 1.0 / total
            parts = [part * factor for part in parts]
            if use is not None:
                use(block, factor, parts)
            for h, part in enumerate(parts):
                sums[n % 2][h] += part
        totals = []
        for first, second in zip(*sums):
            total = jnp.broadcast_to(jnp.sum(first + second, axis=0, keepdims=True), tile)
            low = jnp.minimum(low, total)
            totals.append(total)
        return low, high, totals

    units = noise_ref.shape[1] // UNIT
    share = units // (SWEEPS - 2)

    def squares(first, count, total):
        for n in range(count):
            start = pl.multiple_of((first + n) * UNIT, LANES)
            unit = noise_ref[:, pl.ds(start, UNIT)].astype(jnp.float32)
            total = total + unit * unit
        return total

    def sweep(step, carry):
        low, high, rows, noise_sq = carry
        low, high, totals = over_columns(low, high, rows, None)
        for total in totals:
            high = jnp.maximum(high, total)
        noise_sq = squares((step - 2) * share, share, noise_sq)
        return (low, high, tuple(1.0 / total for total in totals), noise_sq)

    def finish(block, factor, parts):
        col_pot[block, :] += jnp.log2(factor[:, :1])
        for half, part in zip(halves, parts):
            kern[block, half] = part

    totals = [jnp.broadcast_to(total[:, half.start : half.start + LANES], tile) for half in halves]
    low, high = jnp.minimum(*totals), jnp.maximum(*totals)
    noise_sq = jnp.zeros((noise_ref.shape[0], UNIT), jnp.float32)
    carry = (low, high, tuple(1.0 / total for total in totals), noise_sq)
    low, high, rows, noise_sq = lax.fori_loop(2, SWEEPS, sweep, carry)
    done = (SWEEPS - 2) * share
    noise_sq = jnp.sum(squares(done, units - done, noise_sq), axis=1, keepdims=True)
    noise_sq_ref[...] = jnp.broadcast_to(noise_sq, noise_sq_ref.shape)
    low, high, totals = over_columns(low, high, rows, finish)
    row_pot[...] += jnp.log2(jnp.concatenate([row[:1] for row in rows], axis=1))
    row_sum[...] = jnp.concatenate([total[:1] for total in totals], axis=1)
    near = jnp.min(jnp.where((low >= 1.0 / DRIFT) & (high <= DRIFT), 1.0, 0.0)) > 0.5

    def targets():
        weights = (kern[...] * (1.0 / row_sum[...])).astype(jnp.bfloat16)
        moved = lax.dot_general(
            weights, data_ref[...], (((0,), (0,)), ((), ())), preferred_element_type=jnp.float32
        )
        out_ref[...] = moved.astype(jnp.bfloat16).reshape(out_ref.shape)

    targets()

    @pl.when(jnp.logical_not(near))
    def _():
        col_pot[...] = jnp.zeros_like(col_pot)

        def again(step, carry):
            log_sweep(bias[...] + col_pot[...])
            return carry

        lax.fori_loop(0, SWEEPS, again, 0)
        scaled = bias[...] + col_pot[...]
        scaled = jnp.exp2(scaled - jnp.max(scaled, axis=0, keepdims=True))
        kern[...] = scaled
        row_sum[...] = jnp.sum(scaled, axis=0, keepdims=True)
        targets()

    pots_ref[0:1, :] = row_pot[...] * BIT
    pots_ref[1:2, :] = jnp.transpose(col_pot[...] * BIT)


def on_device(noise, data):
    devices = lax.axis_size(AXES)
    own = noise.shape[0]
    ent = UNITS * UNIT
    units = LATENT // UNIT
    params = pltpu.CompilerParams(vmem_limit_bytes=VMEM)
    anywhere = pl.BlockSpec(memory_space=pl.ANY)

    def units_of(rows):
        return rows.reshape(own, units, UNIT).transpose(1, 0, 2)

    both = pl.pallas_call(
        pack_kernel,
        out_shape=jax.ShapeDtypeStruct((devices, 2 * UNITS, own, UNIT), noise.dtype),
        in_specs=[pl.BlockSpec(memory_space=pltpu.HBM)] * 2,
        out_specs=anywhere,
        scratch_shapes=[
            pltpu.VMEM((UNITS * devices - units, own, UNIT), noise.dtype),
            pltpu.SemaphoreType.DMA((4 * UNITS,)),
        ],
        compiler_params=params,
    )(*[pltpu.with_memory_space_constraint(units_of(rows), pltpu.HBM) for rows in (noise, data)])
    both = both.transpose(0, 2, 1, 3).reshape(devices, own, 2 * ent)
    both = lax.all_to_all(both, AXES, split_axis=0, concat_axis=0)

    whole = jax.ShapeDtypeStruct((devices // 2, 8, LANES), jnp.float32)

    def exchange(parts):
        parts = parts.reshape(devices, 4, LANES)
        return lax.all_to_all(parts, AXES, split_axis=0, concat_axis=0).reshape(whole.shape)

    parts, data_ent = pl.pallas_call(
        gram_kernel,
        out_shape=(whole, jax.ShapeDtypeStruct((BATCH, ent), data.dtype)),
        compiler_params=params,
    )(both)
    total = pl.pallas_call(sum_kernel, out_shape=whole, compiler_params=params)(exchange(parts))
    total = exchange(total)

    moved, pots, noise_sq = pl.pallas_call(
        sweep_kernel,
        out_shape=(
            jax.ShapeDtypeStruct((devices, own, ent), jnp.bfloat16),
            jax.ShapeDtypeStruct((2, BATCH), jnp.float32),
            jax.ShapeDtypeStruct((own, LANES), jnp.float32),
        ),
        scratch_shapes=[
            pltpu.VMEM((BATCH, BATCH), jnp.float32),
            pltpu.VMEM((BATCH, BATCH), jnp.float32),
            pltpu.VMEM((1, BATCH), jnp.float32),
            pltpu.VMEM((BATCH, 1), jnp.float32),
            pltpu.VMEM((1, BATCH), jnp.float32),
        ],
        compiler_params=params,
    )(total, data_ent, noise)
    moved = lax.all_to_all(moved, AXES, split_axis=0, concat_axis=0)
    moved = moved.reshape(devices, own, UNITS, UNIT).transpose(0, 2, 1, 3)
    in_vmem = pl.BlockSpec(memory_space=pltpu.VMEM)
    targets, row, col = pl.pallas_call(
        unpack_kernel,
        out_shape=(
            jax.ShapeDtypeStruct((units, own, UNIT), moved.dtype),
            jax.ShapeDtypeStruct((own,), jnp.float32),
            jax.ShapeDtypeStruct((own,), jnp.float32),
        ),
        in_specs=[anywhere, in_vmem, in_vmem],
        out_specs=(anywhere, anywhere, anywhere),
        scratch_shapes=[
            pltpu.SMEM((own,), jnp.float32),
            pltpu.SMEM((own,), jnp.float32),
            pltpu.SemaphoreType.DMA((UNITS + 2,)),
        ],
        compiler_params=params,
    )(moved, pots, noise_sq)
    return (targets.transpose(1, 0, 2).reshape(own, LATENT), row, col)


def solution(mesh):
    return jax.shard_map(
        on_device,
        mesh=mesh,
        in_specs=(P(AXES, None), P(AXES, None)),
        out_specs=(P(AXES, None), P(AXES), P(AXES)),
        check_vma=False,
    )
```

```python
import math

import jax
import jax.numpy as jnp
from jax import lax
from jax.experimental import pallas as pl
from jax.experimental.pallas import tpu as pltpu
from jax.sharding import PartitionSpec as P

SWEEPS = 20
LATENT = 324480
BATCH = 256
AXES = ("dp", "dim")
LANES = 128
TEMPER = 0.25 / math.sqrt(LATENT)
BIT = TEMPER * math.log(2.0)
DRIFT = 2.0**40
VMEM = 24 * 1024 * 1024
UNITS = 4
UNIT = 640


def pack_kernel(noise_ref, data_ref, out_ref, zeros, sems):
    devices, units = out_ref.shape[0], noise_ref.shape[0]
    zeros[...] = jnp.zeros_like(zeros)
    copies = []
    for kind, ref in enumerate((noise_ref, data_ref)):
        for q in range(UNITS):
            slot = kind * UNITS + q
            start = q * devices
            count = min(devices, units - start)
            copies.append((ref.at[pl.ds(start, count)], out_ref.at[pl.ds(0, count), slot]))
            if count < devices:
                copies.append((zeros, out_ref.at[pl.ds(count, devices - count), slot]))
    copies = [pltpu.make_async_copy(src, dst, sems.at[n]) for n, (src, dst) in enumerate(copies)]
    for copy in copies:
        copy.start()
    for copy in copies:
        copy.wait()


def unpack_kernel(moved_ref, pots_ref, noise_sq_ref, out_ref, row_ref, col_ref, row, col, sems):
    devices, units = moved_ref.shape[0], out_ref.shape[0]
    own = out_ref.shape[1]
    copies = []
    for q in range(UNITS):
        start = q * devices
        count = min(devices, units - start)
        copies.append((moved_ref.at[pl.ds(0, count), q], out_ref.at[pl.ds(start, count)]))
    copies.extend([(row, row_ref), (col, col_ref)])
    copies = [pltpu.make_async_copy(src, dst, sems.at[n]) for n, (src, dst) in enumerate(copies)]
    for copy in copies[:UNITS]:
        copy.start()

    first = (lax.axis_index("dp") * lax.axis_size("dim") + lax.axis_index("dim")) * own
    lane = lax.broadcasted_iota(jnp.int32, (1, BATCH), 1)
    for n in range(own):
        mine = lane == first + n
        row_pot = jnp.sum(jnp.where(mine, pots_ref[0:1, :], 0.0))
        row[n] = row_pot + jnp.max(noise_sq_ref[n : n + 1, :]) / LATENT
        col[n] = jnp.sum(jnp.where(mine, pots_ref[1:2, :], 0.0))
    for copy in copies[UNITS:]:
        copy.start()
    for copy in copies:
        copy.wait()


def tiles(rows):
    for tile in range(rows * BATCH // (8 * LANES)):
        row, half = 8 * (tile // 2), LANES * (tile % 2)
        yield tile, slice(row, row + 8), slice(half, half + LANES)


def core():
    return lax.rem(lax.axis_index("dim"), 2)


def half_of(both_ref, noise, part, data, out_ref):
    rows, ent = data.shape
    data[...] = both_ref[:, part, :, ent:].reshape(rows, ent)
    gram = jnp.dot(data[...], noise, preferred_element_type=jnp.float32)
    data_sq = jnp.zeros((rows, LANES), jnp.float32)
    for start in range(0, ent, LANES):
        wide = data[:, start : start + LANES].astype(jnp.float32)
        data_sq = data_sq + wide * wide
    data_sq = jnp.sum(data_sq, axis=1, keepdims=True)
    parts = data_sq - 2.0 * gram
    for tile, span, half in tiles(rows):
        out_ref[tile] = parts[span, half]


def sent_kernel(both_ref, out_ref, noise_ref, data):
    ent = noise_ref.shape[0]
    noise_ref[...] = jnp.transpose(both_ref[:, :, :, :ent].reshape(BATCH, ent))
    half_of(both_ref, noise_ref[...], 1 - core(), data, out_ref)


def kept_kernel(both_ref, noise_ref, out_ref, data_ref, data):
    half_of(both_ref, noise_ref[...], core(), data, out_ref)
    data_ref[...] = both_ref[:, :, :, data_ref.shape[1] :].reshape(data_ref.shape)


def add_kernel(first_ref, second_ref, out_ref):
    out_ref[...] = first_ref[...] + second_ref[...]


def sum_kernel(parts_ref, out_ref):
    total = jnp.sum(parts_ref[...], axis=0)
    total = total[:4] + total[4:]
    total = jnp.concatenate([total, total], axis=0)
    out_ref[...] = jnp.broadcast_to(total[None], out_ref.shape)


def sweep_kernel(
    cost_ref, data_ref, noise_ref, out_ref, pots_ref, noise_sq_ref,
    bias, kern, row_pot, col_pot, row_sum,
):
    for tile, rows, half in tiles(BATCH):
        block, side = tile // 2, tile % 2
        place = 4 * (block // 2) + 2 * side + block % 2
        bias[rows, half] = cost_ref[place] * (-1.0 / (LATENT * BIT))

    def log_sweep(scaled):
        top = jnp.max(scaled, axis=0, keepdims=True)
        row = -(top + jnp.log2(jnp.sum(jnp.exp2(scaled - top), axis=0, keepdims=True)))
        scaled = bias[...] + row
        top = jnp.max(scaled, axis=1, keepdims=True)
        scaled = jnp.exp2(scaled - top)
        total = jnp.sum(scaled, axis=1, keepdims=True)
        row_pot[...] = row
        col_pot[...] = -(top + jnp.log2(total))
        scaled = scaled * (1.0 / total)
        kern[...] = scaled
        return jnp.sum(scaled, axis=0, keepdims=True)

    total = log_sweep(bias[...])

    tile = (8, LANES)
    blocks = [pl.ds(start, 8) for start in range(0, BATCH, 8)]
    halves = [pl.ds(start, LANES) for start in range(0, BATCH, LANES)]

    def over_columns(low, high, rows, use):
        sums = [[jnp.zeros(tile, jnp.float32) for _ in halves] for _ in range(2)]
        for n, block in enumerate(blocks):
            parts = [kern[block, half] for half in halves]
            total = sum(part * row for part, row in zip(parts, rows))
            total = jnp.broadcast_to(jnp.sum(total, axis=1, keepdims=True), tile)
            low, high = jnp.minimum(low, total), jnp.maximum(high, total)
            factor = 1.0 / total
            parts = [part * factor for part in parts]
            if use is not None:
                use(block, factor, parts)
            for h, part in enumerate(parts):
                sums[n % 2][h] += part
        totals = []
        for first, second in zip(*sums):
            total = jnp.broadcast_to(jnp.sum(first + second, axis=0, keepdims=True), tile)
            low = jnp.minimum(low, total)
            totals.append(total)
        return low, high, totals

    units = noise_ref.shape[1] // UNIT
    share = units // (SWEEPS - 2)

    def squares(first, count, total):
        for n in range(count):
            start = pl.multiple_of((first + n) * UNIT, LANES)
            unit = noise_ref[:, pl.ds(start, UNIT)].astype(jnp.float32)
            total = total + unit * unit
        return total

    def sweep(step, carry):
        low, high, rows, noise_sq = carry
        low, high, totals = over_columns(low, high, rows, None)
        for total in totals:
            high = jnp.maximum(high, total)
        noise_sq = squares((step - 2) * share, share, noise_sq)
        return (low, high, tuple(1.0 / total for total in totals), noise_sq)

    def finish(block, factor, parts):
        col_pot[block, :] += jnp.log2(factor[:, :1])
        for half, part in zip(halves, parts):
            kern[block, half] = part

    totals = [jnp.broadcast_to(total[:, half.start : half.start + LANES], tile) for half in halves]
    low, high = jnp.minimum(*totals), jnp.maximum(*totals)
    noise_sq = jnp.zeros((noise_ref.shape[0], UNIT), jnp.float32)
    carry = (low, high, tuple(1.0 / total for total in totals), noise_sq)
    low, high, rows, noise_sq = lax.fori_loop(2, SWEEPS, sweep, carry)
    done = (SWEEPS - 2) * share
    noise_sq = jnp.sum(squares(done, units - done, noise_sq), axis=1, keepdims=True)
    noise_sq_ref[...] = jnp.broadcast_to(noise_sq, noise_sq_ref.shape)
    low, high, totals = over_columns(low, high, rows, finish)
    row_pot[...] += jnp.log2(jnp.concatenate([row[:1] for row in rows], axis=1))
    row_sum[...] = jnp.concatenate([total[:1] for total in totals], axis=1)
    near = jnp.min(jnp.where((low >= 1.0 / DRIFT) & (high <= DRIFT), 1.0, 0.0)) > 0.5

    def targets():
        weights = (kern[...] * (1.0 / row_sum[...])).astype(jnp.bfloat16)
        moved = lax.dot_general(
            weights, data_ref[...], (((0,), (0,)), ((), ())), preferred_element_type=jnp.float32
        )
        out_ref[...] = moved.astype(jnp.bfloat16).reshape(out_ref.shape)

    targets()

    @pl.when(jnp.logical_not(near))
    def _():
        col_pot[...] = jnp.zeros_like(col_pot)

        def again(step, carry):
            log_sweep(bias[...] + col_pot[...])
            return carry

        lax.fori_loop(0, SWEEPS, again, 0)
        scaled = bias[...] + col_pot[...]
        scaled = jnp.exp2(scaled - jnp.max(scaled, axis=0, keepdims=True))
        kern[...] = scaled
        row_sum[...] = jnp.sum(scaled, axis=0, keepdims=True)
        targets()

    pots_ref[0:1, :] = row_pot[...] * BIT
    pots_ref[1:2, :] = jnp.transpose(col_pot[...] * BIT)


def on_device(noise, data):
    devices = lax.axis_size(AXES)
    own = noise.shape[0]
    ent = UNITS * UNIT
    units = LATENT // UNIT
    params = pltpu.CompilerParams(vmem_limit_bytes=VMEM)
    anywhere = pl.BlockSpec(memory_space=pl.ANY)

    def units_of(rows):
        return rows.reshape(own, units, UNIT).transpose(1, 0, 2)

    both = pl.pallas_call(
        pack_kernel,
        out_shape=jax.ShapeDtypeStruct((devices, 2 * UNITS, own, UNIT), noise.dtype),
        in_specs=[pl.BlockSpec(memory_space=pltpu.HBM)] * 2,
        out_specs=anywhere,
        scratch_shapes=[
            pltpu.VMEM((UNITS * devices - units, own, UNIT), noise.dtype),
            pltpu.SemaphoreType.DMA((4 * UNITS,)),
        ],
        compiler_params=params,
    )(*[pltpu.with_memory_space_constraint(units_of(rows), pltpu.HBM) for rows in (noise, data)])
    both = both.transpose(0, 2, 1, 3).reshape(devices, own, 2 * ent)
    both = lax.all_to_all(both, AXES, split_axis=0, concat_axis=0)

    part = jax.ShapeDtypeStruct((devices // 4, 8, LANES), jnp.float32)
    whole = jax.ShapeDtypeStruct((devices // 2, 8, LANES), jnp.float32)
    data_whole = jax.ShapeDtypeStruct((BATCH, ent), data.dtype)
    noise_whole = jax.ShapeDtypeStruct((ent, BATCH), noise.dtype)
    data_half = pltpu.VMEM((BATCH // 2, ent), data.dtype)

    def exchange(parts):
        shape = parts.shape
        parts = parts.reshape(devices, -1, LANES)
        return lax.all_to_all(parts, AXES, split_axis=0, concat_axis=0).reshape(shape)

    both = both.reshape(devices // 2, 2, own, 2 * ent)
    sent, noise_ent = pl.pallas_call(
        sent_kernel, out_shape=(part, noise_whole), scratch_shapes=[data_half], compiler_params=params
    )(both)
    got = lax.ppermute(sent, "dim", [(k, k ^ 1) for k in range(lax.axis_size("dim"))])
    kept, data_ent = pl.pallas_call(
        kept_kernel,
        out_shape=(part, data_whole),
        scratch_shapes=[data_half],
        compiler_params=params,
        cost_estimate=pl.CostEstimate(
            flops=BATCH * BATCH * ent, bytes_accessed=6 * BATCH * ent, transcendentals=0
        ),
    )(both, noise_ent)
    parts = pl.pallas_call(add_kernel, out_shape=part, compiler_params=params)(kept, got)
    total = pl.pallas_call(sum_kernel, out_shape=whole, compiler_params=params)(exchange(parts))
    total = exchange(total)

    moved, pots, noise_sq = pl.pallas_call(
        sweep_kernel,
        out_shape=(
            jax.ShapeDtypeStruct((devices, own, ent), jnp.bfloat16),
            jax.ShapeDtypeStruct((2, BATCH), jnp.float32),
            jax.ShapeDtypeStruct((own, LANES), jnp.float32),
        ),
        scratch_shapes=[
            pltpu.VMEM((BATCH, BATCH), jnp.float32),
            pltpu.VMEM((BATCH, BATCH), jnp.float32),
            pltpu.VMEM((1, BATCH), jnp.float32),
            pltpu.VMEM((BATCH, 1), jnp.float32),
            pltpu.VMEM((1, BATCH), jnp.float32),
        ],
        compiler_params=params,
    )(total, data_ent, noise)
    moved = lax.all_to_all(moved, AXES, split_axis=0, concat_axis=0)
    moved = moved.reshape(devices, own, UNITS, UNIT).transpose(0, 2, 1, 3)
    in_vmem = pl.BlockSpec(memory_space=pltpu.VMEM)
    targets, row, col = pl.pallas_call(
        unpack_kernel,
        out_shape=(
            jax.ShapeDtypeStruct((units, own, UNIT), moved.dtype),
            jax.ShapeDtypeStruct((own,), jnp.float32),
            jax.ShapeDtypeStruct((own,), jnp.float32),
        ),
        in_specs=[anywhere, in_vmem, in_vmem],
        out_specs=(anywhere, anywhere, anywhere),
        scratch_shapes=[
            pltpu.SMEM((own,), jnp.float32),
            pltpu.SMEM((own,), jnp.float32),
            pltpu.SemaphoreType.DMA((UNITS + 2,)),
        ],
        compiler_params=params,
    )(moved, pots, noise_sq)
    return (targets.transpose(1, 0, 2).reshape(own, LATENT), row, col)


def solution(mesh):
    return jax.shard_map(
        on_device,
        mesh=mesh,
        in_specs=(P(AXES, None), P(AXES, None)),
        out_specs=(P(AXES, None), P(AXES), P(AXES)),
        check_vma=False,
    )
```

```python
import math

import jax
import jax.numpy as jnp
from jax import lax
from jax.experimental import pallas as pl
from jax.experimental.pallas import tpu as pltpu
from jax.sharding import PartitionSpec as P

SWEEPS = 20
LATENT = 324480
BATCH = 256
AXES = ("dp", "dim")
LANES = 128
TEMPER = 0.25 / math.sqrt(LATENT)
BIT = TEMPER * math.log(2.0)
DRIFT = 2.0**40
VMEM = 24 * 1024 * 1024
UNITS = 4
UNIT = 640


def pack_kernel(noise_ref, data_ref, out_ref, zeros, sems):
    devices, units = out_ref.shape[0], noise_ref.shape[0]
    zeros[...] = jnp.zeros_like(zeros)
    copies = []
    for kind, ref in enumerate((noise_ref, data_ref)):
        for q in range(UNITS):
            slot = kind * UNITS + q
            start = q * devices
            count = min(devices, units - start)
            copies.append((ref.at[pl.ds(start, count)], out_ref.at[pl.ds(0, count), slot]))
            if count < devices:
                copies.append((zeros, out_ref.at[pl.ds(count, devices - count), slot]))
    copies = [pltpu.make_async_copy(src, dst, sems.at[n]) for n, (src, dst) in enumerate(copies)]
    for copy in copies:
        copy.start()
    for copy in copies:
        copy.wait()


def unpack_kernel(
    moved_ref, row_pot_ref, row_fac_ref, col_pot_ref, col_fac_ref, noise_sq_ref,
    out_ref, row_ref, col_ref, row, col, sems,
):
    devices, units = moved_ref.shape[0], out_ref.shape[0]
    own = out_ref.shape[1]
    copies = []
    for q in range(UNITS):
        start = q * devices
        count = min(devices, units - start)
        copies.append((moved_ref.at[pl.ds(0, count), q], out_ref.at[pl.ds(start, count)]))
    copies.extend([(row, row_ref), (col, col_ref)])
    copies = [pltpu.make_async_copy(src, dst, sems.at[n]) for n, (src, dst) in enumerate(copies)]
    for copy in copies[:UNITS]:
        copy.start()

    first = (lax.axis_index("dp") * lax.axis_size("dim") + lax.axis_index("dim")) * own
    row_pot = (row_pot_ref[...] + jnp.log2(row_fac_ref[...])) * BIT
    col_pot = (col_pot_ref[...] + jnp.log2(col_fac_ref[...])) * BIT
    lane = lax.broadcasted_iota(jnp.int32, row_pot.shape, 1)
    sublane = lax.broadcasted_iota(jnp.int32, col_pot.shape, 0)
    for n in range(own):
        mine = jnp.sum(jnp.where(lane == first + n, row_pot, 0.0))
        row[n] = mine + jnp.max(noise_sq_ref[n : n + 1, :]) / LATENT
        col[n] = jnp.sum(jnp.where(sublane == first + n, col_pot, 0.0))
    for copy in copies[UNITS:]:
        copy.start()
    for copy in copies:
        copy.wait()


def tiles():
    for tile in range(BATCH * BATCH // (8 * LANES)):
        row, half = 8 * (tile // 2), LANES * (tile % 2)
        yield tile, slice(row, row + 8), slice(half, half + LANES)


def gram_kernel(both_ref, out_ref, data_ref):
    ent = data_ref.shape[1]
    noise = jnp.transpose(both_ref[:, :, :ent].reshape(data_ref.shape))
    data_ref[...] = both_ref[:, :, ent:].reshape(data_ref.shape)
    gram = jnp.dot(data_ref[...], noise, preferred_element_type=jnp.float32)
    data_sq = jnp.zeros((BATCH, LANES), jnp.float32)
    for start in range(0, ent, LANES):
        wide = data_ref[:, start : start + LANES].astype(jnp.float32)
        data_sq = data_sq + wide * wide
    data_sq = jnp.sum(data_sq, axis=1, keepdims=True)
    parts = data_sq - 2.0 * gram
    for tile, rows, half in tiles():
        out_ref[tile] = parts[rows, half]


def sum_kernel(parts_ref, out_ref):
    total = jnp.sum(parts_ref[...], axis=0)
    total = total[:4] + total[4:]
    total = jnp.concatenate([total, total], axis=0)
    out_ref[...] = jnp.broadcast_to(total[None], out_ref.shape)


def sweep_kernel(
    cost_ref, data_ref, noise_ref, out_ref, row_pot, row_fac, col_pot, col_fac, noise_sq_ref,
    bias, kern, row_sum,
):
    for tile, rows, half in tiles():
        bias[rows, half] = cost_ref[tile] * (-1.0 / (LATENT * BIT))

    def log_sweep(scaled):
        top = jnp.max(scaled, axis=0, keepdims=True)
        row = -(top + jnp.log2(jnp.sum(jnp.exp2(scaled - top), axis=0, keepdims=True)))
        scaled = bias[...] + row
        top = jnp.max(scaled, axis=1, keepdims=True)
        scaled = jnp.exp2(scaled - top)
        total = jnp.sum(scaled, axis=1, keepdims=True)
        row_pot[...] = row
        col_pot[...] = -(top + jnp.log2(total))
        scaled = scaled * (1.0 / total)
        kern[...] = scaled
        return jnp.sum(scaled, axis=0, keepdims=True)

    total = log_sweep(bias[...])

    tile = (8, LANES)
    blocks = [pl.ds(start, 8) for start in range(0, BATCH, 8)]
    halves = [pl.ds(start, LANES) for start in range(0, BATCH, LANES)]

    def over_columns(low, high, rows, use):
        sums = [[jnp.zeros(tile, jnp.float32) for _ in halves] for _ in range(2)]
        for n, block in enumerate(blocks):
            parts = [kern[block, half] for half in halves]
            total = sum(part * row for part, row in zip(parts, rows))
            total = jnp.broadcast_to(jnp.sum(total, axis=1, keepdims=True), tile)
            low, high = jnp.minimum(low, total), jnp.maximum(high, total)
            factor = 1.0 / total
            parts = [part * factor for part in parts]
            if use is not None:
                use(block, factor, parts)
            for h, part in enumerate(parts):
                sums[n % 2][h] += part
        totals = []
        for first, second in zip(*sums):
            total = jnp.broadcast_to(jnp.sum(first + second, axis=0, keepdims=True), tile)
            low = jnp.minimum(low, total)
            totals.append(total)
        return low, high, totals

    units = noise_ref.shape[1] // UNIT
    share = units // (SWEEPS - 2)

    def squares(first, count, total):
        for n in range(count):
            start = pl.multiple_of((first + n) * UNIT, LANES)
            unit = noise_ref[:, pl.ds(start, UNIT)].astype(jnp.float32)
            total = total + unit * unit
        return total

    def sweep(step, carry):
        low, high, rows, noise_sq = carry
        low, high, totals = over_columns(low, high, rows, None)
        for total in totals:
            high = jnp.maximum(high, total)
        noise_sq = squares((step - 2) * share, share, noise_sq)
        return (low, high, tuple(1.0 / total for total in totals), noise_sq)

    def finish(block, factor, parts):
        col_fac[block, :] = factor[:, :1]
        for half, part in zip(halves, parts):
            kern[block, half] = part

    totals = [jnp.broadcast_to(total[:, half.start : half.start + LANES], tile) for half in halves]
    low, high = jnp.minimum(*totals), jnp.maximum(*totals)
    noise_sq = jnp.zeros((noise_ref.shape[0], UNIT), jnp.float32)
    carry = (low, high, tuple(1.0 / total for total in totals), noise_sq)
    low, high, rows, noise_sq = lax.fori_loop(2, SWEEPS, sweep, carry)
    done = (SWEEPS - 2) * share
    noise_sq = jnp.sum(squares(done, units - done, noise_sq), axis=1, keepdims=True)
    noise_sq_ref[...] = jnp.broadcast_to(noise_sq, noise_sq_ref.shape)
    low, high, totals = over_columns(low, high, rows, finish)
    row_fac[...] = jnp.concatenate([row[:1] for row in rows], axis=1)
    row_sum[...] = jnp.concatenate([total[:1] for total in totals], axis=1)
    near = jnp.min(jnp.where((low >= 1.0 / DRIFT) & (high <= DRIFT), 1.0, 0.0)) > 0.5

    def targets():
        weights = (kern[...] * (1.0 / row_sum[...])).astype(jnp.bfloat16)
        moved = lax.dot_general(
            weights, data_ref[...], (((0,), (0,)), ((), ())), preferred_element_type=jnp.float32
        )
        out_ref[...] = moved.astype(jnp.bfloat16).reshape(out_ref.shape)

    targets()

    @pl.when(jnp.logical_not(near))
    def _():
        col_pot[...] = jnp.zeros_like(col_pot)

        def again(step, carry):
            log_sweep(bias[...] + col_pot[...])
            return carry

        lax.fori_loop(0, SWEEPS, again, 0)
        row_fac[...] = jnp.ones_like(row_fac)
        col_fac[...] = jnp.ones_like(col_fac)
        scaled = bias[...] + col_pot[...]
        scaled = jnp.exp2(scaled - jnp.max(scaled, axis=0, keepdims=True))
        kern[...] = scaled
        row_sum[...] = jnp.sum(scaled, axis=0, keepdims=True)
        targets()


def on_device(noise, data):
    devices = lax.axis_size(AXES)
    own = noise.shape[0]
    ent = UNITS * UNIT
    units = LATENT // UNIT
    params = pltpu.CompilerParams(vmem_limit_bytes=VMEM)
    anywhere = pl.BlockSpec(memory_space=pl.ANY)

    def units_of(rows):
        return rows.reshape(own, units, UNIT).transpose(1, 0, 2)

    both = pl.pallas_call(
        pack_kernel,
        out_shape=jax.ShapeDtypeStruct((devices, 2 * UNITS, own, UNIT), noise.dtype),
        in_specs=[pl.BlockSpec(memory_space=pltpu.HBM)] * 2,
        out_specs=anywhere,
        scratch_shapes=[
            pltpu.VMEM((UNITS * devices - units, own, UNIT), noise.dtype),
            pltpu.SemaphoreType.DMA((4 * UNITS,)),
        ],
        compiler_params=params,
    )(*[pltpu.with_memory_space_constraint(units_of(rows), pltpu.HBM) for rows in (noise, data)])
    both = both.transpose(0, 2, 1, 3).reshape(devices, own, 2 * ent)
    both = lax.all_to_all(both, AXES, split_axis=0, concat_axis=0)

    whole = jax.ShapeDtypeStruct((devices // 2, 8, LANES), jnp.float32)

    def exchange(parts):
        parts = parts.reshape(devices, 4, LANES)
        return lax.all_to_all(parts, AXES, split_axis=0, concat_axis=0).reshape(whole.shape)

    parts, data_ent = pl.pallas_call(
        gram_kernel,
        out_shape=(whole, jax.ShapeDtypeStruct((BATCH, ent), data.dtype)),
        compiler_params=params,
    )(both)
    total = pl.pallas_call(sum_kernel, out_shape=whole, compiler_params=params)(exchange(parts))
    total = exchange(total)

    along_lanes = jax.ShapeDtypeStruct((1, BATCH), jnp.float32)
    along_sublanes = jax.ShapeDtypeStruct((BATCH, 1), jnp.float32)
    moved, *pots, noise_sq = pl.pallas_call(
        sweep_kernel,
        out_shape=(
            jax.ShapeDtypeStruct((devices, own, ent), jnp.bfloat16),
            along_lanes,
            along_lanes,
            along_sublanes,
            along_sublanes,
            jax.ShapeDtypeStruct((own, LANES), jnp.float32),
        ),
        scratch_shapes=[
            pltpu.VMEM((BATCH, BATCH), jnp.float32),
            pltpu.VMEM((BATCH, BATCH), jnp.float32),
            pltpu.VMEM((1, BATCH), jnp.float32),
        ],
        compiler_params=params,
    )(total, data_ent, noise)
    moved = lax.all_to_all(moved, AXES, split_axis=0, concat_axis=0)
    moved = moved.reshape(devices, own, UNITS, UNIT).transpose(0, 2, 1, 3)
    in_vmem = pl.BlockSpec(memory_space=pltpu.VMEM)
    targets, row, col = pl.pallas_call(
        unpack_kernel,
        out_shape=(
            jax.ShapeDtypeStruct((units, own, UNIT), moved.dtype),
            jax.ShapeDtypeStruct((own,), jnp.float32),
            jax.ShapeDtypeStruct((own,), jnp.float32),
        ),
        in_specs=[anywhere] + [in_vmem] * 5,
        out_specs=(anywhere, anywhere, anywhere),
        scratch_shapes=[
            pltpu.SMEM((own,), jnp.float32),
            pltpu.SMEM((own,), jnp.float32),
            pltpu.SemaphoreType.DMA((UNITS + 2,)),
        ],
        compiler_params=params,
    )(moved, *pots, noise_sq)
    return (targets.transpose(1, 0, 2).reshape(own, LATENT), row, col)


def solution(mesh):
    return jax.shard_map(
        on_device,
        mesh=mesh,
        in_specs=(P(AXES, None), P(AXES, None)),
        out_specs=(P(AXES, None), P(AXES), P(AXES)),
        check_vma=False,
    )
```

```python
import math

import jax
import jax.numpy as jnp
from jax import lax
from jax.experimental import pallas as pl
from jax.experimental.pallas import tpu as pltpu
from jax.sharding import PartitionSpec as P

SWEEPS = 20
LATENT = 324480
BATCH = 256
AXES = ("dp", "dim")
LANES = 128
TEMPER = 0.25 / math.sqrt(LATENT)
BIT = TEMPER * math.log(2.0)
DRIFT = 2.0**40
VMEM = 24 * 1024 * 1024
UNITS = 4
UNIT = 640


def pack_kernel(noise_ref, data_ref, out_ref, zeros, sems):
    devices, units = out_ref.shape[0], noise_ref.shape[0]
    zeros[...] = jnp.zeros_like(zeros)
    copies = []
    for kind, ref in enumerate((noise_ref, data_ref)):
        for q in range(UNITS):
            slot = kind * UNITS + q
            start = q * devices
            count = min(devices, units - start)
            copies.append((ref.at[pl.ds(start, count)], out_ref.at[pl.ds(0, count), slot]))
            if count < devices:
                copies.append((zeros, out_ref.at[pl.ds(count, devices - count), slot]))
    copies = [pltpu.make_async_copy(src, dst, sems.at[n]) for n, (src, dst) in enumerate(copies)]
    for copy in copies:
        copy.start()
    for copy in copies:
        copy.wait()


def unpack_kernel(
    moved_ref, row_pot_ref, row_fac_ref, col_pot_ref, col_fac_ref, noise_sq_ref,
    out_ref, row_ref, col_ref, row, col, sems,
):
    devices, units = moved_ref.shape[0], out_ref.shape[0]
    own = out_ref.shape[1]
    copies = []
    for q in range(UNITS):
        start = q * devices
        count = min(devices, units - start)
        copies.append((moved_ref.at[pl.ds(0, count), q], out_ref.at[pl.ds(start, count)]))
    copies.extend([(row, row_ref), (col, col_ref)])
    copies = [pltpu.make_async_copy(src, dst, sems.at[n]) for n, (src, dst) in enumerate(copies)]
    for copy in copies[:UNITS]:
        copy.start()

    first = (lax.axis_index("dp") * lax.axis_size("dim") + lax.axis_index("dim")) * own
    row_pot = (row_pot_ref[...] + jnp.log2(row_fac_ref[...])) * BIT
    col_pot = (col_pot_ref[...] + jnp.log2(col_fac_ref[...])) * BIT
    lane = lax.broadcasted_iota(jnp.int32, row_pot.shape, 1)
    sublane = lax.broadcasted_iota(jnp.int32, col_pot.shape, 0)
    for n in range(own):
        mine = jnp.sum(jnp.where(lane == first + n, row_pot, 0.0))
        row[n] = mine + jnp.sum(noise_sq_ref[n : n + 1, :]) / LATENT
        col[n] = jnp.sum(jnp.where(sublane == first + n, col_pot, 0.0))
    for copy in copies[UNITS:]:
        copy.start()
    for copy in copies:
        copy.wait()


def tiles():
    for tile in range(BATCH * BATCH // (8 * LANES)):
        row, half = 8 * (tile // 2), LANES * (tile % 2)
        yield tile, slice(row, row + 8), slice(half, half + LANES)


def gram_kernel(both_ref, out_ref, data_ref):
    ent = data_ref.shape[1]
    noise = jnp.transpose(both_ref[:, :, :ent].reshape(data_ref.shape))
    data_ref[...] = both_ref[:, :, ent:].reshape(data_ref.shape)
    gram = jnp.dot(data_ref[...], noise, preferred_element_type=jnp.float32)
    data_sq = jnp.zeros((BATCH, LANES), jnp.float32)
    for start in range(0, ent, LANES):
        wide = data_ref[:, start : start + LANES].astype(jnp.float32)
        data_sq = data_sq + wide * wide
    data_sq = jnp.sum(data_sq, axis=1, keepdims=True)
    parts = data_sq - 2.0 * gram
    for tile, rows, half in tiles():
        out_ref[tile] = parts[rows, half]


def sum_kernel(parts_ref, out_ref):
    total = jnp.sum(parts_ref[...], axis=0)
    total = total[:4] + total[4:]
    total = jnp.concatenate([total, total], axis=0)
    out_ref[...] = jnp.broadcast_to(total[None], out_ref.shape)


def sweep_kernel(
    cost_ref, data_ref, noise_ref, out_ref, row_pot, row_fac, col_pot, col_fac, noise_sq_ref,
    bias, kern, row_sum,
):
    for tile, rows, half in tiles():
        bias[rows, half] = cost_ref[tile] * (-1.0 / (LATENT * BIT))

    def log_sweep(scaled):
        top = jnp.max(scaled, axis=0, keepdims=True)
        row = -(top + jnp.log2(jnp.sum(jnp.exp2(scaled - top), axis=0, keepdims=True)))
        scaled = bias[...] + row
        top = jnp.max(scaled, axis=1, keepdims=True)
        scaled = jnp.exp2(scaled - top)
        total = jnp.sum(scaled, axis=1, keepdims=True)
        row_pot[...] = row
        col_pot[...] = -(top + jnp.log2(total))
        scaled = scaled * (1.0 / total)
        kern[...] = scaled
        return jnp.sum(scaled, axis=0, keepdims=True)

    total = log_sweep(bias[...])

    tile = (8, LANES)
    blocks = [pl.ds(start, 8) for start in range(0, BATCH, 8)]
    halves = [pl.ds(start, LANES) for start in range(0, BATCH, LANES)]

    def over_columns(low, high, rows, use):
        sums = [[jnp.zeros(tile, jnp.float32) for _ in halves] for _ in range(2)]
        for n, block in enumerate(blocks):
            parts = [kern[block, half] for half in halves]
            total = sum(part * row for part, row in zip(parts, rows))
            total = jnp.broadcast_to(jnp.sum(total, axis=1, keepdims=True), tile)
            low, high = jnp.minimum(low, total), jnp.maximum(high, total)
            factor = 1.0 / total
            parts = [part * factor for part in parts]
            if use is not None:
                use(block, factor, parts)
            for h, part in enumerate(parts):
                sums[n % 2][h] += part
        totals = []
        for first, second in zip(*sums):
            total = jnp.broadcast_to(jnp.sum(first + second, axis=0, keepdims=True), tile)
            low = jnp.minimum(low, total)
            totals.append(total)
        return low, high, totals

    units = noise_ref.shape[1] // UNIT
    share = units // (SWEEPS - 2)

    def squares(first, count, total):
        for n in range(count):
            start = pl.multiple_of((first + n) * UNIT, LANES)
            unit = noise_ref[:, pl.ds(start, UNIT)].astype(jnp.float32)
            total = total + unit * unit
        return total

    def sweep(step, carry):
        low, high, rows, noise_sq = carry
        low, high, totals = over_columns(low, high, rows, None)
        for total in totals:
            high = jnp.maximum(high, total)
        noise_sq = squares((step - 2) * share, share, noise_sq)
        return (low, high, tuple(1.0 / total for total in totals), noise_sq)

    def finish(block, factor, parts):
        col_fac[block, :] = factor[:, :1]
        for half, part in zip(halves, parts):
            kern[block, half] = part

    totals = [jnp.broadcast_to(total[:, half.start : half.start + LANES], tile) for half in halves]
    low, high = jnp.minimum(*totals), jnp.maximum(*totals)
    noise_sq = jnp.zeros((noise_ref.shape[0], UNIT), jnp.float32)
    carry = (low, high, tuple(1.0 / total for total in totals), noise_sq)
    low, high, rows, noise_sq = lax.fori_loop(2, SWEEPS, sweep, carry)
    done = (SWEEPS - 2) * share
    noise_sq_ref[...] = squares(done, units - done, noise_sq)
    low, high, totals = over_columns(low, high, rows, finish)
    row_fac[...] = jnp.concatenate([row[:1] for row in rows], axis=1)
    row_sum[...] = jnp.concatenate([total[:1] for total in totals], axis=1)
    near = jnp.min(jnp.where((low >= 1.0 / DRIFT) & (high <= DRIFT), 1.0, 0.0)) > 0.5

    def targets():
        weights = (kern[...] * (1.0 / row_sum[...])).astype(jnp.bfloat16)
        moved = lax.dot_general(
            weights, data_ref[...], (((0,), (0,)), ((), ())), preferred_element_type=jnp.float32
        )
        out_ref[...] = moved.astype(jnp.bfloat16).reshape(out_ref.shape)

    targets()

    @pl.when(jnp.logical_not(near))
    def _():
        col_pot[...] = jnp.zeros_like(col_pot)

        def again(step, carry):
            log_sweep(bias[...] + col_pot[...])
            return carry

        lax.fori_loop(0, SWEEPS, again, 0)
        row_fac[...] = jnp.ones_like(row_fac)
        col_fac[...] = jnp.ones_like(col_fac)
        scaled = bias[...] + col_pot[...]
        scaled = jnp.exp2(scaled - jnp.max(scaled, axis=0, keepdims=True))
        kern[...] = scaled
        row_sum[...] = jnp.sum(scaled, axis=0, keepdims=True)
        targets()


def on_device(noise, data):
    devices = lax.axis_size(AXES)
    own = noise.shape[0]
    ent = UNITS * UNIT
    units = LATENT // UNIT
    params = pltpu.CompilerParams(vmem_limit_bytes=VMEM)
    anywhere = pl.BlockSpec(memory_space=pl.ANY)

    def units_of(rows):
        return rows.reshape(own, units, UNIT).transpose(1, 0, 2)

    both = pl.pallas_call(
        pack_kernel,
        out_shape=jax.ShapeDtypeStruct((devices, 2 * UNITS, own, UNIT), noise.dtype),
        in_specs=[pl.BlockSpec(memory_space=pltpu.HBM)] * 2,
        out_specs=anywhere,
        scratch_shapes=[
            pltpu.VMEM((UNITS * devices - units, own, UNIT), noise.dtype),
            pltpu.SemaphoreType.DMA((4 * UNITS,)),
        ],
        compiler_params=params,
    )(*[pltpu.with_memory_space_constraint(units_of(rows), pltpu.HBM) for rows in (noise, data)])
    both = both.transpose(0, 2, 1, 3).reshape(devices, own, 2 * ent)
    both = lax.all_to_all(both, AXES, split_axis=0, concat_axis=0)

    whole = jax.ShapeDtypeStruct((devices // 2, 8, LANES), jnp.float32)

    def exchange(parts):
        parts = parts.reshape(devices, 4, LANES)
        return lax.all_to_all(parts, AXES, split_axis=0, concat_axis=0).reshape(whole.shape)

    parts, data_ent = pl.pallas_call(
        gram_kernel,
        out_shape=(whole, jax.ShapeDtypeStruct((BATCH, ent), data.dtype)),
        compiler_params=params,
    )(both)
    total = pl.pallas_call(sum_kernel, out_shape=whole, compiler_params=params)(exchange(parts))
    total = exchange(total)

    along_lanes = jax.ShapeDtypeStruct((1, BATCH), jnp.float32)
    along_sublanes = jax.ShapeDtypeStruct((BATCH, 1), jnp.float32)
    moved, *pots, noise_sq = pl.pallas_call(
        sweep_kernel,
        out_shape=(
            jax.ShapeDtypeStruct((devices, own, ent), jnp.bfloat16),
            along_lanes,
            along_lanes,
            along_sublanes,
            along_sublanes,
            jax.ShapeDtypeStruct((own, UNIT), jnp.float32),
        ),
        scratch_shapes=[
            pltpu.VMEM((BATCH, BATCH), jnp.float32),
            pltpu.VMEM((BATCH, BATCH), jnp.float32),
            pltpu.VMEM((1, BATCH), jnp.float32),
        ],
        compiler_params=params,
    )(total, data_ent, noise)
    moved = lax.all_to_all(moved, AXES, split_axis=0, concat_axis=0)
    moved = moved.reshape(devices, own, UNITS, UNIT).transpose(0, 2, 1, 3)
    in_vmem = pl.BlockSpec(memory_space=pltpu.VMEM)
    targets, row, col = pl.pallas_call(
        unpack_kernel,
        out_shape=(
            jax.ShapeDtypeStruct((units, own, UNIT), moved.dtype),
            jax.ShapeDtypeStruct((own,), jnp.float32),
            jax.ShapeDtypeStruct((own,), jnp.float32),
        ),
        in_specs=[anywhere] + [in_vmem] * 5,
        out_specs=(anywhere, anywhere, anywhere),
        scratch_shapes=[
            pltpu.SMEM((own,), jnp.float32),
            pltpu.SMEM((own,), jnp.float32),
            pltpu.SemaphoreType.DMA((UNITS + 2,)),
        ],
        compiler_params=params,
    )(moved, *pots, noise_sq)
    return (targets.transpose(1, 0, 2).reshape(own, LATENT), row, col)


def solution(mesh):
    return jax.shard_map(
        on_device,
        mesh=mesh,
        in_specs=(P(AXES, None), P(AXES, None)),
        out_specs=(P(AXES, None), P(AXES), P(AXES)),
        check_vma=False,
    )
```

```python
import math

import jax
import jax.numpy as jnp
from jax import lax
from jax.experimental import pallas as pl
from jax.experimental.pallas import tpu as pltpu
from jax.sharding import PartitionSpec as P

SWEEPS = 20
LATENT = 324480
BATCH = 256
AXES = ("dp", "dim")
LANES = 128
TEMPER = 0.25 / math.sqrt(LATENT)
BIT = TEMPER * math.log(2.0)
DRIFT = 2.0**40
VMEM = 24 * 1024 * 1024
UNITS = 4
UNIT = 640


def pack_kernel(noise_ref, data_ref, out_ref, zeros, sems):
    devices, units = out_ref.shape[0], noise_ref.shape[0]
    zeros[...] = jnp.zeros_like(zeros)
    copies = []
    for kind, ref in enumerate((noise_ref, data_ref)):
        for q in range(UNITS):
            slot = kind * UNITS + q
            start = q * devices
            count = min(devices, units - start)
            copies.append((ref.at[pl.ds(start, count)], out_ref.at[pl.ds(0, count), slot]))
            if count < devices:
                copies.append((zeros, out_ref.at[pl.ds(count, devices - count), slot]))
    copies = [pltpu.make_async_copy(src, dst, sems.at[n]) for n, (src, dst) in enumerate(copies)]
    for copy in copies:
        copy.start()
    for copy in copies:
        copy.wait()


def unpack_kernel(
    moved_ref, row_pot_ref, row_fac_ref, col_pot_ref, col_fac_ref, noise_sq_ref,
    out_ref, row_ref, col_ref, row, col, sems,
):
    devices, units = moved_ref.shape[0], out_ref.shape[0]
    own = out_ref.shape[1]
    copies = []
    for q in range(UNITS):
        start = q * devices
        count = min(devices, units - start)
        copies.append((moved_ref.at[pl.ds(0, count), q], out_ref.at[pl.ds(start, count)]))
    copies.extend([(row, row_ref), (col, col_ref)])
    copies = [pltpu.make_async_copy(src, dst, sems.at[n]) for n, (src, dst) in enumerate(copies)]
    for copy in copies[:UNITS]:
        copy.start()

    first = (lax.axis_index("dp") * lax.axis_size("dim") + lax.axis_index("dim")) * own
    row_pot = (row_pot_ref[...] + jnp.log2(row_fac_ref[...])) * BIT
    col_pot = (col_pot_ref[...] + jnp.log2(col_fac_ref[...])) * BIT
    lane = lax.broadcasted_iota(jnp.int32, row_pot.shape, 1)
    sublane = lax.broadcasted_iota(jnp.int32, col_pot.shape, 0)
    for n in range(own):
        mine = jnp.sum(jnp.where(lane == first + n, row_pot, 0.0))
        row[n] = mine + jnp.max(noise_sq_ref[n : n + 1, :]) / LATENT
        col[n] = jnp.sum(jnp.where(sublane == first + n, col_pot, 0.0))
    for copy in copies[UNITS:]:
        copy.start()
    for copy in copies:
        copy.wait()


def tiles():
    for tile in range(BATCH * BATCH // (8 * LANES)):
        row, half = 8 * (tile // 2), LANES * (tile % 2)
        yield tile, slice(row, row + 8), slice(half, half + LANES)


def gram_kernel(both_ref, out_ref, data_ref):
    ent = data_ref.shape[1]
    noise = jnp.transpose(both_ref[:, :, :ent].reshape(data_ref.shape))
    data_ref[...] = both_ref[:, :, ent:].reshape(data_ref.shape)
    gram = jnp.dot(data_ref[...], noise, preferred_element_type=jnp.float32)
    data_sq = jnp.zeros((BATCH, LANES), jnp.float32)
    for start in range(0, ent, LANES):
        wide = data_ref[:, start : start + LANES].astype(jnp.float32)
        data_sq = data_sq + wide * wide
    data_sq = jnp.sum(data_sq, axis=1, keepdims=True)
    parts = data_sq - 2.0 * gram
    for tile, rows, half in tiles():
        out_ref[tile] = parts[rows, half]


def sum_kernel(parts_ref, out_ref):
    total = jnp.sum(parts_ref[...], axis=0)
    total = total[:4] + total[4:]
    total = jnp.concatenate([total, total], axis=0)
    out_ref[...] = jnp.broadcast_to(total[None], out_ref.shape)


def sweep_kernel(
    cost_ref, data_ref, noise_ref, out_ref, row_pot, row_fac, col_pot, col_fac, noise_sq_ref,
    bias, kern, row_sum,
):
    for tile, rows, half in tiles():
        bias[rows, half] = cost_ref[tile] * (-1.0 / (LATENT * BIT))

    def log_sweep(scaled):
        top = jnp.max(scaled, axis=0, keepdims=True)
        row = -(top + jnp.log2(jnp.sum(jnp.exp2(scaled - top), axis=0, keepdims=True)))
        scaled = bias[...] + row
        top = jnp.max(scaled, axis=1, keepdims=True)
        scaled = jnp.exp2(scaled - top)
        total = jnp.sum(scaled, axis=1, keepdims=True)
        row_pot[...] = row
        col_pot[...] = -(top + jnp.log2(total))
        scaled = scaled * (1.0 / total)
        kern[...] = scaled
        return jnp.sum(scaled, axis=0, keepdims=True)

    total = log_sweep(bias[...])

    tile = (8, LANES)
    blocks = [pl.ds(start, 8) for start in range(0, BATCH, 8)]
    halves = [pl.ds(start, LANES) for start in range(0, BATCH, LANES)]

    def over_columns(low, high, rows, use):
        sums = [[jnp.zeros(tile, jnp.float32) for _ in halves] for _ in range(2)]
        for n, block in enumerate(blocks):
            parts = [kern[block, half] for half in halves]
            total = sum(part * row for part, row in zip(parts, rows))
            total = jnp.broadcast_to(jnp.sum(total, axis=1, keepdims=True), tile)
            low, high = jnp.minimum(low, total), jnp.maximum(high, total)
            factor = 1.0 / total
            parts = [part * factor for part in parts]
            if use is not None:
                use(block, factor, parts)
            for h, part in enumerate(parts):
                sums[n % 2][h] += part
        totals = []
        for first, second in zip(*sums):
            total = jnp.broadcast_to(jnp.sum(first + second, axis=0, keepdims=True), tile)
            low = jnp.minimum(low, total)
            totals.append(total)
        return low, high, totals

    units = noise_ref.shape[1] // UNIT
    share = units // (SWEEPS - 2)

    def squares(first, count, total):
        width = total.shape[1]
        for n in range(count * UNIT // width):
            start = pl.multiple_of(first * UNIT + n * width, LANES)
            wide = noise_ref[:, pl.ds(start, width)].astype(jnp.float32)
            total = total + wide * wide
        return total

    def sweep(step, carry):
        low, high, rows, noise_sq = carry
        low, high, totals = over_columns(low, high, rows, None)
        for total in totals:
            high = jnp.maximum(high, total)
        noise_sq = squares((step - 2) * share, share, noise_sq)
        return (low, high, tuple(1.0 / total for total in totals), noise_sq)

    def finish(block, factor, parts):
        col_fac[block, :] = factor[:, :1]
        for half, part in zip(halves, parts):
            kern[block, half] = part

    totals = [jnp.broadcast_to(total[:, half.start : half.start + LANES], tile) for half in halves]
    low, high = jnp.minimum(*totals), jnp.maximum(*totals)
    noise_sq = jnp.zeros((noise_ref.shape[0], 4 * UNIT), jnp.float32)
    carry = (low, high, tuple(1.0 / total for total in totals), noise_sq)
    low, high, rows, noise_sq = lax.fori_loop(2, SWEEPS, sweep, carry)
    done = (SWEEPS - 2) * share
    rest = squares(done, units - done, jnp.zeros((noise_ref.shape[0], UNIT), jnp.float32))
    noise_sq = jnp.sum(noise_sq, axis=1, keepdims=True) + jnp.sum(rest, axis=1, keepdims=True)
    noise_sq_ref[...] = jnp.broadcast_to(noise_sq, noise_sq_ref.shape)
    low, high, totals = over_columns(low, high, rows, finish)
    row_fac[...] = jnp.concatenate([row[:1] for row in rows], axis=1)
    row_sum[...] = jnp.concatenate([total[:1] for total in totals], axis=1)
    near = jnp.min(jnp.where((low >= 1.0 / DRIFT) & (high <= DRIFT), 1.0, 0.0)) > 0.5

    def targets():
        weights = (kern[...] * (1.0 / row_sum[...])).astype(jnp.bfloat16)
        moved = lax.dot_general(
            weights, data_ref[...], (((0,), (0,)), ((), ())), preferred_element_type=jnp.float32
        )
        out_ref[...] = moved.astype(jnp.bfloat16).reshape(out_ref.shape)

    targets()

    @pl.when(jnp.logical_not(near))
    def _():
        col_pot[...] = jnp.zeros_like(col_pot)

        def again(step, carry):
            log_sweep(bias[...] + col_pot[...])
            return carry

        lax.fori_loop(0, SWEEPS, again, 0)
        row_fac[...] = jnp.ones_like(row_fac)
        col_fac[...] = jnp.ones_like(col_fac)
        scaled = bias[...] + col_pot[...]
        scaled = jnp.exp2(scaled - jnp.max(scaled, axis=0, keepdims=True))
        kern[...] = scaled
        row_sum[...] = jnp.sum(scaled, axis=0, keepdims=True)
        targets()


def on_device(noise, data):
    devices = lax.axis_size(AXES)
    own = noise.shape[0]
    ent = UNITS * UNIT
    units = LATENT // UNIT
    params = pltpu.CompilerParams(vmem_limit_bytes=VMEM)
    anywhere = pl.BlockSpec(memory_space=pl.ANY)

    def units_of(rows):
        return rows.reshape(own, units, UNIT).transpose(1, 0, 2)

    both = pl.pallas_call(
        pack_kernel,
        out_shape=jax.ShapeDtypeStruct((devices, 2 * UNITS, own, UNIT), noise.dtype),
        in_specs=[pl.BlockSpec(memory_space=pltpu.HBM)] * 2,
        out_specs=anywhere,
        scratch_shapes=[
            pltpu.VMEM((UNITS * devices - units, own, UNIT), noise.dtype),
            pltpu.SemaphoreType.DMA((4 * UNITS,)),
        ],
        compiler_params=params,
    )(*[pltpu.with_memory_space_constraint(units_of(rows), pltpu.HBM) for rows in (noise, data)])
    both = both.transpose(0, 2, 1, 3).reshape(devices, own, 2 * ent)
    both = lax.all_to_all(both, AXES, split_axis=0, concat_axis=0)

    whole = jax.ShapeDtypeStruct((devices // 2, 8, LANES), jnp.float32)

    def exchange(parts):
        parts = parts.reshape(devices, 4, LANES)
        return lax.all_to_all(parts, AXES, split_axis=0, concat_axis=0).reshape(whole.shape)

    parts, data_ent = pl.pallas_call(
        gram_kernel,
        out_shape=(whole, jax.ShapeDtypeStruct((BATCH, ent), data.dtype)),
        compiler_params=params,
    )(both)
    total = pl.pallas_call(sum_kernel, out_shape=whole, compiler_params=params)(exchange(parts))
    total = exchange(total)

    along_lanes = jax.ShapeDtypeStruct((1, BATCH), jnp.float32)
    along_sublanes = jax.ShapeDtypeStruct((BATCH, 1), jnp.float32)
    moved, *pots, noise_sq = pl.pallas_call(
        sweep_kernel,
        out_shape=(
            jax.ShapeDtypeStruct((devices, own, ent), jnp.bfloat16),
            along_lanes,
            along_lanes,
            along_sublanes,
            along_sublanes,
            jax.ShapeDtypeStruct((own, LANES), jnp.float32),
        ),
        scratch_shapes=[
            pltpu.VMEM((BATCH, BATCH), jnp.float32),
            pltpu.VMEM((BATCH, BATCH), jnp.float32),
            pltpu.VMEM((1, BATCH), jnp.float32),
        ],
        compiler_params=params,
    )(total, data_ent, noise)
    moved = lax.all_to_all(moved, AXES, split_axis=0, concat_axis=0)
    moved = moved.reshape(devices, own, UNITS, UNIT).transpose(0, 2, 1, 3)
    in_vmem = pl.BlockSpec(memory_space=pltpu.VMEM)
    targets, row, col = pl.pallas_call(
        unpack_kernel,
        out_shape=(
            jax.ShapeDtypeStruct((units, own, UNIT), moved.dtype),
            jax.ShapeDtypeStruct((own,), jnp.float32),
            jax.ShapeDtypeStruct((own,), jnp.float32),
        ),
        in_specs=[anywhere] + [in_vmem] * 5,
        out_specs=(anywhere, anywhere, anywhere),
        scratch_shapes=[
            pltpu.SMEM((own,), jnp.float32),
            pltpu.SMEM((own,), jnp.float32),
            pltpu.SemaphoreType.DMA((UNITS + 2,)),
        ],
        compiler_params=params,
    )(moved, *pots, noise_sq)
    return (targets.transpose(1, 0, 2).reshape(own, LATENT), row, col)


def solution(mesh):
    return jax.shard_map(
        on_device,
        mesh=mesh,
        in_specs=(P(AXES, None), P(AXES, None)),
        out_specs=(P(AXES, None), P(AXES), P(AXES)),
        check_vma=False,
    )
```

```python
import math

import jax
import jax.numpy as jnp
from jax import lax
from jax.experimental import pallas as pl
from jax.experimental.pallas import tpu as pltpu
from jax.sharding import PartitionSpec as P

SWEEPS = 20
LATENT = 324480
BATCH = 256
AXES = ("dp", "dim")
LANES = 128
TEMPER = 0.25 / math.sqrt(LATENT)
BIT = TEMPER * math.log(2.0)
DRIFT = 2.0**40
VMEM = 24 * 1024 * 1024
UNITS = 4
UNIT = 640


def pack_kernel(noise_ref, data_ref, out_ref, zeros, sems):
    devices, units = out_ref.shape[0], noise_ref.shape[0]
    zeros[...] = jnp.zeros_like(zeros)
    copies = []
    for kind, ref in enumerate((noise_ref, data_ref)):
        for q in range(UNITS):
            slot = kind * UNITS + q
            start = q * devices
            count = min(devices, units - start)
            copies.append((ref.at[pl.ds(start, count)], out_ref.at[pl.ds(0, count), slot]))
            if count < devices:
                copies.append((zeros, out_ref.at[pl.ds(count, devices - count), slot]))
    copies = [pltpu.make_async_copy(src, dst, sems.at[n]) for n, (src, dst) in enumerate(copies)]
    for copy in copies:
        copy.start()
    for copy in copies:
        copy.wait()


def unpack_kernel(
    moved_ref, row_pot_ref, row_fac_ref, col_pot_ref, col_fac_ref, noise_sq_ref,
    out_ref, row_ref, col_ref, row, col, sems,
):
    devices, units = moved_ref.shape[0], out_ref.shape[0]
    own = out_ref.shape[1]
    copies = []
    for q in range(UNITS):
        start = q * devices
        count = min(devices, units - start)
        copies.append((moved_ref.at[pl.ds(0, count), q], out_ref.at[pl.ds(start, count)]))
    copies.extend([(row, row_ref), (col, col_ref)])
    copies = [pltpu.make_async_copy(src, dst, sems.at[n]) for n, (src, dst) in enumerate(copies)]
    for copy in copies[:UNITS]:
        copy.start()

    first = (lax.axis_index("dp") * lax.axis_size("dim") + lax.axis_index("dim")) * own
    row_pot = (row_pot_ref[...] + jnp.log2(row_fac_ref[...])) * BIT
    col_pot = (col_pot_ref[...] + jnp.log2(col_fac_ref[...])) * BIT
    lane = lax.broadcasted_iota(jnp.int32, row_pot.shape, 1)
    sublane = lax.broadcasted_iota(jnp.int32, col_pot.shape, 0)
    for n in range(own):
        mine = jnp.sum(jnp.where(lane == first + n, row_pot, 0.0))
        row[n] = mine + jnp.max(noise_sq_ref[n : n + 1, :]) / LATENT
        col[n] = jnp.sum(jnp.where(sublane == first + n, col_pot, 0.0))
    for copy in copies[UNITS:]:
        copy.start()
    for copy in copies:
        copy.wait()


def tiles():
    for tile in range(BATCH * BATCH // (8 * LANES)):
        row, half = 8 * (tile // 2), LANES * (tile % 2)
        yield tile, slice(row, row + 8), slice(half, half + LANES)


def gram_kernel(both_ref, out_ref, data_ref):
    ent = data_ref.shape[1]
    noise = jnp.transpose(both_ref[:, :, :ent].reshape(data_ref.shape))
    data_ref[...] = both_ref[:, :, ent:].reshape(data_ref.shape)
    gram = jnp.dot(data_ref[...], noise, preferred_element_type=jnp.float32)
    data_sq = jnp.zeros((BATCH, LANES), jnp.float32)
    for start in range(0, ent, LANES):
        wide = data_ref[:, start : start + LANES].astype(jnp.float32)
        data_sq = data_sq + wide * wide
    data_sq = jnp.sum(data_sq, axis=1, keepdims=True)
    parts = data_sq - 2.0 * gram
    for tile, rows, half in tiles():
        out_ref[tile] = parts[rows, half]


def sum_kernel(parts_ref, out_ref):
    total = jnp.sum(parts_ref[...], axis=0)
    total = total[:4] + total[4:]
    total = jnp.concatenate([total, total], axis=0)
    out_ref[...] = jnp.broadcast_to(total[None], out_ref.shape)


def sweep_kernel(
    cost_ref, data_ref, noise_ref, out_ref, row_pot, row_fac, col_pot, col_fac, noise_sq_ref,
    bias, kern, row_sum,
):
    for tile, rows, half in tiles():
        bias[rows, half] = cost_ref[tile] * (-1.0 / (LATENT * BIT))

    def log_sweep(scaled):
        top = jnp.max(scaled, axis=0, keepdims=True)
        row = -(top + jnp.log2(jnp.sum(jnp.exp2(scaled - top), axis=0, keepdims=True)))
        scaled = bias[...] + row
        top = jnp.max(scaled, axis=1, keepdims=True)
        scaled = jnp.exp2(scaled - top)
        total = jnp.sum(scaled, axis=1, keepdims=True)
        row_pot[...] = row
        col_pot[...] = -(top + jnp.log2(total))
        scaled = scaled * (1.0 / total)
        kern[...] = scaled
        return jnp.sum(scaled, axis=0, keepdims=True)

    total = log_sweep(bias[...])

    tile = (8, LANES)
    blocks = [pl.ds(start, 8) for start in range(0, BATCH, 8)]
    halves = [pl.ds(start, LANES) for start in range(0, BATCH, LANES)]

    def over_columns(low, high, rows, use):
        sums = [[jnp.zeros(tile, jnp.float32) for _ in halves] for _ in range(2)]
        for n, block in enumerate(blocks):
            parts = [kern[block, half] for half in halves]
            total = sum(part * row for part, row in zip(parts, rows))
            total = jnp.broadcast_to(jnp.sum(total, axis=1, keepdims=True), tile)
            low, high = jnp.minimum(low, total), jnp.maximum(high, total)
            factor = 1.0 / total
            parts = [part * factor for part in parts]
            if use is not None:
                use(block, factor, parts)
            for h, part in enumerate(parts):
                sums[n % 2][h] += part
        totals = []
        for first, second in zip(*sums):
            total = jnp.broadcast_to(jnp.sum(first + second, axis=0, keepdims=True), tile)
            low = jnp.minimum(low, total)
            totals.append(total)
        return low, high, totals

    units = noise_ref.shape[1] // UNIT
    share = units // (SWEEPS - 2)

    def squares(first, count, total):
        for n in range(count):
            start = pl.multiple_of((first + n) * UNIT, LANES)
            unit = noise_ref[:, pl.ds(start, UNIT)].astype(jnp.float32)
            total = total + unit * unit
        return total

    def sweep(step, carry):
        low, high, rows, noise_sq = carry
        low, high, totals = over_columns(low, high, rows, None)
        for total in totals:
            high = jnp.maximum(high, total)
        noise_sq = squares((step - 2) * share, share, noise_sq)
        return (low, high, tuple(1.0 / total for total in totals), noise_sq)

    def finish(block, factor, parts):
        col_fac[block, :] = factor[:, :1]
        for half, part in zip(halves, parts):
            kern[block, half] = part

    totals = [jnp.broadcast_to(total[:, half.start : half.start + LANES], tile) for half in halves]
    low, high = jnp.minimum(*totals), jnp.maximum(*totals)
    noise_sq = jnp.zeros((noise_ref.shape[0], UNIT), jnp.float32)
    carry = (low, high, tuple(1.0 / total for total in totals), noise_sq)
    low, high, rows, noise_sq = lax.fori_loop(2, SWEEPS, sweep, carry)
    done = (SWEEPS - 2) * share
    noise_sq = jnp.sum(squares(done, units - done, noise_sq), axis=1, keepdims=True)
    noise_sq_ref[...] = jnp.broadcast_to(noise_sq, noise_sq_ref.shape)
    low, high, totals = over_columns(low, high, rows, finish)
    row_fac[...] = jnp.concatenate([row[:1] for row in rows], axis=1)
    row_sum[...] = jnp.concatenate([total[:1] for total in totals], axis=1)
    near = jnp.min(jnp.where((low >= 1.0 / DRIFT) & (high <= DRIFT), 1.0, 0.0)) > 0.5

    def targets():
        weights = (kern[...] * (1.0 / row_sum[...])).astype(jnp.bfloat16)
        moved = lax.dot_general(
            weights, data_ref[...], (((0,), (0,)), ((), ())), preferred_element_type=jnp.float32
        )
        out_ref[...] = moved.astype(jnp.bfloat16).reshape(out_ref.shape)

    targets()

    @pl.when(jnp.logical_not(near))
    def _():
        col_pot[...] = jnp.zeros_like(col_pot)

        def again(step, carry):
            log_sweep(bias[...] + col_pot[...])
            return carry

        lax.fori_loop(0, SWEEPS, again, 0)
        row_fac[...] = jnp.ones_like(row_fac)
        col_fac[...] = jnp.ones_like(col_fac)
        scaled = bias[...] + col_pot[...]
        scaled = jnp.exp2(scaled - jnp.max(scaled, axis=0, keepdims=True))
        kern[...] = scaled
        row_sum[...] = jnp.sum(scaled, axis=0, keepdims=True)
        targets()


def on_device(noise, data):
    devices = lax.axis_size(AXES)
    own = noise.shape[0]
    ent = UNITS * UNIT
    units = LATENT // UNIT
    params = pltpu.CompilerParams(vmem_limit_bytes=VMEM)
    anywhere = pl.BlockSpec(memory_space=pl.ANY)

    def units_of(rows):
        return rows.reshape(own, units, UNIT).transpose(1, 0, 2)

    both = pl.pallas_call(
        pack_kernel,
        out_shape=jax.ShapeDtypeStruct((devices, 2 * UNITS, own, UNIT), noise.dtype),
        in_specs=[pl.BlockSpec(memory_space=pltpu.HBM)] * 2,
        out_specs=anywhere,
        scratch_shapes=[
            pltpu.VMEM((UNITS * devices - units, own, UNIT), noise.dtype),
            pltpu.SemaphoreType.DMA((4 * UNITS,)),
        ],
        compiler_params=params,
    )(*[pltpu.with_memory_space_constraint(units_of(rows), pltpu.HBM) for rows in (noise, data)])
    both = both.transpose(0, 2, 1, 3).reshape(devices, own, 2 * ent)
    both = lax.all_to_all(both, AXES, split_axis=0, concat_axis=0)

    whole = jax.ShapeDtypeStruct((devices // 2, 8, LANES), jnp.float32)

    def exchange(parts):
        parts = parts.reshape(devices, 4, LANES)
        return lax.all_to_all(parts, AXES, split_axis=0, concat_axis=0).reshape(whole.shape)

    parts, data_ent = pl.pallas_call(
        gram_kernel,
        out_shape=(whole, jax.ShapeDtypeStruct((BATCH, ent), data.dtype)),
        compiler_params=params,
    )(both)
    noise, parts = lax.optimization_barrier((noise, parts))
    total = pl.pallas_call(sum_kernel, out_shape=whole, compiler_params=params)(exchange(parts))
    total = exchange(total)

    along_lanes = jax.ShapeDtypeStruct((1, BATCH), jnp.float32)
    along_sublanes = jax.ShapeDtypeStruct((BATCH, 1), jnp.float32)
    moved, *pots, noise_sq = pl.pallas_call(
        sweep_kernel,
        out_shape=(
            jax.ShapeDtypeStruct((devices, own, ent), jnp.bfloat16),
            along_lanes,
            along_lanes,
            along_sublanes,
            along_sublanes,
            jax.ShapeDtypeStruct((own, LANES), jnp.float32),
        ),
        scratch_shapes=[
            pltpu.VMEM((BATCH, BATCH), jnp.float32),
            pltpu.VMEM((BATCH, BATCH), jnp.float32),
            pltpu.VMEM((1, BATCH), jnp.float32),
        ],
        compiler_params=params,
    )(total, data_ent, noise)
    moved = lax.all_to_all(moved, AXES, split_axis=0, concat_axis=0)
    moved = moved.reshape(devices, own, UNITS, UNIT).transpose(0, 2, 1, 3)
    in_vmem = pl.BlockSpec(memory_space=pltpu.VMEM)
    targets, row, col = pl.pallas_call(
        unpack_kernel,
        out_shape=(
            jax.ShapeDtypeStruct((units, own, UNIT), moved.dtype),
            jax.ShapeDtypeStruct((own,), jnp.float32),
            jax.ShapeDtypeStruct((own,), jnp.float32),
        ),
        in_specs=[anywhere] + [in_vmem] * 5,
        out_specs=(anywhere, anywhere, anywhere),
        scratch_shapes=[
            pltpu.SMEM((own,), jnp.float32),
            pltpu.SMEM((own,), jnp.float32),
            pltpu.SemaphoreType.DMA((UNITS + 2,)),
        ],
        compiler_params=params,
    )(moved, *pots, noise_sq)
    return (targets.transpose(1, 0, 2).reshape(own, LATENT), row, col)


def solution(mesh):
    return jax.shard_map(
        on_device,
        mesh=mesh,
        in_specs=(P(AXES, None), P(AXES, None)),
        out_specs=(P(AXES, None), P(AXES), P(AXES)),
        check_vma=False,
    )
```

```python
import math

import jax
import jax.numpy as jnp
from jax import lax
from jax.experimental import pallas as pl
from jax.experimental.pallas import tpu as pltpu
from jax.sharding import PartitionSpec as P

SWEEPS = 20
LATENT = 324480
BATCH = 256
AXES = ("dp", "dim")
LANES = 128
TEMPER = 0.25 / math.sqrt(LATENT)
BIT = TEMPER * math.log(2.0)
DRIFT = 2.0**40
VMEM = 24 * 1024 * 1024
UNITS = 4
UNIT = 640


def pack_kernel(noise_ref, data_ref, out_ref, zeros, sems):
    devices, units = out_ref.shape[0], noise_ref.shape[0]
    zeros[...] = jnp.zeros_like(zeros)
    copies = []
    for kind, ref in enumerate((noise_ref, data_ref)):
        for q in range(UNITS):
            slot = kind * UNITS + q
            start = q * devices
            count = min(devices, units - start)
            copies.append((ref.at[pl.ds(start, count)], out_ref.at[pl.ds(0, count), slot]))
            if count < devices:
                copies.append((zeros, out_ref.at[pl.ds(count, devices - count), slot]))
    copies = [pltpu.make_async_copy(src, dst, sems.at[n]) for n, (src, dst) in enumerate(copies)]
    for copy in copies:
        copy.start()
    for copy in copies:
        copy.wait()


def unpack_kernel(
    moved_ref, row_pot_ref, row_fac_ref, col_pot_ref, col_fac_ref, noise_sq_ref,
    out_ref, row_ref, col_ref, row, col, sems,
):
    devices, units = moved_ref.shape[0], out_ref.shape[0]
    own = out_ref.shape[1]
    copies = []
    for q in range(UNITS):
        start = q * devices
        count = min(devices, units - start)
        copies.append((moved_ref.at[pl.ds(0, count), q], out_ref.at[pl.ds(start, count)]))
    copies.extend([(row, row_ref), (col, col_ref)])
    copies = [pltpu.make_async_copy(src, dst, sems.at[n]) for n, (src, dst) in enumerate(copies)]
    for copy in copies[:UNITS]:
        copy.start()

    first = (lax.axis_index("dp") * lax.axis_size("dim") + lax.axis_index("dim")) * own
    row_pot = (row_pot_ref[...] + jnp.log2(row_fac_ref[...])) * BIT
    col_pot = (col_pot_ref[...] + jnp.log2(col_fac_ref[...])) * BIT
    lane = lax.broadcasted_iota(jnp.int32, row_pot.shape, 1)
    sublane = lax.broadcasted_iota(jnp.int32, col_pot.shape, 0)
    for n in range(own):
        col[n] = jnp.sum(jnp.where(sublane == first + n, col_pot, 0.0))
    copies[UNITS + 1].start()
    for n in range(own):
        mine = jnp.sum(jnp.where(lane == first + n, row_pot, 0.0))
        row[n] = mine + jnp.max(noise_sq_ref[n : n + 1, :]) / LATENT
    copies[UNITS].start()
    for copy in copies:
        copy.wait()


def tiles():
    for tile in range(BATCH * BATCH // (8 * LANES)):
        row, half = 8 * (tile // 2), LANES * (tile % 2)
        yield tile, slice(row, row + 8), slice(half, half + LANES)


def gram_kernel(both_ref, out_ref, data_ref):
    ent = data_ref.shape[1]
    noise = jnp.transpose(both_ref[:, :, :ent].reshape(data_ref.shape))
    data_ref[...] = both_ref[:, :, ent:].reshape(data_ref.shape)
    gram = jnp.dot(data_ref[...], noise, preferred_element_type=jnp.float32)
    data_sq = jnp.zeros((BATCH, LANES), jnp.float32)
    for start in range(0, ent, LANES):
        wide = data_ref[:, start : start + LANES].astype(jnp.float32)
        data_sq = data_sq + wide * wide
    data_sq = jnp.sum(data_sq, axis=1, keepdims=True)
    parts = data_sq - 2.0 * gram
    for tile, rows, half in tiles():
        out_ref[tile] = parts[rows, half]


def sum_kernel(parts_ref, out_ref):
    total = jnp.sum(parts_ref[...], axis=0)
    total = total[:4] + total[4:]
    total = jnp.concatenate([total, total], axis=0)
    out_ref[...] = jnp.broadcast_to(total[None], out_ref.shape)


def sweep_kernel(
    cost_ref, data_ref, noise_ref, out_ref, row_pot, row_fac, col_pot, col_fac, noise_sq_ref,
    bias, kern, row_sum,
):
    for tile, rows, half in tiles():
        bias[rows, half] = cost_ref[tile] * (-1.0 / (LATENT * BIT))

    def log_sweep(scaled):
        top = jnp.max(scaled, axis=0, keepdims=True)
        row = -(top + jnp.log2(jnp.sum(jnp.exp2(scaled - top), axis=0, keepdims=True)))
        scaled = bias[...] + row
        top = jnp.max(scaled, axis=1, keepdims=True)
        scaled = jnp.exp2(scaled - top)
        total = jnp.sum(scaled, axis=1, keepdims=True)
        row_pot[...] = row
        col_pot[...] = -(top + jnp.log2(total))
        scaled = scaled * (1.0 / total)
        kern[...] = scaled
        return jnp.sum(scaled, axis=0, keepdims=True)

    total = log_sweep(bias[...])

    tile = (8, LANES)
    blocks = [pl.ds(start, 8) for start in range(0, BATCH, 8)]
    halves = [pl.ds(start, LANES) for start in range(0, BATCH, LANES)]

    def over_columns(low, high, rows, use):
        sums = [[jnp.zeros(tile, jnp.float32) for _ in halves] for _ in range(2)]
        for n, block in enumerate(blocks):
            parts = [kern[block, half] for half in halves]
            total = sum(part * row for part, row in zip(parts, rows))
            total = jnp.broadcast_to(jnp.sum(total, axis=1, keepdims=True), tile)
            low, high = jnp.minimum(low, total), jnp.maximum(high, total)
            factor = 1.0 / total
            parts = [part * factor for part in parts]
            if use is not None:
                use(block, factor, parts)
            for h, part in enumerate(parts):
                sums[n % 2][h] += part
        totals = []
        for first, second in zip(*sums):
            total = jnp.broadcast_to(jnp.sum(first + second, axis=0, keepdims=True), tile)
            low = jnp.minimum(low, total)
            totals.append(total)
        return low, high, totals

    units = noise_ref.shape[1] // UNIT
    share = units // (SWEEPS - 2)

    def squares(first, count, total):
        for n in range(count):
            start = pl.multiple_of((first + n) * UNIT, LANES)
            unit = noise_ref[:, pl.ds(start, UNIT)].astype(jnp.float32)
            total = total + unit * unit
        return total

    def sweep(step, carry):
        low, high, rows, noise_sq = carry
        low, high, totals = over_columns(low, high, rows, None)
        for total in totals:
            high = jnp.maximum(high, total)
        noise_sq = squares((step - 2) * share, share, noise_sq)
        return (low, high, tuple(1.0 / total for total in totals), noise_sq)

    def finish(block, factor, parts):
        col_fac[block, :] = factor[:, :1]
        for half, part in zip(halves, parts):
            kern[block, half] = part

    totals = [jnp.broadcast_to(total[:, half.start : half.start + LANES], tile) for half in halves]
    low, high = jnp.minimum(*totals), jnp.maximum(*totals)
    noise_sq = jnp.zeros((noise_ref.shape[0], UNIT), jnp.float32)
    carry = (low, high, tuple(1.0 / total for total in totals), noise_sq)
    low, high, rows, noise_sq = lax.fori_loop(2, SWEEPS, sweep, carry)
    done = (SWEEPS - 2) * share
    noise_sq = jnp.sum(squares(done, units - done, noise_sq), axis=1, keepdims=True)
    noise_sq_ref[...] = jnp.broadcast_to(noise_sq, noise_sq_ref.shape)
    low, high, totals = over_columns(low, high, rows, finish)
    row_fac[...] = jnp.concatenate([row[:1] for row in rows], axis=1)
    row_sum[...] = jnp.concatenate([total[:1] for total in totals], axis=1)
    near = jnp.min(jnp.where((low >= 1.0 / DRIFT) & (high <= DRIFT), 1.0, 0.0)) > 0.5

    def targets():
        weights = (kern[...] * (1.0 / row_sum[...])).astype(jnp.bfloat16)
        moved = lax.dot_general(
            weights, data_ref[...], (((0,), (0,)), ((), ())), preferred_element_type=jnp.float32
        )
        out_ref[...] = moved.astype(jnp.bfloat16).reshape(out_ref.shape)

    targets()

    @pl.when(jnp.logical_not(near))
    def _():
        col_pot[...] = jnp.zeros_like(col_pot)

        def again(step, carry):
            log_sweep(bias[...] + col_pot[...])
            return carry

        lax.fori_loop(0, SWEEPS, again, 0)
        row_fac[...] = jnp.ones_like(row_fac)
        col_fac[...] = jnp.ones_like(col_fac)
        scaled = bias[...] + col_pot[...]
        scaled = jnp.exp2(scaled - jnp.max(scaled, axis=0, keepdims=True))
        kern[...] = scaled
        row_sum[...] = jnp.sum(scaled, axis=0, keepdims=True)
        targets()


def on_device(noise, data):
    devices = lax.axis_size(AXES)
    own = noise.shape[0]
    ent = UNITS * UNIT
    units = LATENT // UNIT
    params = pltpu.CompilerParams(vmem_limit_bytes=VMEM)
    anywhere = pl.BlockSpec(memory_space=pl.ANY)

    def units_of(rows):
        return rows.reshape(own, units, UNIT).transpose(1, 0, 2)

    both = pl.pallas_call(
        pack_kernel,
        out_shape=jax.ShapeDtypeStruct((devices, 2 * UNITS, own, UNIT), noise.dtype),
        in_specs=[pl.BlockSpec(memory_space=pltpu.HBM)] * 2,
        out_specs=anywhere,
        scratch_shapes=[
            pltpu.VMEM((UNITS * devices - units, own, UNIT), noise.dtype),
            pltpu.SemaphoreType.DMA((4 * UNITS,)),
        ],
        compiler_params=params,
    )(*[pltpu.with_memory_space_constraint(units_of(rows), pltpu.HBM) for rows in (noise, data)])
    both = both.transpose(0, 2, 1, 3).reshape(devices, own, 2 * ent)
    both = lax.all_to_all(both, AXES, split_axis=0, concat_axis=0)

    whole = jax.ShapeDtypeStruct((devices // 2, 8, LANES), jnp.float32)

    def exchange(parts):
        parts = parts.reshape(devices, 4, LANES)
        return lax.all_to_all(parts, AXES, split_axis=0, concat_axis=0).reshape(whole.shape)

    parts, data_ent = pl.pallas_call(
        gram_kernel,
        out_shape=(whole, jax.ShapeDtypeStruct((BATCH, ent), data.dtype)),
        compiler_params=params,
    )(both)
    total = pl.pallas_call(sum_kernel, out_shape=whole, compiler_params=params)(exchange(parts))
    total = exchange(total)

    along_lanes = jax.ShapeDtypeStruct((1, BATCH), jnp.float32)
    along_sublanes = jax.ShapeDtypeStruct((BATCH, 1), jnp.float32)
    moved, *pots, noise_sq = pl.pallas_call(
        sweep_kernel,
        out_shape=(
            jax.ShapeDtypeStruct((devices, own, ent), jnp.bfloat16),
            along_lanes,
            along_lanes,
            along_sublanes,
            along_sublanes,
            jax.ShapeDtypeStruct((own, LANES), jnp.float32),
        ),
        scratch_shapes=[
            pltpu.VMEM((BATCH, BATCH), jnp.float32),
            pltpu.VMEM((BATCH, BATCH), jnp.float32),
            pltpu.VMEM((1, BATCH), jnp.float32),
        ],
        compiler_params=params,
    )(total, data_ent, noise)
    moved = lax.all_to_all(moved, AXES, split_axis=0, concat_axis=0)
    moved = moved.reshape(devices, own, UNITS, UNIT).transpose(0, 2, 1, 3)
    in_vmem = pl.BlockSpec(memory_space=pltpu.VMEM)
    targets, row, col = pl.pallas_call(
        unpack_kernel,
        out_shape=(
            jax.ShapeDtypeStruct((units, own, UNIT), moved.dtype),
            jax.ShapeDtypeStruct((own,), jnp.float32),
            jax.ShapeDtypeStruct((own,), jnp.float32),
        ),
        in_specs=[anywhere] + [in_vmem] * 5,
        out_specs=(anywhere, anywhere, anywhere),
        scratch_shapes=[
            pltpu.SMEM((own,), jnp.float32),
            pltpu.SMEM((own,), jnp.float32),
            pltpu.SemaphoreType.DMA((UNITS + 2,)),
        ],
        compiler_params=params,
    )(moved, *pots, noise_sq)
    return (targets.transpose(1, 0, 2).reshape(own, LATENT), row, col)


def solution(mesh):
    return jax.shard_map(
        on_device,
        mesh=mesh,
        in_specs=(P(AXES, None), P(AXES, None)),
        out_specs=(P(AXES, None), P(AXES), P(AXES)),
        check_vma=False,
    )
```
